32 devices in a mesh: gx: 2 (over x), gy: 16 (over z, y, core).
Axes of the slice: x: 2, y: 2, z: 4, core: 2. Of those that a mesh axis runs over, the one named last changes fastest.
Arguments:
- level_set: float32 [16, 512, 128], P('gx', 'gy'), may hold values from -3 to 3
- velocity: float32 [3, 16, 512, 128], P(None, 'gx', 'gy'), may hold values from -5 to 5
- source: float32 [16, 512, 128], P('gx', 'gy'), may hold values from -6 to 6
- wick_solid: int32 [2, 64, 16], P('gx', 'gy'), may hold values 0 or 1
Outputs:
- level_new: float32 [16, 512, 128], P('gx', 'gy')
- pressure: float32 [16, 512, 128], P('gx', 'gy')
The draws below stay inside these ranges and needn't reach their ends.
All inputs are finite; a program needn't handle non-finite values. No bound on the sum of `wick_solid` on one device may be relied on, other than what follows from the above.
Results may differ from the reference program's by a relative error of at most 0.00055.
Values sent between devices are 32-bit elements; how exact they have to be, the bound alone decides.
A program may use at most 64 MiB of HBM per device.

```python
import jax
import jax.numpy as jnp
import numpy as np
from jax import lax

EZ = 1
EY = 4
EX = 16
ITERS = 2
NZ = 16
NY = 512
NX = 128
N_GX = 2
N_GY = 16


def touch_ends(entries, rng, low, top_value):
    longest = entries.shape.index(max(entries.shape))
    spots = []
    for shift in (0, 1):
        where = [jax.random.randint(jax.random.fold_in(rng, axis), (), 0, length) for axis, length in enumerate(entries.shape)]
        where[longest] = (where[longest] + shift) % entries.shape[longest]
        spots.append(tuple(where))
    return entries.at[spots[0]].set(low).at[spots[1]].set(top_value)


def block_levels(rng, dims, cuts, least, high):
    factor_of = 1.0
    for axis_at, blocks in cuts:
        heights = jax.random.uniform(jax.random.fold_in(jax.random.fold_in(rng, 6), axis_at), (blocks,), jnp.float32, least / len(cuts), high / len(cuts))
        factor_of = factor_of * jnp.repeat(jnp.exp(heights), dims[axis_at] // blocks).reshape((-1,) + (1,) * (len(dims) - 1 - axis_at))
    return factor_of


def normal_values(own_key, shape, width, reach, pieces=(), kind=jnp.bfloat16):
    values = width * jax.random.normal(own_key, shape, jnp.float32)
    if pieces:
        values = values * block_levels(own_key, shape, pieces, -0.22, 0.18)
    return jnp.clip(values, -reach, reach).astype(kind)


def setup_inputs(seed: int = 0) -> dict:
    splits = jax.random.split(jax.random.key(seed), 5)
    level_set = normal_values(splits[0], (NZ, NY, NX), 0.5, 3.0, ((0, 2), (1, 16)), jnp.float32)
    velocity = normal_values(splits[1], (3, NZ, NY, NX), 1.0, 5.0, ((1, 2), (2, 16)), jnp.float32)
    source = normal_values(splits[2], (NZ, NY, NX), 1.0, 6.0, ((0, 2), (1, 16)), jnp.float32)
    wick_solid = touch_ends((jax.random.randint(splits[3], (EZ * N_GX, EY * N_GY, EX), 0, 3) < 1).astype(jnp.int32), jax.random.fold_in(splits[3], 1), 0, 1)
    return {"level_set": level_set, "velocity": velocity, "source": source, "wick_solid": wick_solid}


TIME_STEP = 0.02
HELM_COEF = 0.25
LEVEL_WIDTH = 0.25
GAS_RATIO = 10.0
SOLID_FACTOR = 0.25
SCHWARZ_SCALE = 0.5
SCHWARZ_SHIFT = 0.05

def gll_tables():
    gll_nodes = np.array([-1.0, -0.8717401485096066, -0.5917001814331423, -0.2092992179024789, 0.2092992179024789, 0.5917001814331423, 0.8717401485096066, 1.0])
    weight_np = np.array([1.0 / 28.0, 0.21070422714350603, 0.3411226924835044, 0.4124587946587038, 0.4124587946587038, 0.3411226924835044, 0.21070422714350603, 1.0 / 28.0])
    bary_weights = np.array([1.0 / np.prod([gll_nodes[i] - gll_nodes[j] for j in range(8) if j != i]) for i in range(8)])
    derivative = np.zeros((8, 8))
    for i in range(8):
        for j in range(8):
            if i != j:
                derivative[i, j] = bary_weights[j] / bary_weights[i] / (gll_nodes[i] - gll_nodes[j])
        derivative[i, i] = -np.sum(derivative[i])
    return (weight_np, derivative)

def sine_tables():
    indices = np.arange(10) + 1.0
    sine_basis = np.sqrt(2.0 / 11.0) * np.sin(np.pi * np.outer(indices, indices) / 11.0)
    eigen_vals = 2.0 - 2.0 * np.cos(np.pi * indices / 11.0)
    return (sine_basis, eigen_vals)

def apply_blocks(values, matrix, axis_id):
    block_size = matrix.shape[0]
    dim_shape = values.shape
    if axis_id == 2:
        big_table = jnp.kron(jnp.eye(dim_shape[2] // block_size, dtype=jnp.float32), matrix.T)
        return jnp.dot(values, big_table, precision=lax.Precision.HIGHEST)
    if axis_id == 0:
        parted = values.reshape(dim_shape[0] // block_size, block_size, dim_shape[1], dim_shape[2])
        return jnp.einsum('ij,ajyx->aiyx', matrix, parted, precision=lax.Precision.HIGHEST).reshape(dim_shape)
    parted = values.reshape(dim_shape[0], dim_shape[1] // block_size, block_size, dim_shape[2])
    return jnp.einsum('ij,zajx->zaix', matrix, parted, precision=lax.Precision.HIGHEST).reshape(dim_shape)

def node_weights(weight_np, grid_shape):
    weight_row = jnp.asarray(weight_np, dtype=jnp.float32)
    along_z = jnp.tile(weight_row, grid_shape[0] // 8)
    along_y = jnp.tile(weight_row, grid_shape[1] // 8)
    along_x = jnp.tile(weight_row, grid_shape[2] // 8)
    return along_z[:, None, None] * along_y[None, :, None] * along_x[None, None, :]

def axis_count(length, start, total):
    position = jnp.arange(length) + start
    node_pos = jnp.arange(length) % 8
    inner_lo = jnp.logical_and(node_pos == 0, position > 0).astype(jnp.float32)
    inner_hi = jnp.logical_and(node_pos == 7, position < total - 1).astype(jnp.float32)
    return 1.0 + inner_lo + inner_hi

def fold_axis(padded, axis_id):
    length = padded.shape[axis_id] - 2
    node_pos = jnp.arange(length) % 8
    mask_shape = [1, 1, 1]
    mask_shape[axis_id] = length
    first_mask = (node_pos == 0).astype(jnp.float32).reshape(mask_shape)
    last_mask = (node_pos == 7).astype(jnp.float32).reshape(mask_shape)
    middle = lax.slice_in_dim(padded, 1, length + 1, axis=axis_id)
    lower_rim = lax.slice_in_dim(padded, 0, length, axis=axis_id)
    upper_rim = lax.slice_in_dim(padded, 2, length + 2, axis=axis_id)
    return middle + first_mask * lower_rim + last_mask * upper_rim

def fold_all(padded):
    summed = fold_axis(padded, 1)
    summed = fold_axis(summed, 0)
    summed = jnp.pad(summed, ((0, 0), (0, 0), (1, 1)))
    return fold_axis(summed, 2)

def extend_axis(padded, axis_id):
    length = padded.shape[axis_id] - 4
    blocks = length // 8
    dim_shape = list(padded.shape)
    part_shape = dim_shape[:axis_id] + [blocks, 8] + dim_shape[axis_id + 1:]
    center_part = lax.slice_in_dim(padded, 2, length + 2, axis=axis_id).reshape(part_shape)
    lower_part = lax.slice_in_dim(padded, 0, length, axis=axis_id).reshape(part_shape)
    upper_part = lax.slice_in_dim(padded, 4, length + 4, axis=axis_id).reshape(part_shape)
    lower_rim = lax.slice_in_dim(lower_part, 0, 1, axis=axis_id + 1)
    upper_rim = lax.slice_in_dim(upper_part, 7, 8, axis=axis_id + 1)
    joined = jnp.concatenate([lower_rim, center_part, upper_rim], axis=axis_id + 1)
    return joined.reshape(dim_shape[:axis_id] + [blocks * 10] + dim_shape[axis_id + 1:])

def extend_all(padded):
    widened = extend_axis(padded, 1)
    widened = extend_axis(widened, 0)
    widened = jnp.pad(widened, ((0, 0), (0, 0), (2, 2)))
    return extend_axis(widened, 2)

def inner_axis(values, axis_id):
    dim_shape = list(values.shape)
    blocks = dim_shape[axis_id] // 10
    parted = values.reshape(dim_shape[:axis_id] + [blocks, 10] + dim_shape[axis_id + 1:])
    kept_nodes = lax.slice_in_dim(parted, 1, 9, axis=axis_id + 1)
    return kept_nodes.reshape(dim_shape[:axis_id] + [blocks * 8] + dim_shape[axis_id + 1:])

def schwarz_solve(widened, sine_basis, eigen_vals):
    spectral = apply_blocks(apply_blocks(apply_blocks(widened, sine_basis, 0), sine_basis, 1), sine_basis, 2)
    lam_z = jnp.tile(eigen_vals, widened.shape[0] // 10)
    lam_y = jnp.tile(eigen_vals, widened.shape[1] // 10)
    lam_x = jnp.tile(eigen_vals, widened.shape[2] // 10)
    denominator = SCHWARZ_SCALE * (lam_z[:, None, None] + lam_y[None, :, None] + lam_x[None, None, :]) + SCHWARZ_SHIFT
    spectral = spectral / denominator
    restored = apply_blocks(apply_blocks(apply_blocks(spectral, sine_basis, 0), sine_basis, 1), sine_basis, 2)
    return inner_axis(inner_axis(inner_axis(restored, 0), 1), 2)

def coarse_matrix(kbar):
    rows_gx, rows_gy = kbar.shape
    along_z = 2.0 * kbar[:-1] * kbar[1:] / (kbar[:-1] + kbar[1:]) * (EY * EX / EZ)
    along_y = 2.0 * kbar[:, :-1] * kbar[:, 1:] / (kbar[:, :-1] + kbar[:, 1:]) * (EZ * EX / EY)
    diagonal = HELM_COEF * EZ * EY * EX + jnp.pad(along_z, ((1, 0), (0, 0))) + jnp.pad(along_z, ((0, 1), (0, 0)))
    diagonal = diagonal + jnp.pad(along_y, ((0, 0), (1, 0))) + jnp.pad(along_y, ((0, 0), (0, 1)))
    total = rows_gx * rows_gy
    z_links = jnp.pad(along_z, ((0, 1), (0, 0))).reshape(total)[:total - rows_gy]
    y_links = jnp.pad(along_y, ((0, 0), (0, 1))).reshape(total)[:total - 1]
    matrix = jnp.diag(diagonal.reshape(total)) - jnp.diag(z_links, rows_gy) - jnp.diag(z_links, -rows_gy)
    return matrix - jnp.diag(y_links, 1) - jnp.diag(y_links, -1)

def chol_solve(factor, rhs_vec):
    column = rhs_vec.reshape(-1, 1)
    middle = lax.linalg.triangular_solve(factor, column, left_side=True, lower=True)
    return lax.linalg.triangular_solve(factor, middle, left_side=True, lower=True, transpose_a=True).reshape(-1)

def reference(level_set, velocity, source, wick_solid):
    weight_np, deriv_np = gll_tables()
    deriv = jnp.asarray(deriv_np, dtype=jnp.float32)
    deriv_t = jnp.asarray(deriv_np.T, dtype=jnp.float32)
    basis_np, eigen_np = sine_tables()
    sine_basis = jnp.asarray(basis_np, dtype=jnp.float32)
    eigen_vals = jnp.asarray(eigen_np, dtype=jnp.float32)
    grid_shape = level_set.shape
    node_w = node_weights(weight_np, grid_shape)
    mass_w = 0.125 * node_w
    mult = axis_count(grid_shape[0], 0, grid_shape[0])[:, None, None] * axis_count(grid_shape[1], 0, grid_shape[1])[None, :, None] * axis_count(grid_shape[2], 0, grid_shape[2])[None, None, :]
    inv_mult = 1.0 / mult

    def assemble(values):
        return fold_all(jnp.pad(values, ((1, 1), (1, 1), (0, 0))))
    advect = velocity[0] * 2.0 * apply_blocks(level_set, deriv, 0)
    advect = advect + velocity[1] * 2.0 * apply_blocks(level_set, deriv, 1)
    advect = advect + velocity[2] * 2.0 * apply_blocks(level_set, deriv, 2)
    moved = level_set - TIME_STEP * advect
    level_new = assemble(mass_w * moved) / (mass_w * mult)
    heavi = jax.nn.sigmoid(level_new / LEVEL_WIDTH)
    solid_pts = jnp.repeat(jnp.repeat(jnp.repeat(wick_solid, 8, axis=0), 8, axis=1), 8, axis=2).astype(jnp.float32)
    coef = (GAS_RATIO - (GAS_RATIO - 1.0) * heavi) * (1.0 - (1.0 - SOLID_FACTOR) * solid_pts)
    flux_w = 0.5 * coef * node_w

    def helm(values):
        result = HELM_COEF * mass_w * values
        for axis_id in range(3):
            result = result + apply_blocks(flux_w * apply_blocks(values, deriv, axis_id), deriv_t, axis_id)
        return assemble(result)
    diverge = 2.0 * (apply_blocks(velocity[0], deriv, 0) + apply_blocks(velocity[1], deriv, 1) + apply_blocks(velocity[2], deriv, 2))
    rhs = assemble(mass_w * (source - TIME_STEP * diverge))
    slab_rows = EZ * 8
    col_rows = EY * 8
    kbar = lax.optimization_barrier(jnp.mean(coef.reshape(N_GX, slab_rows, N_GY, col_rows, grid_shape[2]), axis=(1, 3, 4)))
    factor = jnp.linalg.cholesky(coarse_matrix(kbar))

    def coarse_field(residual):
        totals = lax.optimization_barrier(jnp.sum((residual * inv_mult).reshape(N_GX, slab_rows, N_GY, col_rows, grid_shape[2]), axis=(1, 3, 4)))
        solved = chol_solve(factor, totals.reshape(-1)).reshape(N_GX, N_GY)
        return jnp.repeat(jnp.repeat(solved, slab_rows, axis=0), col_rows, axis=1)[:, :, None]

    def precond(residual):
        widened = extend_all(jnp.pad(residual, ((2, 2), (2, 2), (0, 0))))
        local = schwarz_solve(widened, sine_basis, eigen_vals)
        return assemble(inv_mult * (local + coarse_field(residual)))

    def inner(left, right):
        return jnp.sum(left * right * inv_mult)
    pressure = jnp.zeros_like(rhs)
    residual = rhs
    precon = precond(residual)
    rz_now = inner(residual, precon)
    search = precon
    for sweep_id in range(ITERS):
        applied = helm(search)
        step_len = rz_now / inner(search, applied)
        pressure = pressure + step_len * search
        residual = residual - step_len * applied
        if sweep_id + 1 < ITERS:
            precon = precond(residual)
            rz_next = inner(residual, precon)
            search = precon + rz_next / rz_now * search
            rz_now = rz_next
    return (level_new, pressure)
```

```python
import functools

import jax
import jax.numpy as jnp
import ml_dtypes
import numpy as np
from jax import lax
from jax.experimental import pallas as pl
from jax.experimental.pallas import tpu as pltpu
from jax.sharding import PartitionSpec as P

EZ = 1
EY = 4
EX = 16
ROWS = 256
EXT = 384
SPEC = 400

TIME_STEP = 0.02
HELM_COEF = 0.25
LEVEL_WIDTH = 0.25
GAS_RATIO = 10.0
SOLID_FACTOR = 0.25
SCHWARZ_SCALE = 0.5
SCHWARZ_SHIFT = 0.05

MESH = pl.DeviceIdType.MESH
F32 = jnp.float32
BF16 = jnp.bfloat16

SIDES = ((-1, 0), (1, 0), (0, -1), (0, 1), (-1, -1), (-1, 1), (1, -1), (1, 1))
OPPOSITE = tuple(SIDES.index((-dz, -dy)) for dz, dy in SIDES)


def gll_tables():
    nodes = np.array(
        [
            -1.0,
            -0.8717401485096066,
            -0.5917001814331423,
            -0.2092992179024789,
            0.2092992179024789,
            0.5917001814331423,
            0.8717401485096066,
            1.0,
        ]
    )
    weight = np.array(
        [
            1.0 / 28.0,
            0.21070422714350603,
            0.3411226924835044,
            0.4124587946587038,
            0.4124587946587038,
            0.3411226924835044,
            0.21070422714350603,
            1.0 / 28.0,
        ]
    )
    bary = np.array(
        [1.0 / np.prod([nodes[i] - nodes[j] for j in range(8) if j != i]) for i in range(8)]
    )
    deriv = np.zeros((8, 8))
    for i in range(8):
        for j in range(8):
            if i != j:
                deriv[i, j] = bary[j] / bary[i] / (nodes[i] - nodes[j])
        deriv[i, i] = -np.sum(deriv[i])
    return weight, deriv


def halves(table):
    table = np.asarray(table, np.float32)
    high = table.astype(ml_dtypes.bfloat16)
    low = (table - high.astype(np.float32)).astype(ml_dtypes.bfloat16)
    return high, low


def tables():
    weight, deriv = gll_tables()
    ids = np.arange(10) + 1.0
    sine = np.sqrt(2.0 / 11.0) * np.sin(np.pi * np.outer(ids, ids) / 11.0)
    eig = 2.0 - 2.0 * np.cos(np.pi * ids / 11.0)
    dz = np.kron(deriv, np.eye(32))
    dy = np.kron(np.eye(32), deriv)
    grad = np.concatenate([dz, dy], axis=0)
    dx_t = np.kron(np.eye(EX), deriv.T)
    dx = np.kron(np.eye(EX), deriv)

    def ext_row(z, y):
        zlo, zhi, ylo, yhi = z < 0, z > 7, y < 0, y > 31
        if zlo or zhi:
            if ylo or yhi:
                return 336 + 2 * int(zhi) + int(yhi)
            return 256 + 32 * int(zhi) + y
        if ylo or yhi:
            return 320 + 8 * int(yhi) + z
        return 32 * z + y

    widen = np.zeros((SPEC, EXT))
    for zi in range(10):
        z = zi - 1
        for e in range(EY):
            for yi in range(10):
                y = 8 * e - 2 if yi == 0 else (8 * e + 9 if yi == 9 else 8 * e + yi - 1)
                widen[zi * 40 + e * 10 + yi, ext_row(z, y)] = 1.0
    spec_zy = np.kron(sine, np.kron(np.eye(EY), sine)) @ widen
    widen_x = np.zeros((160, 128))
    for e in range(EX):
        for xi in range(10):
            x = 8 * e - 2 if xi == 0 else (8 * e + 9 if xi == 9 else 8 * e + xi - 1)
            if 0 <= x < 128:
                widen_x[e * 10 + xi, x] = 1.0
    spec_x = np.zeros((128, 256))
    spec_x[:, :160] = (np.kron(np.eye(EX), sine) @ widen_x).T
    back_zy = np.kron(sine[1:9], np.kron(np.eye(EY), sine[1:9]))
    back_x = np.zeros((256, 128))
    back_x[:160] = np.kron(np.eye(EX), sine[1:9]).T
    lam_zy = (eig[:, None] + np.tile(eig, EY)[None, :]).reshape(SPEC)
    inv_den = np.zeros((SPEC, 256))
    inv_den[:, :160] = 1.0 / (
        SCHWARZ_SCALE * (lam_zy[:, None] + np.tile(eig, EX)[None, :]) + SCHWARZ_SHIFT
    )
    mass = 0.125 * (
        np.kron(weight, np.tile(weight, EY))[:, None] * np.tile(weight, EX)[None, :]
    )
    out = []
    for table in (grad, grad.T, dx_t, dx, spec_zy, spec_x, back_zy, back_x):
        out.extend(halves(table))
    spread = np.kron(np.eye(EX), np.ones((1, 8)))
    out += [inv_den.astype(np.float32), mass.astype(np.float32), spread.astype(np.float32)]
    return out


def split(v):
    high = v.astype(BF16)
    low = (v - high.astype(F32)).astype(BF16)
    return high, low


def dot(a, b):
    return jnp.dot(a, b, preferred_element_type=F32)


def left(high_ref, low_ref, v, rows=None):
    pick = slice(None) if rows is None else rows
    vh, vl = split(v)
    both = dot(high_ref[pick, :], jnp.concatenate([vh, vl], axis=1))
    return both[:, :128] + both[:, 128:] + dot(low_ref[pick, :], vh)


def right(v, high_ref, low_ref):
    vh, vl = split(v)
    return dot(vh, high_ref[...]) + dot(vl, high_ref[...]) + dot(vh, low_ref[...])


def total(v):
    return jnp.sum(jnp.sum(v, axis=0, keepdims=True), axis=1, keepdims=True)


def sweep_step(a, row, col, k, sub, lane):
    pivot = jnp.sum(jnp.where(lane[:1] == k, row, 0.0), axis=1, keepdims=True)
    row_m = jnp.where(lane[:1] == k, -1.0, row) / pivot
    col_m = jnp.where(sub == k, -1.0, col)
    return jnp.where(jnp.logical_or(lane == k, sub == k), 0.0, a) - col_m * row_m


def kernel(
    ngx, ngy,
    level_ref, vel_ref, source_ref, solid_ref,
    gh, gl, gth, gtl, dxth, dxtl, dxh, dxl, szh, szl, sxh, sxl, bzh, bzl, bxh, bxl,
    inv_den_ref, mass_ref, spread_ref,
    level_out, pressure_out,
    flux_ref, invm_ref, part_ref, lev_ref, app_ref, res_ref, search_ref, a_ref,
    zs, zr, ys, yr, cs, cr, gbuf,
    send_sem, recv_sem, gsend_sem, grecv_sem,
):
    n = ngx * ngy
    ix = lax.axis_index("gx")
    iy = lax.axis_index("gy")
    me = ix * ngy + iy

    zr[...] = jnp.zeros_like(zr)
    yr[...] = jnp.zeros_like(yr)
    cr[...] = jnp.zeros_like(cr)

    barrier = pltpu.get_barrier_semaphore()

    def greet(i, carry):
        dst = lax.rem(me + i, n)
        pl.semaphore_signal(
            barrier, inc=1, device_id=(dst // ngy, lax.rem(dst, ngy)), device_id_type=MESH
        )
        return carry

    lax.fori_loop(1, n, greet, 0)

    has_zlo, has_zhi = ix > 0, ix < ngx - 1
    has_ylo, has_yhi = iy > 0, iy < ngy - 1

    def exists(d):
        dz, dy = SIDES[d]
        conds = []
        if dz:
            conds.append(has_zlo if dz < 0 else has_zhi)
        if dy:
            conds.append(has_ylo if dy < 0 else has_yhi)
        return conds[0] if len(conds) == 1 else jnp.logical_and(*conds)

    def buffers(r, d, layers):
        if d < 2:
            return zs.at[r, d, pl.ds(0, 32 * layers)], zr.at[r, OPPOSITE[d], pl.ds(0, 32 * layers)]
        if d < 4:
            return (
                ys.at[r, d - 2, pl.ds(0, 8 * layers)],
                yr.at[r, OPPOSITE[d] - 2, pl.ds(0, 8 * layers)],
            )
        return cs.at[r, d - 4], cr.at[r, OPPOSITE[d] - 4]

    def halo_copy(r, d, layers):
        src, dst = buffers(r, d, layers)
        dz, dy = SIDES[d]
        return pltpu.make_async_remote_copy(
            src_ref=src,
            dst_ref=dst,
            send_sem=send_sem.at[r, d],
            recv_sem=recv_sem.at[r, OPPOSITE[d]],
            device_id=(ix + dz, iy + dy),
            device_id_type=MESH,
        )

    def halo_send(r, layers, second=None):
        for s in range(2):
            zo, zi = ((0, 32), (224, 192))[s]
            zs[r, s, 0:32] = part_ref[zo : zo + 32]
            yo, yi = ((0, 1), (31, 30))[s]
            ys[r, s, 0:8] = part_ref[pl.ds(yo, 8, stride=32), :]
            if layers > 1:
                zs[r, s, 32:64] = part_ref[zi : zi + 32]
                ys[r, s, 8:16] = part_ref[pl.ds(yi, 8, stride=32), :]
            if second is not None:
                zs[r, s, 64:96] = second[zo : zo + 32]
                ys[r, s, 16:24] = second[pl.ds(yo, 8, stride=32), :]
        for c in range(4):
            dz, dy = SIDES[4 + c]
            zo, zi = (0, 32) if dz < 0 else (224, 192)
            yo, yi = (0, 1) if dy < 0 else (31, 30)
            cs[r, c, 0:1] = part_ref[zo + yo : zo + yo + 1]
            if layers > 1:
                cs[r, c, 1:2] = part_ref[zo + yi : zo + yi + 1]
                cs[r, c, 2:3] = part_ref[zi + yo : zi + yo + 1]
                cs[r, c, 3:4] = part_ref[zi + yi : zi + yi + 1]
            if second is not None:
                cs[r, c, 4:5] = second[zo + yo : zo + yo + 1]
        for d in range(8):

            @pl.when(exists(d))
            def _():
                halo_copy(r, d, layers).start()

    def halo_wait(r, layers):
        for d in range(8):

            @pl.when(exists(d))
            def _():
                src, _ = buffers(r, d, layers)
                _, dst = buffers(r, OPPOSITE[d], layers)
                dz, dy = SIDES[d]
                pltpu.make_async_remote_copy(
                    src_ref=src,
                    dst_ref=dst,
                    send_sem=send_sem.at[r, d],
                    recv_sem=recv_sem.at[r, d],
                    device_id=(ix + dz, iy + dy),
                    device_id_type=MESH,
                ).wait_recv()

    def halo_drain(r, layers):
        for d in range(8):

            @pl.when(exists(d))
            def _():
                halo_copy(r, d, layers).wait_send()

    def add_rim(r, ref, zoff, yoff, crow):
        ref[0:32] = ref[0:32] + zr[r, 0, zoff : zoff + 32]
        ref[224:256] = ref[224:256] + zr[r, 1, zoff : zoff + 32]
        for s, yo in ((0, 0), (1, 31)):
            at = pl.ds(yo, 8, stride=32)
            ref[at, :] = ref[at, :] + yr[r, s, yoff : yoff + 8]
        for c, row in enumerate((0, 31, 224, 255)):
            ref[row : row + 1] = ref[row : row + 1] + cr[r, c, crow : crow + 1]

    def outer_halo(r, ref):
        for s in range(2):
            base = 256 + 32 * s
            ref[base : base + 32] = zr[r, s, 32:64]
            ref[base : base + 1] = ref[base : base + 1] + cr[r, 2 * s, 2:3]
            ref[base + 31 : base + 32] = ref[base + 31 : base + 32] + cr[r, 2 * s + 1, 2:3]
            base = 320 + 8 * s
            ref[base : base + 8] = yr[r, s, 8:16]
            ref[base : base + 1] = ref[base : base + 1] + cr[r, s, 1:2]
            ref[base + 7 : base + 8] = ref[base + 7 : base + 8] + cr[r, 2 + s, 1:2]
        ref[336:384] = jnp.zeros((48, 128), F32)
        for c in range(4):
            ref[336 + c : 337 + c] = cr[r, c, 3:4]

    def gather_copy(g, dst):
        return pltpu.make_async_remote_copy(
            src_ref=gbuf.at[g, me],
            dst_ref=gbuf.at[g, me],
            send_sem=gsend_sem.at[g],
            recv_sem=grecv_sem.at[g],
            device_id=(dst // ngy, lax.rem(dst, ngy)),
            device_id_type=MESH,
        )

    def gather_send(g, first, second=None):
        gbuf[g, me, 0:1] = jnp.broadcast_to(first, (1, 128))
        if second is not None:
            gbuf[g, me, 1:2] = jnp.broadcast_to(second, (1, 128))

        def send(i, carry):
            gather_copy(g, lax.rem(me + i, n)).start()
            return carry

        lax.fori_loop(1, n, send, 0)

    def gather_bytes(g, sem):
        ref = gbuf.at[g, pl.ds(0, n - 1)]
        pltpu.make_async_copy(ref, ref, sem).wait()

    def gather_wait(g):
        gather_bytes(g, grecv_sem.at[g])

    row = lax.broadcasted_iota(jnp.int32, (ROWS, 128), 0)
    lane = lax.broadcasted_iota(jnp.int32, (ROWS, 128), 1)
    zpos, ypos = row // 32, row % 32
    y8, x8 = row % 8, lane % 8
    y_first = jnp.logical_and(y8 == 0, ypos > 0).astype(F32)
    y_last = jnp.logical_and(y8 == 7, ypos < 31).astype(F32)
    x_first = jnp.logical_and(x8 == 0, lane > 0).astype(F32)
    x_last = jnp.logical_and(x8 == 7, lane < 127).astype(F32)

    def flag(c):
        return c.astype(jnp.int32).astype(F32)

    zlo_f, zhi_f, ylo_f, yhi_f = flag(has_zlo), flag(has_zhi), flag(has_ylo), flag(has_yhi)
    z0, z7 = (zpos == 0).astype(F32), (zpos == 7).astype(F32)
    yb0, yb31 = (ypos == 0).astype(F32), (ypos == 31).astype(F32)
    half_zlo, half_zhi = 0.5 * zlo_f * z0, 0.5 * zhi_f * z7
    half_ylo, half_yhi = 0.5 * ylo_f * yb0, 0.5 * yhi_f * yb31
    own_z, own_y = 1.0 - half_zlo - half_zhi, 1.0 - half_ylo - half_yhi
    inv_m = (
        own_z
        * (own_y - 0.5 * (y_first + y_last))
        * (1.0 - 0.5 * (x_first + x_last))
    )
    invm_ref[...] = inv_m

    def fold_in(v):
        v = v + x_first * pltpu.roll(v, 1, 1) + x_last * pltpu.roll(v, 127, 1)
        return v + y_first * pltpu.roll(v, 1, 0) + y_last * pltpu.roll(v, ROWS - 1, 0)

    mass = mass_ref[...]
    level = level_ref[...]
    grads = left(gh, gl, level)
    advect = (
        vel_ref[0:ROWS] * grads[:ROWS]
        + vel_ref[ROWS : 2 * ROWS] * grads[ROWS:]
        + vel_ref[2 * ROWS : 3 * ROWS] * right(level, dxth, dxtl)
    )
    lev_ref[...] = fold_in(mass * (level - (2.0 * TIME_STEP) * advect))
    diverge = (
        left(gh, gl, vel_ref[0:ROWS], slice(0, ROWS))
        + left(gh, gl, vel_ref[ROWS : 2 * ROWS], slice(ROWS, 2 * ROWS))
        + right(vel_ref[2 * ROWS : 3 * ROWS], dxth, dxtl)
    )
    part_ref[...] = fold_in(mass * (source_ref[...] - (2.0 * TIME_STEP) * diverge))

    pl.semaphore_wait(barrier, n - 1)
    halo_send(0, 3, lev_ref)
    res_ref[0:ROWS] = part_ref[...]
    solid = dot(solid_ref[0].astype(F32), spread_ref[...])
    solid = jnp.concatenate(
        [jnp.broadcast_to(solid[e : e + 1], (8, 128)) for e in range(EY)], axis=0
    )
    solid = jnp.concatenate([solid] * 8, axis=0)
    halo_wait(0, 3)
    add_rim(0, res_ref, 0, 0, 0)
    add_rim(0, lev_ref, 64, 16, 4)
    outer_halo(0, res_ref)
    level_new = lev_ref[...] * inv_m / mass
    level_out[...] = level_new
    coef = (GAS_RATIO - (GAS_RATIO - 1.0) * jax.nn.sigmoid(level_new / LEVEL_WIDTH)) * (
        1.0 - (1.0 - SOLID_FACTOR) * solid
    )
    flux_ref[...] = 4.0 * coef * mass
    gather_send(0, total(coef) / (ROWS * 128.0), total(res_ref[0:ROWS] * inv_m))

    def local_solve():
        spectral = right(left(szh, szl, res_ref[...]), sxh, sxl) * inv_den_ref[...]
        return left(bzh, bzl, right(spectral, bxh, bxl))

    def helm(v):
        grads = left(gh, gl, v)
        flux = flux_ref[...]
        out = left(gth, gtl, jnp.concatenate([flux * grads[:ROWS], flux * grads[ROWS:]], axis=0))
        out = out + right(flux * right(v, dxth, dxtl), dxh, dxl)
        return out + HELM_COEF * mass_ref[...] * v

    npad = a_ref.shape[1]
    sub_n = lax.broadcasted_iota(jnp.int32, (n, npad), 0)
    lane_n = lax.broadcasted_iota(jnp.int32, (n, npad), 1)

    def gathered(g, item):
        got = gbuf[g, :, item, :]
        return got if npad == 128 else jnp.concatenate([got] * (npad // 128), axis=1)

    def invert(k_col):
        diag = lane_n == sub_n
        k_row = jnp.sum(jnp.where(diag, k_col, 0.0), axis=0, keepdims=True)
        gap = lane_n - sub_n
        same = lane_n // ngy == sub_n // ngy
        y_link = jnp.logical_and(jnp.logical_or(gap == 1, gap == -1), same)
        z_link = jnp.logical_or(gap == ngy, gap == -ngy)
        rate = jnp.where(z_link, float(EY * EX) / EZ, 0.0) + jnp.where(
            y_link, float(EZ * EX) / EY, 0.0
        )
        rate = jnp.where(lane_n < n, rate, 0.0)
        link = 2.0 * k_col * k_row / (k_col + k_row) * rate
        diagonal = HELM_COEF * EZ * EY * EX + jnp.sum(link, axis=1, keepdims=True)
        a = jnp.where(diag, diagonal, -link)
        if n <= 64:
            for k in range(n):
                a = sweep_step(a, a[k : k + 1, :], a[:, k : k + 1], k, sub_n, lane_n)
            a_ref[...] = a
        else:
            a_ref[...] = a

            def step(k, carry):
                a = a_ref[...]
                row = a_ref[pl.ds(k, 1), :]
                col = jnp.sum(jnp.where(lane_n == k, a, 0.0), axis=1, keepdims=True)
                a_ref[...] = sweep_step(a, row, col, k, sub_n, lane_n)
                return carry

            lax.fori_loop(0, n, step, 0)

    def coarse(t_col):
        x = -jnp.sum(a_ref[...] * t_col, axis=0, keepdims=True)
        t_row = jnp.sum(jnp.where(lane_n == sub_n, t_col, 0.0), axis=0, keepdims=True)
        return x, jnp.sum(x * t_row, axis=1, keepdims=True)

    def coarse_field(x):
        def value(dz, dy):
            at = me + dz * ngy + dy
            return jnp.sum(jnp.where(lane_n[:1] == at, x, 0.0), axis=1, keepdims=True)

        def along_y(dz):
            return own_y * value(dz, 0) + half_ylo * value(dz, -1) + half_yhi * value(dz, 1)

        return own_z * along_y(0) + half_zlo * along_y(-1) + half_zhi * along_y(1)

    local = local_solve() * inv_m
    part_ref[...] = fold_in(local)
    halo_send(1, 1)
    rz_part = total(res_ref[0:ROWS] * local)
    gather_wait(0)
    invert(gathered(0, 0))
    x, rz_coarse = coarse(gathered(0, 1))
    field = coarse_field(x)
    halo_wait(1, 1)
    search_ref[...] = part_ref[...]
    add_rim(1, search_ref, 0, 0, 0)
    search = search_ref[...] + field
    search_ref[...] = search

    applied = helm(search)
    gather_send(1, rz_part, total(search * applied))
    part_ref[...] = fold_in(applied)
    halo_send(2, 2)
    app_ref[0:ROWS] = part_ref[...]
    halo_wait(2, 2)
    add_rim(2, app_ref, 0, 0, 0)
    outer_halo(2, app_ref)
    gather_wait(1)
    sums = jnp.sum(gbuf[1], axis=0)
    rz_now = sums[0:1, 0:1] + rz_coarse
    step_len = rz_now / sums[1:2, 0:1]
    pressure = step_len * search
    res_ref[...] = res_ref[...] - step_len * app_ref[...]
    gather_send(2, total(res_ref[0:ROWS] * invm_ref[...]))

    local = local_solve() * invm_ref[...]
    part_ref[...] = fold_in(local)
    halo_send(3, 1)
    gather_send(3, total(res_ref[0:ROWS] * local))
    gather_wait(2)
    x, rz_coarse = coarse(gathered(2, 0))
    field = coarse_field(x)
    halo_wait(3, 1)
    add_rim(3, part_ref, 0, 0, 0)
    gather_wait(3)
    sums = jnp.sum(gbuf[3], axis=0)
    rz_next = sums[0:1, 0:1] + rz_coarse
    search = part_ref[...] + field + (rz_next / rz_now) * search_ref[...]

    applied = helm(search)
    gather_send(4, total(search * applied))
    gather_wait(4)
    sums = jnp.sum(gbuf[4], axis=0)
    pressure_out[...] = pressure + (rz_next / sums[0:1, 0:1]) * search

    for r, layers in enumerate((3, 1, 2, 1)):
        halo_drain(r, layers)
    for g in range(5):
        gather_bytes(g, gsend_sem.at[g])


def body(ngx, ngy, level_set, velocity, source, wick_solid):
    n = ngx * ngy
    npad = -(-n // 128) * 128
    consts = [jnp.asarray(t) for t in tables()]
    vmem = pl.BlockSpec(memory_space=pltpu.VMEM)
    shape = level_set.shape
    level_new, pressure = pl.pallas_call(
        functools.partial(kernel, ngx, ngy),
        out_shape=[jax.ShapeDtypeStruct((ROWS, 128), F32)] * 2,
        in_specs=[vmem] * (4 + len(consts)),
        out_specs=[vmem] * 2,
        scratch_shapes=[
            pltpu.VMEM((ROWS, 128), F32),
            pltpu.VMEM((ROWS, 128), F32),
            pltpu.VMEM((ROWS, 128), F32),
            pltpu.VMEM((ROWS, 128), F32),
            pltpu.VMEM((EXT, 128), F32),
            pltpu.VMEM((EXT, 128), F32),
            pltpu.VMEM((ROWS, 128), F32),
            pltpu.VMEM((n, npad), F32),
            pltpu.VMEM((4, 2, 96, 128), F32),
            pltpu.VMEM((4, 2, 96, 128), F32),
            pltpu.VMEM((4, 2, 24, 128), F32),
            pltpu.VMEM((4, 2, 24, 128), F32),
            pltpu.VMEM((4, 4, 8, 128), F32),
            pltpu.VMEM((4, 4, 8, 128), F32),
            pltpu.VMEM((5, n, 2, 128), F32),
            pltpu.SemaphoreType.DMA((4, 8)),
            pltpu.SemaphoreType.DMA((4, 8)),
            pltpu.SemaphoreType.DMA((5,)),
            pltpu.SemaphoreType.DMA((5,)),
        ],
        compiler_params=pltpu.CompilerParams(
            collective_id=0, has_side_effects=True, vmem_limit_bytes=48 * 1024 * 1024
        ),
    )(
        level_set.reshape(ROWS, 128),
        velocity.reshape(3 * ROWS, 128),
        source.reshape(ROWS, 128),
        wick_solid,
        *consts,
    )
    return level_new.reshape(shape), pressure.reshape(shape)


def solution(mesh):
    placed = (
        P("gx", "gy", None),
        P(None, "gx", "gy", None),
        P("gx", "gy", None),
        P("gx", "gy", None),
    )
    return jax.shard_map(
        functools.partial(body, mesh.shape["gx"], mesh.shape["gy"]),
        mesh=mesh,
        in_specs=placed,
        out_specs=(P("gx", "gy", None), P("gx", "gy", None)),
        check_vma=False,
    )
```

```python
import functools

import jax
import jax.numpy as jnp
import ml_dtypes
import numpy as np
from jax import lax
from jax.experimental import pallas as pl
from jax.experimental.pallas import tpu as pltpu
from jax.sharding import PartitionSpec as P

EZ = 1
EY = 4
EX = 16
ROWS = 256
EXT = 384
SPEC = 400

TIME_STEP = 0.02
HELM_COEF = 0.25
LEVEL_WIDTH = 0.25
GAS_RATIO = 10.0
SOLID_FACTOR = 0.25
SCHWARZ_SCALE = 0.5
SCHWARZ_SHIFT = 0.05

MESH = pl.DeviceIdType.MESH
LOGICAL = pl.DeviceIdType.LOGICAL
F32 = jnp.float32
BF16 = jnp.bfloat16

SIDES = ((-1, 0), (1, 0), (0, -1), (0, 1), (-1, -1), (-1, 1), (1, -1), (1, 1))
OPPOSITE = tuple(SIDES.index((-dz, -dy)) for dz, dy in SIDES)


def gll_tables():
    nodes = np.array(
        [
            -1.0,
            -0.8717401485096066,
            -0.5917001814331423,
            -0.2092992179024789,
            0.2092992179024789,
            0.5917001814331423,
            0.8717401485096066,
            1.0,
        ]
    )
    weight = np.array(
        [
            1.0 / 28.0,
            0.21070422714350603,
            0.3411226924835044,
            0.4124587946587038,
            0.4124587946587038,
            0.3411226924835044,
            0.21070422714350603,
            1.0 / 28.0,
        ]
    )
    bary = np.array(
        [1.0 / np.prod([nodes[i] - nodes[j] for j in range(8) if j != i]) for i in range(8)]
    )
    deriv = np.zeros((8, 8))
    for i in range(8):
        for j in range(8):
            if i != j:
                deriv[i, j] = bary[j] / bary[i] / (nodes[i] - nodes[j])
        deriv[i, i] = -np.sum(deriv[i])
    return weight, deriv


def halves(table):
    table = np.asarray(table, np.float32)
    high = table.astype(ml_dtypes.bfloat16)
    low = (table - high.astype(np.float32)).astype(ml_dtypes.bfloat16)
    return high, low


def tables():
    weight, deriv = gll_tables()
    ids = np.arange(10) + 1.0
    sine = np.sqrt(2.0 / 11.0) * np.sin(np.pi * np.outer(ids, ids) / 11.0)
    eig = 2.0 - 2.0 * np.cos(np.pi * ids / 11.0)
    dy = np.kron(np.eye(32), deriv)
    dx_t = np.kron(np.eye(EX), deriv.T)
    dx = np.kron(np.eye(EX), deriv)

    def ext_row(z, y):
        zlo, zhi, ylo, yhi = z < 0, z > 7, y < 0, y > 31
        if zlo or zhi:
            if ylo or yhi:
                return 336 + 2 * int(zhi) + int(yhi)
            return 256 + 32 * int(zhi) + y
        if ylo or yhi:
            return 320 + 8 * int(yhi) + z
        return 32 * z + y

    widen = np.zeros((SPEC, EXT))
    for zi in range(10):
        z = zi - 1
        for e in range(EY):
            for yi in range(10):
                y = 8 * e - 2 if yi == 0 else (8 * e + 9 if yi == 9 else 8 * e + yi - 1)
                widen[zi * 40 + e * 10 + yi, ext_row(z, y)] = 1.0
    spec_zy = np.kron(sine, np.kron(np.eye(EY), sine)) @ widen
    widen_x = np.zeros((160, 128))
    for e in range(EX):
        for xi in range(10):
            x = 8 * e - 2 if xi == 0 else (8 * e + 9 if xi == 9 else 8 * e + xi - 1)
            if 0 <= x < 128:
                widen_x[e * 10 + xi, x] = 1.0
    spec_x = np.zeros((128, 256))
    spec_x[:, :160] = (np.kron(np.eye(EX), sine) @ widen_x).T
    back_zy = np.kron(sine[1:9], np.kron(np.eye(EY), sine[1:9]))
    back_x = np.zeros((256, 128))
    back_x[:160] = np.kron(np.eye(EX), sine[1:9]).T
    lam_zy = (eig[:, None] + np.tile(eig, EY)[None, :]).reshape(SPEC)
    inv_den = np.zeros((SPEC, 256))
    inv_den[:, :160] = 1.0 / (
        SCHWARZ_SCALE * (lam_zy[:, None] + np.tile(eig, EX)[None, :]) + SCHWARZ_SHIFT
    )
    mass = 0.125 * (
        np.kron(weight, np.tile(weight, EY))[:, None] * np.tile(weight, EX)[None, :]
    )
    spread = np.zeros((16, 128))
    spread[:EX] = np.kron(np.eye(EX), np.ones((1, 8)))

    def stack(*parts):
        return np.concatenate([half for part in parts for half in halves(part)], axis=0)

    return (
        stack(dy, dy.T, spec_x),
        stack(dx_t, dx, back_x),
        np.concatenate([mass, spread], axis=0).astype(np.float32),
        stack(spec_zy),
        inv_den.astype(np.float32),
        stack(back_zy),
    )


def split(v):
    high = v.astype(BF16)
    low = (v - high.astype(F32)).astype(BF16)
    return high, low


def dot(a, b):
    return jnp.dot(a, b, preferred_element_type=F32)


def left(ref, base, rows, v):
    vh, vl = split(v)
    both = dot(ref[base : base + rows, :], jnp.concatenate([vh, vl], axis=1))
    return both[:, :128] + both[:, 128:] + dot(ref[base + rows : base + 2 * rows, :], vh)


def right(v, ref, base, rows):
    vh, vl = split(v)
    high = ref[base : base + rows, :]
    return dot(vh, high) + dot(vl, high) + dot(vh, ref[base + rows : base + 2 * rows, :])


def along_z(v, table):
    planes = [v[32 * i : 32 * i + 32] for i in range(8)]
    even = [planes[j] + planes[7 - j] for j in range(4)]
    odd = [planes[j] - planes[7 - j] for j in range(4)]
    low, high = [], []
    for i in range(4):
        a = b = None
        for j in range(4):
            p = float(table[i, j] + table[i, 7 - j]) / 2.0 * even[j]
            q = float(table[i, j] - table[i, 7 - j]) / 2.0 * odd[j]
            a, b = (p, q) if a is None else (a + p, b + q)
        low.append(a + b)
        high.insert(0, b - a)
    return jnp.concatenate(low + high, axis=0)


def total(v):
    return jnp.sum(jnp.sum(v, axis=0, keepdims=True), axis=1, keepdims=True)


def sweep_step(a, row, col, k, sub, lane):
    pivot = jnp.sum(jnp.where(lane[:1] == k, row, 0.0), axis=1, keepdims=True)
    row_m = jnp.where(lane[:1] == k, -1.0, row) / pivot
    col_m = jnp.where(sub == k, -1.0, col)
    return jnp.where(jnp.logical_or(lane == k, sub == k), 0.0, a) - col_m * row_m


def kernel(
    ngx, ngy, deriv,
    level_hbm, vel_hbm, source_hbm, solid_hbm, *refs
):
    tables_hbm, refs = refs[:6], refs[6:]
    level_out, pressure_out = refs[:2]
    (
        flux_ref, invm_ref, part_ref, lev_ref, app_ref, res_ref, search_ref, a_ref,
        zs, zr, ys, yr, cs, cr, gbuf,
        level_ref, vel_ref, source_ref, solid_ref,
        t256, t128, mass_ref, spec_ref, den_ref, back_ref,
        send_sem, recv_sem, gsend_sem, grecv_sem, load_sem,
    ) = refs[2:]
    loads = [
        pltpu.make_async_copy(src, dst, load_sem.at[i])
        for i, (src, dst) in enumerate(
            zip(
                (level_hbm, vel_hbm, source_hbm, solid_hbm) + tables_hbm,
                (level_ref, vel_ref, source_ref, solid_ref)
                + (t256, t128, mass_ref, spec_ref, den_ref, back_ref),
            )
        )
    ]
    for i in (4, 5, 0, 1, 6, 2, 3, 7, 8, 9):
        loads[i].start()
    n = ngx * ngy
    ix = lax.axis_index("gx")
    iy = lax.axis_index("gy")
    me = ix * ngy + iy

    def other(i):
        at = me + i
        return jnp.where(at >= n, at - n, at)

    zr[...] = jnp.zeros_like(zr)
    yr[...] = jnp.zeros_like(yr)
    cr[...] = jnp.zeros_like(cr)

    barrier = pltpu.get_barrier_semaphore()

    def greet(i, carry):
        pl.semaphore_signal(barrier, inc=1, device_id=other(i), device_id_type=LOGICAL)
        return carry

    lax.fori_loop(1, n, greet, 0, unroll=n <= 64)

    has_zlo, has_zhi = ix > 0, ix < ngx - 1
    has_ylo, has_yhi = iy > 0, iy < ngy - 1

    def exists(d):
        dz, dy = SIDES[d]
        conds = []
        if dz:
            conds.append(has_zlo if dz < 0 else has_zhi)
        if dy:
            conds.append(has_ylo if dy < 0 else has_yhi)
        return conds[0] if len(conds) == 1 else jnp.logical_and(*conds)

    def buffers(r, d, layers):
        if d < 2:
            return zs.at[r, d, pl.ds(0, 32 * layers)], zr.at[r, OPPOSITE[d], pl.ds(0, 32 * layers)]
        if d < 4:
            return (
                ys.at[r, d - 2, pl.ds(0, 8 * layers)],
                yr.at[r, OPPOSITE[d] - 2, pl.ds(0, 8 * layers)],
            )
        return cs.at[r, d - 4], cr.at[r, OPPOSITE[d] - 4]

    def halo_copy(r, d, layers):
        src, dst = buffers(r, d, layers)
        dz, dy = SIDES[d]
        return pltpu.make_async_remote_copy(
            src_ref=src,
            dst_ref=dst,
            send_sem=send_sem.at[r, d],
            recv_sem=recv_sem.at[r, OPPOSITE[d]],
            device_id=(ix + dz, iy + dy),
            device_id_type=MESH,
        )

    def halo_send(r, layers, second=None):
        for s in range(2):
            zo, zi = ((0, 32), (224, 192))[s]
            zs[r, s, 0:32] = part_ref[zo : zo + 32]
            yo, yi = ((0, 1), (31, 30))[s]
            ys[r, s, 0:8] = part_ref[pl.ds(yo, 8, stride=32), :]
            if layers > 1:
                zs[r, s, 32:64] = part_ref[zi : zi + 32]
                ys[r, s, 8:16] = part_ref[pl.ds(yi, 8, stride=32), :]
            if second is not None:
                zs[r, s, 64:96] = second[zo : zo + 32]
                ys[r, s, 16:24] = second[pl.ds(yo, 8, stride=32), :]
        for c in range(4):
            dz, dy = SIDES[4 + c]
            zo, zi = (0, 32) if dz < 0 else (224, 192)
            yo, yi = (0, 1) if dy < 0 else (31, 30)
            cs[r, c, 0:1] = part_ref[zo + yo : zo + yo + 1]
            if layers > 1:
                cs[r, c, 1:2] = part_ref[zo + yi : zo + yi + 1]
                cs[r, c, 2:3] = part_ref[zi + yo : zi + yo + 1]
                cs[r, c, 3:4] = part_ref[zi + yi : zi + yi + 1]
            if second is not None:
                cs[r, c, 4:5] = second[zo + yo : zo + yo + 1]
        for d in range(8):

            @pl.when(exists(d))
            def _():
                halo_copy(r, d, layers).start()

    def halo_wait(r, layers):
        for d in range(8):

            @pl.when(exists(d))
            def _():
                src, _ = buffers(r, d, layers)
                _, dst = buffers(r, OPPOSITE[d], layers)
                dz, dy = SIDES[d]
                pltpu.make_async_remote_copy(
                    src_ref=src,
                    dst_ref=dst,
                    send_sem=send_sem.at[r, d],
                    recv_sem=recv_sem.at[r, d],
                    device_id=(ix + dz, iy + dy),
                    device_id_type=MESH,
                ).wait_recv()

    def halo_drain(r, layers):
        for d in range(8):

            @pl.when(exists(d))
            def _():
                halo_copy(r, d, layers).wait_send()

    def add_rim(r, ref, zoff, yoff, crow):
        ref[0:32] = ref[0:32] + zr[r, 0, zoff : zoff + 32]
        ref[224:256] = ref[224:256] + zr[r, 1, zoff : zoff + 32]
        for s, yo in ((0, 0), (1, 31)):
            at = pl.ds(yo, 8, stride=32)
            ref[at, :] = ref[at, :] + yr[r, s, yoff : yoff + 8]
        for c, row in enumerate((0, 31, 224, 255)):
            ref[row : row + 1] = ref[row : row + 1] + cr[r, c, crow : crow + 1]

    def outer_halo(r, ref):
        for s in range(2):
            base = 256 + 32 * s
            ref[base : base + 32] = zr[r, s, 32:64]
            ref[base : base + 1] = ref[base : base + 1] + cr[r, 2 * s, 2:3]
            ref[base + 31 : base + 32] = ref[base + 31 : base + 32] + cr[r, 2 * s + 1, 2:3]
            base = 320 + 8 * s
            ref[base : base + 8] = yr[r, s, 8:16]
            ref[base : base + 1] = ref[base : base + 1] + cr[r, s, 1:2]
            ref[base + 7 : base + 8] = ref[base + 7 : base + 8] + cr[r, 2 + s, 1:2]
        ref[336:384] = jnp.zeros((48, 128), F32)
        for c in range(4):
            ref[336 + c : 337 + c] = cr[r, c, 3:4]

    def gather_copy(g, dst):
        return pltpu.make_async_remote_copy(
            src_ref=gbuf.at[g, me],
            dst_ref=gbuf.at[g, me],
            send_sem=gsend_sem.at[g],
            recv_sem=grecv_sem.at[g],
            device_id=dst,
            device_id_type=LOGICAL,
        )

    def gather_send(g, first, second=None):
        gbuf[g, me, 0:1] = jnp.broadcast_to(first, (1, 128))
        if second is not None:
            gbuf[g, me, 1:2] = jnp.broadcast_to(second, (1, 128))

        def send(i, carry):
            gather_copy(g, other(i)).start()
            return carry

        lax.fori_loop(1, n, send, 0, unroll=n <= 64)

    def gather_bytes(g, sem):
        ref = gbuf.at[g, pl.ds(0, n - 1)]
        pltpu.make_async_copy(ref, ref, sem).wait()

    def gather_wait(g):
        gather_bytes(g, grecv_sem.at[g])

    row = lax.broadcasted_iota(jnp.int32, (ROWS, 128), 0)
    lane = lax.broadcasted_iota(jnp.int32, (ROWS, 128), 1)
    zpos, ypos = row // 32, row % 32
    y8, x8 = row % 8, lane % 8
    y_first = jnp.logical_and(y8 == 0, ypos > 0).astype(F32)
    y_last = jnp.logical_and(y8 == 7, ypos < 31).astype(F32)
    x_first = jnp.logical_and(x8 == 0, lane > 0).astype(F32)
    x_last = jnp.logical_and(x8 == 7, lane < 127).astype(F32)

    def flag(c):
        return c.astype(jnp.int32).astype(F32)

    zlo_f, zhi_f, ylo_f, yhi_f = flag(has_zlo), flag(has_zhi), flag(has_ylo), flag(has_yhi)
    z0, z7 = (zpos == 0).astype(F32), (zpos == 7).astype(F32)
    yb0, yb31 = (ypos == 0).astype(F32), (ypos == 31).astype(F32)
    half_zlo, half_zhi = 0.5 * zlo_f * z0, 0.5 * zhi_f * z7
    half_ylo, half_yhi = 0.5 * ylo_f * yb0, 0.5 * yhi_f * yb31
    own_z, own_y = 1.0 - half_zlo - half_zhi, 1.0 - half_ylo - half_yhi
    inv_m = (
        own_z
        * (own_y - 0.5 * (y_first + y_last))
        * (1.0 - 0.5 * (x_first + x_last))
    )
    invm_ref[...] = inv_m

    def fold_in(v):
        v = v + x_first * pltpu.roll(v, 1, 1) + x_last * pltpu.roll(v, 127, 1)
        return v + y_first * pltpu.roll(v, 1, 0) + y_last * pltpu.roll(v, ROWS - 1, 0)

    for i in (4, 5, 0, 1, 6):
        loads[i].wait()
    mass = mass_ref[0:ROWS]
    level = level_ref[...]
    advect = (
        vel_ref[0:ROWS] * along_z(level, deriv)
        + vel_ref[ROWS : 2 * ROWS] * left(t256, 0, ROWS, level)
        + vel_ref[2 * ROWS : 3 * ROWS] * right(level, t128, 0, 128)
    )
    lev_ref[...] = fold_in(mass * (level - (2.0 * TIME_STEP) * advect))
    diverge = (
        along_z(vel_ref[0:ROWS], deriv)
        + left(t256, 0, ROWS, vel_ref[ROWS : 2 * ROWS])
        + right(vel_ref[2 * ROWS : 3 * ROWS], t128, 0, 128)
    )
    loads[2].wait()
    part_ref[...] = fold_in(mass * (source_ref[...] - (2.0 * TIME_STEP) * diverge))

    pl.semaphore_wait(barrier, n - 1)
    halo_send(0, 3, lev_ref)
    res_ref[0:ROWS] = part_ref[...]
    loads[3].wait()
    solid = dot(solid_ref[0].astype(F32), mass_ref[ROWS : ROWS + EX])
    solid = jnp.concatenate(
        [jnp.broadcast_to(solid[e : e + 1], (8, 128)) for e in range(EY)], axis=0
    )
    solid = jnp.concatenate([solid] * 8, axis=0)
    halo_wait(0, 3)
    add_rim(0, res_ref, 0, 0, 0)
    add_rim(0, lev_ref, 64, 16, 4)
    outer_halo(0, res_ref)
    level_new = lev_ref[...] * inv_m / mass
    level_out[...] = level_new
    coef = (GAS_RATIO - (GAS_RATIO - 1.0) * jax.nn.sigmoid(level_new / LEVEL_WIDTH)) * (
        1.0 - (1.0 - SOLID_FACTOR) * solid
    )
    flux_ref[...] = 4.0 * coef * mass
    gather_send(0, total(coef) / (ROWS * 128.0), total(res_ref[0:ROWS] * inv_m))

    def local_solve():
        spectral = right(left(spec_ref, 0, SPEC, res_ref[...]), t256, 4 * ROWS, 128)
        spectral = spectral * den_ref[...]
        return left(back_ref, 0, ROWS, right(spectral, t128, 512, 256))

    def helm(v):
        flux = flux_ref[...]
        out = along_z(flux * along_z(v, deriv), deriv.T)
        out = out + left(t256, 2 * ROWS, ROWS, flux * left(t256, 0, ROWS, v))
        out = out + right(flux * right(v, t128, 0, 128), t128, 256, 128)
        return out + HELM_COEF * mass_ref[0:ROWS] * v

    npad = a_ref.shape[1]
    sub_n = lax.broadcasted_iota(jnp.int32, (n, npad), 0)
    lane_n = lax.broadcasted_iota(jnp.int32, (n, npad), 1)

    def gathered(g, item):
        got = gbuf[g, :, item, :]
        return got if npad == 128 else jnp.concatenate([got] * (npad // 128), axis=1)

    def invert(k_col):
        diag = lane_n == sub_n
        k_row = jnp.sum(jnp.where(diag, k_col, 0.0), axis=0, keepdims=True)
        gap = lane_n - sub_n
        same = lane_n // ngy == sub_n // ngy
        y_link = jnp.logical_and(jnp.logical_or(gap == 1, gap == -1), same)
        z_link = jnp.logical_or(gap == ngy, gap == -ngy)
        rate = jnp.where(z_link, float(EY * EX) / EZ, 0.0) + jnp.where(
            y_link, float(EZ * EX) / EY, 0.0
        )
        rate = jnp.where(lane_n < n, rate, 0.0)
        link = 2.0 * k_col * k_row / (k_col + k_row) * rate
        diagonal = HELM_COEF * EZ * EY * EX + jnp.sum(link, axis=1, keepdims=True)
        a = jnp.where(diag, diagonal, -link)
        if n <= 64:
            for k in range(n):
                col = jnp.broadcast_to(a[:, k : k + 1], (n, npad))
                row_m = jnp.where(lane_n[:1] == k, -1.0, a[k : k + 1, :]) / col[k : k + 1, :]
                col_m = jnp.where(sub_n == k, -1.0, col)
                cross = jnp.logical_or(lane_n == k, sub_n == k)
                a = jnp.where(cross, 0.0, a) - col_m * row_m
            a_ref[...] = a
        else:
            a_ref[...] = a

            def step(k, carry):
                a = a_ref[...]
                row = a_ref[pl.ds(k, 1), :]
                col = jnp.sum(jnp.where(lane_n == k, a, 0.0), axis=1, keepdims=True)
                a_ref[...] = sweep_step(a, row, col, k, sub_n, lane_n)
                return carry

            lax.fori_loop(0, n, step, 0)

    def coarse(t_col):
        x = -jnp.sum(a_ref[...] * t_col, axis=0, keepdims=True)
        t_row = jnp.sum(jnp.where(lane_n == sub_n, t_col, 0.0), axis=0, keepdims=True)
        return x, jnp.sum(x * t_row, axis=1, keepdims=True)

    def coarse_field(x):
        def value(dz, dy):
            at = me + dz * ngy + dy
            return jnp.sum(jnp.where(lane_n[:1] == at, x, 0.0), axis=1, keepdims=True)

        def along_y(dz):
            return own_y * value(dz, 0) + half_ylo * value(dz, -1) + half_yhi * value(dz, 1)

        return own_z * along_y(0) + half_zlo * along_y(-1) + half_zhi * along_y(1)

    for i in (7, 8, 9):
        loads[i].wait()
    local = local_solve() * inv_m
    part_ref[...] = fold_in(local)
    halo_send(1, 1)
    rz_part = total(res_ref[0:ROWS] * local)
    gather_wait(0)
    invert(gathered(0, 0))
    x, rz_coarse = coarse(gathered(0, 1))
    field = coarse_field(x)
    halo_wait(1, 1)
    search_ref[...] = part_ref[...]
    add_rim(1, search_ref, 0, 0, 0)
    search = search_ref[...] + field
    search_ref[...] = search

    applied = helm(search)
    gather_send(1, rz_part, total(search * applied))
    part_ref[...] = fold_in(applied)
    halo_send(2, 2)
    app_ref[0:ROWS] = part_ref[...]
    halo_wait(2, 2)
    add_rim(2, app_ref, 0, 0, 0)
    outer_halo(2, app_ref)
    gather_wait(1)
    sums = jnp.sum(gbuf[1], axis=0)
    rz_now = sums[0:1, 0:1] + rz_coarse
    step_len = rz_now / sums[1:2, 0:1]
    pressure = step_len * search
    res_ref[...] = res_ref[...] - step_len * app_ref[...]
    gather_send(2, total(res_ref[0:ROWS] * invm_ref[...]))

    local = local_solve() * invm_ref[...]
    part_ref[...] = fold_in(local)
    halo_send(3, 1)
    gather_send(3, total(res_ref[0:ROWS] * local))
    gather_wait(2)
    x, rz_coarse = coarse(gathered(2, 0))
    field = coarse_field(x)
    halo_wait(3, 1)
    add_rim(3, part_ref, 0, 0, 0)
    gather_wait(3)
    sums = jnp.sum(gbuf[3], axis=0)
    rz_next = sums[0:1, 0:1] + rz_coarse
    search = part_ref[...] + field + (rz_next / rz_now) * search_ref[...]

    applied = helm(search)
    gather_send(4, total(search * applied))
    gather_wait(4)
    sums = jnp.sum(gbuf[4], axis=0)
    pressure_out[...] = pressure + (rz_next / sums[0:1, 0:1]) * search

    for r, layers in enumerate((3, 1, 2, 1)):
        halo_drain(r, layers)
    for g in range(5):
        gather_bytes(g, gsend_sem.at[g])


def body(ngx, ngy, level_set, velocity, source, wick_solid):
    n = ngx * ngy
    npad = -(-n // 128) * 128
    consts = [jnp.asarray(t) for t in tables()]
    hbm = pl.BlockSpec(memory_space=pltpu.HBM)
    vmem = pl.BlockSpec(memory_space=pltpu.VMEM)
    shape = level_set.shape
    level_new, pressure = pl.pallas_call(
        functools.partial(kernel, ngx, ngy, gll_tables()[1]),
        out_shape=[jax.ShapeDtypeStruct((ROWS, 128), F32)] * 2,
        in_specs=[hbm] * (4 + len(consts)),
        out_specs=[vmem] * 2,
        scratch_shapes=[
            pltpu.VMEM((ROWS, 128), F32),
            pltpu.VMEM((ROWS, 128), F32),
            pltpu.VMEM((ROWS, 128), F32),
            pltpu.VMEM((ROWS, 128), F32),
            pltpu.VMEM((EXT, 128), F32),
            pltpu.VMEM((EXT, 128), F32),
            pltpu.VMEM((ROWS, 128), F32),
            pltpu.VMEM((n, npad), F32),
            pltpu.VMEM((4, 2, 96, 128), F32),
            pltpu.VMEM((4, 2, 96, 128), F32),
            pltpu.VMEM((4, 2, 24, 128), F32),
            pltpu.VMEM((4, 2, 24, 128), F32),
            pltpu.VMEM((4, 4, 8, 128), F32),
            pltpu.VMEM((4, 4, 8, 128), F32),
            pltpu.VMEM((5, n, 2, 128), F32),
            pltpu.VMEM((ROWS, 128), F32),
            pltpu.VMEM((3 * ROWS, 128), F32),
            pltpu.VMEM((ROWS, 128), F32),
            pltpu.VMEM((1, EY, EX), jnp.int32),
            *[pltpu.VMEM(t.shape, t.dtype) for t in consts],
            pltpu.SemaphoreType.DMA((4, 8)),
            pltpu.SemaphoreType.DMA((4, 8)),
            pltpu.SemaphoreType.DMA((5,)),
            pltpu.SemaphoreType.DMA((5,)),
            pltpu.SemaphoreType.DMA((10,)),
        ],
        compiler_params=pltpu.CompilerParams(
            collective_id=0, has_side_effects=True, vmem_limit_bytes=63 * 1024 * 1024
        ),
    )(
        level_set.reshape(ROWS, 128),
        velocity.reshape(3 * ROWS, 128),
        source.reshape(ROWS, 128),
        wick_solid,
        *consts,
    )
    return level_new.reshape(shape), pressure.reshape(shape)


def solution(mesh):
    placed = (
        P("gx", "gy", None),
        P(None, "gx", "gy", None),
        P("gx", "gy", None),
        P("gx", "gy", None),
    )
    return jax.shard_map(
        functools.partial(body, mesh.shape["gx"], mesh.shape["gy"]),
        mesh=mesh,
        in_specs=placed,
        out_specs=(P("gx", "gy", None), P("gx", "gy", None)),
        check_vma=False,
    )
```

```python
import functools

import jax
import jax.numpy as jnp
import ml_dtypes
import numpy as np
from jax import lax
from jax.experimental import pallas as pl
from jax.experimental.pallas import tpu as pltpu
from jax.sharding import PartitionSpec as P

EZ = 1
EY = 4
EX = 16
ROWS = 256
EXT = 384
SPEC = 400

TIME_STEP = 0.02
HELM_COEF = 0.25
LEVEL_WIDTH = 0.25
GAS_RATIO = 10.0
SOLID_FACTOR = 0.25
SCHWARZ_SCALE = 0.5
SCHWARZ_SHIFT = 0.05

MESH = pl.DeviceIdType.MESH
LOGICAL = pl.DeviceIdType.LOGICAL
F32 = jnp.float32
BF16 = jnp.bfloat16

SIDES = ((-1, 0), (1, 0), (0, -1), (0, 1), (-1, -1), (-1, 1), (1, -1), (1, 1))
OPPOSITE = tuple(SIDES.index((-dz, -dy)) for dz, dy in SIDES)


def gll_tables():
    nodes = np.array(
        [
            -1.0,
            -0.8717401485096066,
            -0.5917001814331423,
            -0.2092992179024789,
            0.2092992179024789,
            0.5917001814331423,
            0.8717401485096066,
            1.0,
        ]
    )
    weight = np.array(
        [
            1.0 / 28.0,
            0.21070422714350603,
            0.3411226924835044,
            0.4124587946587038,
            0.4124587946587038,
            0.3411226924835044,
            0.21070422714350603,
            1.0 / 28.0,
        ]
    )
    bary = np.array(
        [1.0 / np.prod([nodes[i] - nodes[j] for j in range(8) if j != i]) for i in range(8)]
    )
    deriv = np.zeros((8, 8))
    for i in range(8):
        for j in range(8):
            if i != j:
                deriv[i, j] = bary[j] / bary[i] / (nodes[i] - nodes[j])
        deriv[i, i] = -np.sum(deriv[i])
    return weight, deriv


def halves(table):
    table = np.asarray(table, np.float32)
    high = table.astype(ml_dtypes.bfloat16)
    low = (table - high.astype(np.float32)).astype(ml_dtypes.bfloat16)
    return high, low


def tables():
    weight, deriv = gll_tables()
    ids = np.arange(10) + 1.0
    sine = np.sqrt(2.0 / 11.0) * np.sin(np.pi * np.outer(ids, ids) / 11.0)
    eig = 2.0 - 2.0 * np.cos(np.pi * ids / 11.0)
    dy = np.kron(np.eye(32), deriv)
    dx_t = np.kron(np.eye(EX), deriv.T)
    dx = np.kron(np.eye(EX), deriv)

    def ext_row(z, y):
        zlo, zhi, ylo, yhi = z < 0, z > 7, y < 0, y > 31
        if zlo or zhi:
            if ylo or yhi:
                return 336 + 2 * int(zhi) + int(yhi)
            return 256 + 32 * int(zhi) + y
        if ylo or yhi:
            return 320 + 8 * int(yhi) + z
        return 32 * z + y

    widen = np.zeros((SPEC, EXT))
    for zi in range(10):
        z = zi - 1
        for e in range(EY):
            for yi in range(10):
                y = 8 * e - 2 if yi == 0 else (8 * e + 9 if yi == 9 else 8 * e + yi - 1)
                widen[zi * 40 + e * 10 + yi, ext_row(z, y)] = 1.0
    spec_zy = np.kron(sine, np.kron(np.eye(EY), sine)) @ widen
    widen_x = np.zeros((160, 128))
    for e in range(EX):
        for xi in range(10):
            x = 8 * e - 2 if xi == 0 else (8 * e + 9 if xi == 9 else 8 * e + xi - 1)
            if 0 <= x < 128:
                widen_x[e * 10 + xi, x] = 1.0
    spec_x = np.zeros((128, 256))
    spec_x[:, :160] = (np.kron(np.eye(EX), sine) @ widen_x).T
    back_zy = np.kron(sine[1:9], np.kron(np.eye(EY), sine[1:9]))
    back_x = np.zeros((256, 128))
    back_x[:160] = np.kron(np.eye(EX), sine[1:9]).T
    lam_zy = (eig[:, None] + np.tile(eig, EY)[None, :]).reshape(SPEC)
    inv_den = np.zeros((SPEC, 256))
    inv_den[:, :160] = 1.0 / (
        SCHWARZ_SCALE * (lam_zy[:, None] + np.tile(eig, EX)[None, :]) + SCHWARZ_SHIFT
    )
    mass = 0.125 * (
        np.kron(weight, np.tile(weight, EY))[:, None] * np.tile(weight, EX)[None, :]
    )
    spread = np.zeros((16, 128))
    spread[:EX] = np.kron(np.eye(EX), np.ones((1, 8)))

    def stack(*parts):
        return np.concatenate([half for part in parts for half in halves(part)], axis=0)

    return (
        stack(dy, dy.T, spec_x),
        stack(dx_t, dx, back_x),
        np.concatenate([mass, spread], axis=0).astype(np.float32),
        stack(spec_zy),
        inv_den.astype(np.float32),
        stack(back_zy),
    )


def split(v):
    high = v.astype(BF16)
    low = (v - high.astype(F32)).astype(BF16)
    return high, low


def dot(a, b):
    return jnp.dot(a, b, preferred_element_type=F32)


def left(ref, base, rows, v):
    vh, vl = split(v)
    both = dot(ref[base : base + rows, :], jnp.concatenate([vh, vl], axis=1))
    return both[:, :128] + both[:, 128:] + dot(ref[base + rows : base + 2 * rows, :], vh)


def right(v, ref, base, rows):
    vh, vl = split(v)
    high = ref[base : base + rows, :]
    return dot(vh, high) + dot(vl, high) + dot(vh, ref[base + rows : base + 2 * rows, :])


def along_z(v, table):
    planes = [v[32 * i : 32 * i + 32] for i in range(8)]
    even = [planes[j] + planes[7 - j] for j in range(4)]
    odd = [planes[j] - planes[7 - j] for j in range(4)]
    low, high = [], []
    for i in range(4):
        a = b = None
        for j in range(4):
            p = float(table[i, j] + table[i, 7 - j]) / 2.0 * even[j]
            q = float(table[i, j] - table[i, 7 - j]) / 2.0 * odd[j]
            a, b = (p, q) if a is None else (a + p, b + q)
        low.append(a + b)
        high.insert(0, b - a)
    return jnp.concatenate(low + high, axis=0)


def total(v):
    return jnp.sum(jnp.sum(v, axis=0, keepdims=True), axis=1, keepdims=True)


def sweep_step(a, row, col, k, sub, lane):
    pivot = jnp.sum(jnp.where(lane[:1] == k, row, 0.0), axis=1, keepdims=True)
    row_m = jnp.where(lane[:1] == k, -1.0, row) / pivot
    col_m = jnp.where(sub == k, -1.0, col)
    return jnp.where(jnp.logical_or(lane == k, sub == k), 0.0, a) - col_m * row_m


def kernel(
    ngx, ngy, deriv,
    level_hbm, vel_hbm, source_hbm, solid_hbm, *refs
):
    tables_hbm, refs = refs[:6], refs[6:]
    level_out, pressure_out = refs[:2]
    (
        flux_ref, invm_ref, part_ref, lev_ref, app_ref, res_ref, search_ref, a_ref,
        zs, zr, ys, yr, cs, cr, gbuf0, gbuf1, gbuf2,
        level_ref, vel_ref, source_ref, solid_ref,
        t256, t128, mass_ref, spec_ref, den_ref, back_ref,
        send_sem, recv_sem, gsend_sem, grecv_sem, load_sem,
    ) = refs[2:]
    loads = [
        pltpu.make_async_copy(src, dst, load_sem.at[i])
        for i, (src, dst) in enumerate(
            zip(
                (level_hbm, vel_hbm, source_hbm, solid_hbm) + tables_hbm,
                (level_ref, vel_ref, source_ref, solid_ref)
                + (t256, t128, mass_ref, spec_ref, den_ref, back_ref),
            )
        )
    ]
    for i in (4, 5, 0, 1, 6, 2, 3, 7, 8, 9):
        loads[i].start()
    gbufs = (gbuf0, gbuf1, gbuf2)
    n = ngx * ngy
    ix = lax.axis_index("gx")
    iy = lax.axis_index("gy")
    me = ix * ngy + iy

    def other(i):
        at = me + i
        return jnp.where(at >= n, at - n, at)

    zr[...] = jnp.zeros_like(zr)
    yr[...] = jnp.zeros_like(yr)
    cr[...] = jnp.zeros_like(cr)

    barrier = pltpu.get_barrier_semaphore()

    def greet(i, carry):
        pl.semaphore_signal(barrier, inc=1, device_id=other(i), device_id_type=LOGICAL)
        return carry

    lax.fori_loop(1, n, greet, 0, unroll=n <= 64)

    has_zlo, has_zhi = ix > 0, ix < ngx - 1
    has_ylo, has_yhi = iy > 0, iy < ngy - 1

    def exists(d):
        dz, dy = SIDES[d]
        conds = []
        if dz:
            conds.append(has_zlo if dz < 0 else has_zhi)
        if dy:
            conds.append(has_ylo if dy < 0 else has_yhi)
        return conds[0] if len(conds) == 1 else jnp.logical_and(*conds)

    def buffers(r, d, layers):
        if d < 2:
            return zs.at[r, d, pl.ds(0, 32 * layers)], zr.at[r, OPPOSITE[d], pl.ds(0, 32 * layers)]
        if d < 4:
            return (
                ys.at[r, d - 2, pl.ds(0, 8 * layers)],
                yr.at[r, OPPOSITE[d] - 2, pl.ds(0, 8 * layers)],
            )
        return cs.at[r, d - 4], cr.at[r, OPPOSITE[d] - 4]

    def halo_copy(r, d, layers):
        src, dst = buffers(r, d, layers)
        dz, dy = SIDES[d]
        return pltpu.make_async_remote_copy(
            src_ref=src,
            dst_ref=dst,
            send_sem=send_sem.at[r, d],
            recv_sem=recv_sem.at[r, OPPOSITE[d]],
            device_id=(ix + dz, iy + dy),
            device_id_type=MESH,
        )

    def halo_send(r, layers, second=None):
        for s in range(2):
            zo, zi = ((0, 32), (224, 192))[s]
            zs[r, s, 0:32] = part_ref[zo : zo + 32]
            yo, yi = ((0, 1), (31, 30))[s]
            ys[r, s, 0:8] = part_ref[pl.ds(yo, 8, stride=32), :]
            if layers > 1:
                zs[r, s, 32:64] = part_ref[zi : zi + 32]
                ys[r, s, 8:16] = part_ref[pl.ds(yi, 8, stride=32), :]
            if second is not None:
                zs[r, s, 64:96] = second[zo : zo + 32]
                ys[r, s, 16:24] = second[pl.ds(yo, 8, stride=32), :]
        for c in range(4):
            dz, dy = SIDES[4 + c]
            zo, zi = (0, 32) if dz < 0 else (224, 192)
            yo, yi = (0, 1) if dy < 0 else (31, 30)
            cs[r, c, 0:1] = part_ref[zo + yo : zo + yo + 1]
            if layers > 1:
                cs[r, c, 1:2] = part_ref[zo + yi : zo + yi + 1]
                cs[r, c, 2:3] = part_ref[zi + yo : zi + yo + 1]
                cs[r, c, 3:4] = part_ref[zi + yi : zi + yi + 1]
            if second is not None:
                cs[r, c, 4:5] = second[zo + yo : zo + yo + 1]
        for d in range(8):

            @pl.when(exists(d))
            def _():
                halo_copy(r, d, layers).start()

    def halo_wait(r, layers):
        for d in range(8):

            @pl.when(exists(d))
            def _():
                src, _ = buffers(r, d, layers)
                _, dst = buffers(r, OPPOSITE[d], layers)
                dz, dy = SIDES[d]
                pltpu.make_async_remote_copy(
                    src_ref=src,
                    dst_ref=dst,
                    send_sem=send_sem.at[r, d],
                    recv_sem=recv_sem.at[r, d],
                    device_id=(ix + dz, iy + dy),
                    device_id_type=MESH,
                ).wait_recv()

    def halo_drain(r, layers):
        for d in range(8):

            @pl.when(exists(d))
            def _():
                halo_copy(r, d, layers).wait_send()

    def add_rim(r, ref, zoff, yoff, crow):
        ref[0:32] = ref[0:32] + zr[r, 0, zoff : zoff + 32]
        ref[224:256] = ref[224:256] + zr[r, 1, zoff : zoff + 32]
        for s, yo in ((0, 0), (1, 31)):
            at = pl.ds(yo, 8, stride=32)
            ref[at, :] = ref[at, :] + yr[r, s, yoff : yoff + 8]
        for c, row in enumerate((0, 31, 224, 255)):
            ref[row : row + 1] = ref[row : row + 1] + cr[r, c, crow : crow + 1]

    def outer_halo(r, ref):
        for s in range(2):
            base = 256 + 32 * s
            ref[base : base + 32] = zr[r, s, 32:64]
            ref[base : base + 1] = ref[base : base + 1] + cr[r, 2 * s, 2:3]
            ref[base + 31 : base + 32] = ref[base + 31 : base + 32] + cr[r, 2 * s + 1, 2:3]
            base = 320 + 8 * s
            ref[base : base + 8] = yr[r, s, 8:16]
            ref[base : base + 1] = ref[base : base + 1] + cr[r, s, 1:2]
            ref[base + 7 : base + 8] = ref[base + 7 : base + 8] + cr[r, 2 + s, 1:2]
        ref[336:384] = jnp.zeros((48, 128), F32)
        for c in range(4):
            ref[336 + c : 337 + c] = cr[r, c, 3:4]

    def gather_copy(g, dst):
        ref = gbufs[g].at[me]
        return pltpu.make_async_remote_copy(
            src_ref=ref,
            dst_ref=ref,
            send_sem=gsend_sem.at[g],
            recv_sem=grecv_sem.at[g],
            device_id=dst,
            device_id_type=LOGICAL,
        )

    def gather_send(g, rows):
        for k, value in enumerate(rows):
            gbufs[g][me, k : k + 1] = jnp.broadcast_to(value, (1, 128))

        def send(i, carry):
            gather_copy(g, other(i)).start()
            return carry

        lax.fori_loop(1, n, send, 0, unroll=n <= 64)

    def gather_bytes(g, sem):
        ref = gbufs[g].at[pl.ds(0, n - 1)]
        pltpu.make_async_copy(ref, ref, sem).wait()

    def gather_wait(g):
        gather_bytes(g, grecv_sem.at[g])

    row = lax.broadcasted_iota(jnp.int32, (ROWS, 128), 0)
    lane = lax.broadcasted_iota(jnp.int32, (ROWS, 128), 1)
    zpos, ypos = row // 32, row % 32
    y8, x8 = row % 8, lane % 8
    y_first = jnp.logical_and(y8 == 0, ypos > 0).astype(F32)
    y_last = jnp.logical_and(y8 == 7, ypos < 31).astype(F32)
    x_first = jnp.logical_and(x8 == 0, lane > 0).astype(F32)
    x_last = jnp.logical_and(x8 == 7, lane < 127).astype(F32)

    def flag(c):
        return c.astype(jnp.int32).astype(F32)

    zlo_f, zhi_f, ylo_f, yhi_f = flag(has_zlo), flag(has_zhi), flag(has_ylo), flag(has_yhi)
    z0, z7 = (zpos == 0).astype(F32), (zpos == 7).astype(F32)
    yb0, yb31 = (ypos == 0).astype(F32), (ypos == 31).astype(F32)
    half_zlo, half_zhi = 0.5 * zlo_f * z0, 0.5 * zhi_f * z7
    half_ylo, half_yhi = 0.5 * ylo_f * yb0, 0.5 * yhi_f * yb31
    own_z, own_y = 1.0 - half_zlo - half_zhi, 1.0 - half_ylo - half_yhi
    inv_m = (
        own_z
        * (own_y - 0.5 * (y_first + y_last))
        * (1.0 - 0.5 * (x_first + x_last))
    )
    invm_ref[...] = inv_m

    def fold_in(v):
        v = v + x_first * pltpu.roll(v, 1, 1) + x_last * pltpu.roll(v, 127, 1)
        return v + y_first * pltpu.roll(v, 1, 0) + y_last * pltpu.roll(v, ROWS - 1, 0)

    for i in (4, 5, 0, 1, 6):
        loads[i].wait()
    mass = mass_ref[0:ROWS]
    level = level_ref[...]
    advect = (
        vel_ref[0:ROWS] * along_z(level, deriv)
        + vel_ref[ROWS : 2 * ROWS] * left(t256, 0, ROWS, level)
        + vel_ref[2 * ROWS : 3 * ROWS] * right(level, t128, 0, 128)
    )
    lev_ref[...] = fold_in(mass * (level - (2.0 * TIME_STEP) * advect))
    diverge = (
        along_z(vel_ref[0:ROWS], deriv)
        + left(t256, 0, ROWS, vel_ref[ROWS : 2 * ROWS])
        + right(vel_ref[2 * ROWS : 3 * ROWS], t128, 0, 128)
    )
    loads[2].wait()
    part_ref[...] = fold_in(mass * (source_ref[...] - (2.0 * TIME_STEP) * diverge))

    pl.semaphore_wait(barrier, n - 1)
    halo_send(0, 3, lev_ref)
    res_ref[0:ROWS] = part_ref[...]
    loads[3].wait()
    solid = dot(solid_ref[0].astype(F32), mass_ref[ROWS : ROWS + EX])
    solid = jnp.concatenate(
        [jnp.broadcast_to(solid[e : e + 1], (8, 128)) for e in range(EY)], axis=0
    )
    solid = jnp.concatenate([solid] * 8, axis=0)
    halo_wait(0, 3)
    add_rim(0, res_ref, 0, 0, 0)
    add_rim(0, lev_ref, 64, 16, 4)
    outer_halo(0, res_ref)
    level_new = lev_ref[...] * inv_m / mass
    level_out[...] = level_new
    coef = (GAS_RATIO - (GAS_RATIO - 1.0) * jax.nn.sigmoid(level_new / LEVEL_WIDTH)) * (
        1.0 - (1.0 - SOLID_FACTOR) * solid
    )
    flux_ref[...] = 4.0 * coef * mass
    gather_send(0, (total(coef) / (ROWS * 128.0), total(res_ref[0:ROWS] * inv_m)))

    def local_solve(ref):
        spectral = right(left(spec_ref, 0, SPEC, ref[...]), t256, 4 * ROWS, 128)
        spectral = spectral * den_ref[...]
        return left(back_ref, 0, ROWS, right(spectral, t128, 512, 256))

    def helm(v):
        flux = flux_ref[...]
        out = along_z(flux * along_z(v, deriv), deriv.T)
        out = out + left(t256, 2 * ROWS, ROWS, flux * left(t256, 0, ROWS, v))
        out = out + right(flux * right(v, t128, 0, 128), t128, 256, 128)
        return out + HELM_COEF * mass_ref[0:ROWS] * v

    npad = a_ref.shape[1]
    sub_n = lax.broadcasted_iota(jnp.int32, (n, npad), 0)
    lane_n = lax.broadcasted_iota(jnp.int32, (n, npad), 1)

    def gathered(g, item):
        got = gbufs[g][:, item, :]
        return got if npad == 128 else jnp.concatenate([got] * (npad // 128), axis=1)

    def invert(k_col):
        diag = lane_n == sub_n
        k_row = jnp.sum(jnp.where(diag, k_col, 0.0), axis=0, keepdims=True)
        gap = lane_n - sub_n
        same = lane_n // ngy == sub_n // ngy
        y_link = jnp.logical_and(jnp.logical_or(gap == 1, gap == -1), same)
        z_link = jnp.logical_or(gap == ngy, gap == -ngy)
        rate = jnp.where(z_link, float(EY * EX) / EZ, 0.0) + jnp.where(
            y_link, float(EZ * EX) / EY, 0.0
        )
        rate = jnp.where(lane_n < n, rate, 0.0)
        link = 2.0 * k_col * k_row / (k_col + k_row) * rate
        diagonal = HELM_COEF * EZ * EY * EX + jnp.sum(link, axis=1, keepdims=True)
        a = jnp.where(diag, diagonal, -link)
        if n <= 64 and n % 2 == 0:
            for k in range(0, n, 2):
                c1 = jnp.broadcast_to(a[:, k : k + 1], (n, npad))
                c2 = jnp.broadcast_to(a[:, k + 1 : k + 2], (n, npad))
                p11, p12, p22 = c1[k : k + 1], c2[k : k + 1], c2[k + 1 : k + 2]
                scale = 1.0 / (p11 * p22 - p12 * p12)
                at1, at2 = lane_n == k, lane_n == k + 1
                on1, on2 = sub_n == k, sub_n == k + 1
                r1 = jnp.where(at1[:1], -1.0, jnp.where(at2[:1], 0.0, a[k : k + 1]))
                r2 = jnp.where(at2[:1], -1.0, jnp.where(at1[:1], 0.0, a[k + 1 : k + 2]))
                q1 = (p22 * r1 - p12 * r2) * scale
                q2 = (p11 * r2 - p12 * r1) * scale
                c1 = jnp.where(on1, -1.0, jnp.where(on2, 0.0, c1))
                c2 = jnp.where(on2, -1.0, jnp.where(on1, 0.0, c2))
                cross = jnp.logical_or(jnp.logical_or(at1, at2), jnp.logical_or(on1, on2))
                a = jnp.where(cross, 0.0, a) - c1 * q1 - c2 * q2
            a_ref[...] = a
        else:
            a_ref[...] = a

            def step(k, carry):
                a = a_ref[...]
                row = a_ref[pl.ds(k, 1), :]
                col = jnp.sum(jnp.where(lane_n == k, a, 0.0), axis=1, keepdims=True)
                a_ref[...] = sweep_step(a, row, col, k, sub_n, lane_n)
                return carry

            lax.fori_loop(0, n, step, 0)

    def coarse(t_col):
        return -jnp.sum(a_ref[...] * t_col, axis=0, keepdims=True)

    def coarse_field(x):
        def value(dz, dy):
            at = me + dz * ngy + dy
            return jnp.sum(jnp.where(lane_n[:1] == at, x, 0.0), axis=1, keepdims=True)

        def along_y(dz):
            return own_y * value(dz, 0) + half_ylo * value(dz, -1) + half_yhi * value(dz, 1)

        return own_z * along_y(0) + half_zlo * along_y(-1) + half_zhi * along_y(1)

    def rows_sum(v):
        return jnp.sum(v, axis=0, keepdims=True)

    for i in (7, 8, 9):
        loads[i].wait()
    part_ref[...] = fold_in(local_solve(res_ref) * inv_m)
    halo_send(1, 1)
    gather_wait(0)
    invert(gathered(0, 0))
    field = coarse_field(coarse(gathered(0, 1)))
    halo_wait(1, 1)
    search_ref[...] = part_ref[...]
    add_rim(1, search_ref, 0, 0, 0)
    z1 = search_ref[...] + field
    search_ref[...] = z1

    applied = helm(z1)
    part_ref[...] = fold_in(applied)
    halo_send(2, 2)
    sum_rz = rows_sum(res_ref[0:ROWS] * z1 * inv_m)
    sum_za = rows_sum(z1 * applied)
    app_ref[0:ROWS] = part_ref[...]
    halo_wait(2, 2)
    add_rim(2, app_ref, 0, 0, 0)
    outer_halo(2, app_ref)
    gather_send(1, (total(app_ref[0:ROWS] * invm_ref[...]),))

    part_ref[...] = fold_in(local_solve(app_ref) * invm_ref[...])
    halo_send(3, 1)
    gather_wait(1)
    field = coarse_field(coarse(gathered(1, 0)))
    halo_wait(3, 1)
    add_rim(3, part_ref, 0, 0, 0)
    q = part_ref[...] + field

    q_m = q * invm_ref[...]
    gz, gy, gx = along_z(q, deriv), left(t256, 0, ROWS, q), right(q, t128, 0, 128)
    energy = flux_ref[...] * (gz * gz + gy * gy + gx * gx)
    energy = energy + HELM_COEF * mass_ref[0:ROWS] * (q * q)
    sum_rq = rows_sum(res_ref[0:ROWS] * q_m)
    sum_aq = rows_sum(app_ref[0:ROWS] * q_m)
    gather_send(2, (sum_rz, sum_za, sum_rq, sum_aq, rows_sum(energy), 0.0, 0.0, 0.0))
    gather_wait(2)
    sums = jnp.sum(jnp.sum(gbuf2[...], axis=0), axis=1, keepdims=True)
    rz, za, rq, aq, qq = (sums[k : k + 1] for k in range(5))

    step1 = rz / za
    rz_next = step1 * (step1 * aq - rq)
    beta1 = 1.0 + rz_next / rz
    norm2 = beta1 * beta1 * za - 2.0 * beta1 * step1 * aq + step1 * step1 * qq
    step2 = rz_next / norm2
    pressure_out[...] = (step1 + step2 * beta1) * search_ref[...] - (step2 * step1) * q

    for r, layers in enumerate((3, 1, 2, 1)):
        halo_drain(r, layers)
    for g in range(3):
        gather_bytes(g, gsend_sem.at[g])


def body(ngx, ngy, level_set, velocity, source, wick_solid):
    n = ngx * ngy
    npad = -(-n // 128) * 128
    consts = [jnp.asarray(t) for t in tables()]
    hbm = pl.BlockSpec(memory_space=pltpu.HBM)
    vmem = pl.BlockSpec(memory_space=pltpu.VMEM)
    shape = level_set.shape
    level_new, pressure = pl.pallas_call(
        functools.partial(kernel, ngx, ngy, gll_tables()[1]),
        out_shape=[jax.ShapeDtypeStruct((ROWS, 128), F32)] * 2,
        in_specs=[hbm] * (4 + len(consts)),
        out_specs=[vmem] * 2,
        scratch_shapes=[
            pltpu.VMEM((ROWS, 128), F32),
            pltpu.VMEM((ROWS, 128), F32),
            pltpu.VMEM((ROWS, 128), F32),
            pltpu.VMEM((ROWS, 128), F32),
            pltpu.VMEM((EXT, 128), F32),
            pltpu.VMEM((EXT, 128), F32),
            pltpu.VMEM((ROWS, 128), F32),
            pltpu.VMEM((n, npad), F32),
            pltpu.VMEM((4, 2, 96, 128), F32),
            pltpu.VMEM((4, 2, 96, 128), F32),
            pltpu.VMEM((4, 2, 24, 128), F32),
            pltpu.VMEM((4, 2, 24, 128), F32),
            pltpu.VMEM((4, 4, 8, 128), F32),
            pltpu.VMEM((4, 4, 8, 128), F32),
            pltpu.VMEM((n, 2, 128), F32),
            pltpu.VMEM((n, 1, 128), F32),
            pltpu.VMEM((n, 8, 128), F32),
            pltpu.VMEM((ROWS, 128), F32),
            pltpu.VMEM((3 * ROWS, 128), F32),
            pltpu.VMEM((ROWS, 128), F32),
            pltpu.VMEM((1, EY, EX), jnp.int32),
            *[pltpu.VMEM(t.shape, t.dtype) for t in consts],
            pltpu.SemaphoreType.DMA((4, 8)),
            pltpu.SemaphoreType.DMA((4, 8)),
            pltpu.SemaphoreType.DMA((3,)),
            pltpu.SemaphoreType.DMA((3,)),
            pltpu.SemaphoreType.DMA((10,)),
        ],
        compiler_params=pltpu.CompilerParams(
            collective_id=0, has_side_effects=True, vmem_limit_bytes=63 * 1024 * 1024
        ),
    )(
        level_set.reshape(ROWS, 128),
        velocity.reshape(3 * ROWS, 128),
        source.reshape(ROWS, 128),
        wick_solid,
        *consts,
    )
    return level_new.reshape(shape), pressure.reshape(shape)


def solution(mesh):
    placed = (
        P("gx", "gy", None),
        P(None, "gx", "gy", None),
        P("gx", "gy", None),
        P("gx", "gy", None),
    )
    return jax.shard_map(
        functools.partial(body, mesh.shape["gx"], mesh.shape["gy"]),
        mesh=mesh,
        in_specs=placed,
        out_specs=(P("gx", "gy", None), P("gx", "gy", None)),
        check_vma=False,
    )
```

```python
import functools

import jax
import jax.numpy as jnp
import ml_dtypes
import numpy as np
from jax import lax
from jax.experimental import pallas as pl
from jax.experimental.pallas import tpu as pltpu
from jax.sharding import PartitionSpec as P

EZ = 1
EY = 4
EX = 16
ROWS = 256
PLANE = 40
SPEC = 400
T_DY, T_DYT, T_DXT, T_DX, T_SX, T_BX = 0, 128, 256, 512, 768, 1152
T_SY, T_BY, T_END = 1408, 1824, 2144

TIME_STEP = 0.02
HELM_COEF = 0.25
LEVEL_WIDTH = 0.25
GAS_RATIO = 10.0
SOLID_FACTOR = 0.25
SCHWARZ_SCALE = 0.5
SCHWARZ_SHIFT = 0.05

MESH = pl.DeviceIdType.MESH
LOGICAL = pl.DeviceIdType.LOGICAL
F32 = jnp.float32
BF16 = jnp.bfloat16

SIDES = ((-1, 0), (1, 0), (0, -1), (0, 1), (-1, -1), (-1, 1), (1, -1), (1, 1))
OPPOSITE = tuple(SIDES.index((-dz, -dy)) for dz, dy in SIDES)


def gll_tables():
    nodes = np.array(
        [
            -1.0,
            -0.8717401485096066,
            -0.5917001814331423,
            -0.2092992179024789,
            0.2092992179024789,
            0.5917001814331423,
            0.8717401485096066,
            1.0,
        ]
    )
    weight = np.array(
        [
            1.0 / 28.0,
            0.21070422714350603,
            0.3411226924835044,
            0.4124587946587038,
            0.4124587946587038,
            0.3411226924835044,
            0.21070422714350603,
            1.0 / 28.0,
        ]
    )
    bary = np.array(
        [1.0 / np.prod([nodes[i] - nodes[j] for j in range(8) if j != i]) for i in range(8)]
    )
    deriv = np.zeros((8, 8))
    for i in range(8):
        for j in range(8):
            if i != j:
                deriv[i, j] = bary[j] / bary[i] / (nodes[i] - nodes[j])
        deriv[i, i] = -np.sum(deriv[i])
    return weight, deriv


def halves(table):
    table = np.asarray(table, np.float32)
    high = table.astype(ml_dtypes.bfloat16)
    low = (table - high.astype(np.float32)).astype(ml_dtypes.bfloat16)
    return high, low


def tables():
    weight, deriv = gll_tables()
    ids = np.arange(10) + 1.0
    sine = sine_table()
    eig = 2.0 - 2.0 * np.cos(np.pi * ids / 11.0)
    dy = np.kron(np.eye(16), deriv)
    dx_t = np.kron(np.eye(EX), deriv.T)
    dx = np.kron(np.eye(EX), deriv)

    widen_y = np.zeros((PLANE, PLANE))
    for e in range(EY):
        for yi in range(10):
            y = 8 * e - 2 if yi == 0 else (8 * e + 9 if yi == 9 else 8 * e + yi - 1)
            widen_y[e * 10 + yi, 32 if y < 0 else (33 if y > 31 else y)] = 1.0
    spec_y = np.kron(np.eye(5), np.kron(np.eye(EY), sine) @ widen_y)
    widen_x = np.zeros((160, 128))
    for e in range(EX):
        for xi in range(10):
            x = 8 * e - 2 if xi == 0 else (8 * e + 9 if xi == 9 else 8 * e + xi - 1)
            if 0 <= x < 128:
                widen_x[e * 10 + xi, x] = 1.0
    spec_x = np.zeros((128, 256))
    spec_x[:, :160] = (np.kron(np.eye(EX), sine) @ widen_x).T
    back_y = np.kron(np.eye(5), np.kron(np.eye(EY), sine[1:9]))
    back_x = np.zeros((256, 128))
    back_x[:160] = np.kron(np.eye(EX), sine[1:9]).T
    lam_zy = (eig[:, None] + np.tile(eig, EY)[None, :]).reshape(SPEC)
    inv_den = np.zeros((SPEC, 256))
    inv_den[:, :160] = 1.0 / (
        SCHWARZ_SCALE * (lam_zy[:, None] + np.tile(eig, EX)[None, :]) + SCHWARZ_SHIFT
    )
    mass = 0.125 * (
        np.kron(weight, np.tile(weight, EY))[:, None] * np.tile(weight, EX)[None, :]
    )
    spread = np.zeros((16, 128))
    spread[:EX] = np.kron(np.eye(EX), np.ones((1, 8)))

    def beside(table):
        high, low = halves(table)
        return np.concatenate([high, low], axis=1)

    def both(table):
        high, low = halves(table)
        zero = np.zeros_like(low)
        return np.concatenate(
            [np.concatenate([high, low], axis=1), np.concatenate([high, zero], axis=1)], axis=0
        )

    def under(table):
        high, low = halves(table)
        return np.concatenate([high, high, low], axis=0)

    def padded(table, rows, cols):
        out = np.zeros((rows, cols))
        out[: table.shape[0], : table.shape[1]] = table
        return out

    return (
        np.concatenate(
            [
                beside(dy), beside(dy.T), both(dx_t), both(dx), under(spec_x), beside(back_x),
                *halves(padded(spec_y, 208, 256)), *halves(padded(back_y, 160, 256)),
            ],
            axis=0,
        ),
        np.concatenate([mass, spread], axis=0).astype(np.float32),
        inv_den.astype(np.float32),
    )


def sine_table():
    ids = np.arange(10) + 1.0
    return np.sqrt(2.0 / 11.0) * np.sin(np.pi * np.outer(ids, ids) / 11.0)


def split(v):
    high = v.astype(BF16)
    low = (v - high.astype(F32)).astype(BF16)
    return high, low


def dot(a, b):
    return jnp.dot(a, b, preferred_element_type=F32)


def along_y(v, ref, base):
    vh, vl = split(jnp.concatenate([v[:128], v[128:]], axis=1))
    table = ref[base : base + 128, :]
    out = dot(table, jnp.concatenate([vh, vh], axis=0)) + dot(table[:, :128], vl)
    return jnp.concatenate([out[:, :128], out[:, 128:]], axis=0)


def along_x(v, ref, base):
    vh, vl = split(v)
    out = dot(jnp.concatenate([vh, vl], axis=1), ref[base : base + 256, :])
    return out[:, :128] + out[:, 128:]


def planes_y(v, ref, base, rows, pad):
    vh, vl = split(jnp.concatenate([v[:200], v[200:]], axis=1))
    high = ref[base : base + pad, :200]
    low = ref[base + pad : base + 2 * pad, :200]
    out = dot(high, vh) + dot(high, vl) + dot(low, vh)
    return jnp.concatenate([out[:rows, :128], out[:rows, 128:]], axis=0)


def sine_z(planes, sine, keep):
    even = [planes[k] + planes[9 - k] for k in range(5)]
    odd = [planes[k] - planes[9 - k] for k in range(5)]
    out = []
    for j in keep:
        terms = [float(sine[j, k]) * (odd if j % 2 else even)[k] for k in range(5)]
        out.append(functools.reduce(lambda a, b: a + b, terms))
    return out


def along_z(v, table):
    planes = [v[32 * i : 32 * i + 32] for i in range(8)]
    even = [planes[j] + planes[7 - j] for j in range(4)]
    odd = [planes[j] - planes[7 - j] for j in range(4)]
    low, high = [], []
    for i in range(4):
        a = b = None
        for j in range(4):
            p = float(table[i, j] + table[i, 7 - j]) / 2.0 * even[j]
            q = float(table[i, j] - table[i, 7 - j]) / 2.0 * odd[j]
            a, b = (p, q) if a is None else (a + p, b + q)
        low.append(a + b)
        high.insert(0, b - a)
    return jnp.concatenate(low + high, axis=0)


def total(v):
    return jnp.sum(jnp.sum(v, axis=0, keepdims=True), axis=1, keepdims=True)


def sweep_step(a, row, col, k, sub, lane):
    pivot = jnp.sum(jnp.where(lane[:1] == k, row, 0.0), axis=1, keepdims=True)
    row_m = jnp.where(lane[:1] == k, -1.0, row) / pivot
    col_m = jnp.where(sub == k, -1.0, col)
    return jnp.where(jnp.logical_or(lane == k, sub == k), 0.0, a) - col_m * row_m


def kernel(
    ngx, ngy, deriv, sine,
    level_hbm, vel_hbm, source_hbm, solid_hbm, *refs
):
    tables_hbm, refs = refs[:3], refs[3:]
    level_out, pressure_out = refs[:2]
    (
        flux_ref, invm_ref, part_ref, lev_ref, app_ref, res_ref, search_ref, ext_ref, a_ref,
        zs, zr, ys, yr, cs, cr, gbuf0, gbuf1, gbuf2,
        level_ref, vel_ref, source_ref, solid_ref,
        table, mass_ref, den_ref,
        send_sem, recv_sem, gsend_sem, grecv_sem, load_sem,
    ) = refs[2:]
    loads = [
        pltpu.make_async_copy(src, dst, load_sem.at[i])
        for i, (src, dst) in enumerate(
            zip(
                (level_hbm, vel_hbm, source_hbm, solid_hbm) + tables_hbm,
                (level_ref, vel_ref, source_ref, solid_ref)
                + (table, mass_ref, den_ref),
            )
        )
    ]
    for i in (4, 0, 1, 5, 2, 3, 6):
        loads[i].start()
    gbufs = (gbuf0, gbuf1, gbuf2)
    n = ngx * ngy
    ix = lax.axis_index("gx")
    iy = lax.axis_index("gy")
    me = ix * ngy + iy

    def other(i):
        at = me + i
        return jnp.where(at >= n, at - n, at)

    zr[...] = jnp.zeros_like(zr)
    yr[...] = jnp.zeros_like(yr)
    cr[...] = jnp.zeros_like(cr)
    ext_ref[...] = jnp.zeros_like(ext_ref)

    barrier = pltpu.get_barrier_semaphore()

    def greet(i, carry):
        pl.semaphore_signal(barrier, inc=1, device_id=other(i), device_id_type=LOGICAL)
        return carry

    lax.fori_loop(1, n, greet, 0, unroll=n <= 64)

    has_zlo, has_zhi = ix > 0, ix < ngx - 1
    has_ylo, has_yhi = iy > 0, iy < ngy - 1

    def exists(d):
        dz, dy = SIDES[d]
        conds = []
        if dz:
            conds.append(has_zlo if dz < 0 else has_zhi)
        if dy:
            conds.append(has_ylo if dy < 0 else has_yhi)
        return conds[0] if len(conds) == 1 else jnp.logical_and(*conds)

    def buffers(r, d, layers):
        if d < 2:
            return zs.at[r, d, pl.ds(0, 32 * layers)], zr.at[r, OPPOSITE[d], pl.ds(0, 32 * layers)]
        if d < 4:
            return (
                ys.at[r, d - 2, pl.ds(0, 8 * layers)],
                yr.at[r, OPPOSITE[d] - 2, pl.ds(0, 8 * layers)],
            )
        return cs.at[r, d - 4], cr.at[r, OPPOSITE[d] - 4]

    def halo_copy(r, d, layers):
        src, dst = buffers(r, d, layers)
        dz, dy = SIDES[d]
        return pltpu.make_async_remote_copy(
            src_ref=src,
            dst_ref=dst,
            send_sem=send_sem.at[r, d],
            recv_sem=recv_sem.at[r, OPPOSITE[d]],
            device_id=(ix + dz, iy + dy),
            device_id_type=MESH,
        )

    def halo_send(r, layers, second=None):
        for s in range(2):
            zo, zi = ((0, 32), (224, 192))[s]
            zs[r, s, 0:32] = part_ref[zo : zo + 32]
            yo, yi = ((0, 1), (31, 30))[s]
            ys[r, s, 0:8] = part_ref[pl.ds(yo, 8, stride=32), :]
            if layers > 1:
                zs[r, s, 32:64] = part_ref[zi : zi + 32]
                ys[r, s, 8:16] = part_ref[pl.ds(yi, 8, stride=32), :]
            if second is not None:
                zs[r, s, 64:96] = second[zo : zo + 32]
                ys[r, s, 16:24] = second[pl.ds(yo, 8, stride=32), :]
        for c in range(4):
            dz, dy = SIDES[4 + c]
            zo, zi = (0, 32) if dz < 0 else (224, 192)
            yo, yi = (0, 1) if dy < 0 else (31, 30)
            cs[r, c, 0:1] = part_ref[zo + yo : zo + yo + 1]
            if layers > 1:
                cs[r, c, 1:2] = part_ref[zo + yi : zo + yi + 1]
                cs[r, c, 2:3] = part_ref[zi + yo : zi + yo + 1]
                cs[r, c, 3:4] = part_ref[zi + yi : zi + yi + 1]
            if second is not None:
                cs[r, c, 4:5] = second[zo + yo : zo + yo + 1]
        for d in range(8):

            @pl.when(exists(d))
            def _():
                halo_copy(r, d, layers).start()

    def halo_wait(r, layers):
        for d in range(8):

            @pl.when(exists(d))
            def _():
                src, _ = buffers(r, d, layers)
                _, dst = buffers(r, OPPOSITE[d], layers)
                dz, dy = SIDES[d]
                pltpu.make_async_remote_copy(
                    src_ref=src,
                    dst_ref=dst,
                    send_sem=send_sem.at[r, d],
                    recv_sem=recv_sem.at[r, d],
                    device_id=(ix + dz, iy + dy),
                    device_id_type=MESH,
                ).wait_recv()

    def halo_drain(r, layers):
        for d in range(8):

            @pl.when(exists(d))
            def _():
                halo_copy(r, d, layers).wait_send()

    def add_rim(r, ref, zoff, yoff, crow):
        ref[0:32] = ref[0:32] + zr[r, 0, zoff : zoff + 32]
        ref[224:256] = ref[224:256] + zr[r, 1, zoff : zoff + 32]
        for s, yo in ((0, 0), (1, 31)):
            at = pl.ds(yo, 8, stride=32)
            ref[at, :] = ref[at, :] + yr[r, s, yoff : yoff + 8]
        for c, row in enumerate((0, 31, 224, 255)):
            ref[row : row + 1] = ref[row : row + 1] + cr[r, c, crow : crow + 1]

    def outer_halo(r):
        for s in range(2):
            base = 9 * PLANE * s
            ext_ref[base : base + 32] = zr[r, s, 32:64]
            ext_ref[base : base + 1] = ext_ref[base : base + 1] + cr[r, 2 * s, 2:3]
            at = base + 31
            ext_ref[at : at + 1] = ext_ref[at : at + 1] + cr[r, 2 * s + 1, 2:3]
            ext_ref[pl.ds(PLANE + 32 + s, 8, stride=PLANE), :] = yr[r, s, 8:16]
            for at, c in ((PLANE + 32 + s, s), (8 * PLANE + 32 + s, 2 + s)):
                ext_ref[at : at + 1] = ext_ref[at : at + 1] + cr[r, c, 1:2]
        for c in range(4):
            at = 9 * PLANE * (c // 2) + 32 + c % 2
            ext_ref[at : at + 1] = cr[r, c, 3:4]

    def gather_copy(g, dst):
        ref = gbufs[g].at[me]
        return pltpu.make_async_remote_copy(
            src_ref=ref,
            dst_ref=ref,
            send_sem=gsend_sem.at[g],
            recv_sem=grecv_sem.at[g],
            device_id=dst,
            device_id_type=LOGICAL,
        )

    def gather_send(g, rows):
        for k, value in enumerate(rows):
            gbufs[g][me, k : k + 1] = jnp.broadcast_to(value, (1, 128))

        def send(i, carry):
            gather_copy(g, other(i)).start()
            return carry

        lax.fori_loop(1, n, send, 0, unroll=n <= 64)

    def gather_bytes(g, sem):
        ref = gbufs[g].at[pl.ds(0, n - 1)]
        pltpu.make_async_copy(ref, ref, sem).wait()

    def gather_wait(g):
        gather_bytes(g, grecv_sem.at[g])

    row = lax.broadcasted_iota(jnp.int32, (ROWS, 128), 0)
    lane = lax.broadcasted_iota(jnp.int32, (ROWS, 128), 1)
    zpos, ypos = row // 32, row % 32
    y8, x8 = row % 8, lane % 8
    y_first = jnp.logical_and(y8 == 0, ypos > 0).astype(F32)
    y_last = jnp.logical_and(y8 == 7, ypos < 31).astype(F32)
    x_first = jnp.logical_and(x8 == 0, lane > 0).astype(F32)
    x_last = jnp.logical_and(x8 == 7, lane < 127).astype(F32)

    def flag(c):
        return c.astype(jnp.int32).astype(F32)

    zlo_f, zhi_f, ylo_f, yhi_f = flag(has_zlo), flag(has_zhi), flag(has_ylo), flag(has_yhi)
    z0, z7 = (zpos == 0).astype(F32), (zpos == 7).astype(F32)
    yb0, yb31 = (ypos == 0).astype(F32), (ypos == 31).astype(F32)
    half_zlo, half_zhi = 0.5 * zlo_f * z0, 0.5 * zhi_f * z7
    half_ylo, half_yhi = 0.5 * ylo_f * yb0, 0.5 * yhi_f * yb31
    own_z, own_y = 1.0 - half_zlo - half_zhi, 1.0 - half_ylo - half_yhi
    inv_m = (
        own_z
        * (own_y - 0.5 * (y_first + y_last))
        * (1.0 - 0.5 * (x_first + x_last))
    )
    invm_ref[...] = inv_m

    def fold_in(v):
        v = v + x_first * pltpu.roll(v, 1, 1) + x_last * pltpu.roll(v, 127, 1)
        return v + y_first * pltpu.roll(v, 1, 0) + y_last * pltpu.roll(v, ROWS - 1, 0)

    for i in (4, 0, 1, 5):
        loads[i].wait()
    mass = mass_ref[0:ROWS]
    level = level_ref[...]
    advect = (
        vel_ref[0:ROWS] * along_z(level, deriv)
        + vel_ref[ROWS : 2 * ROWS] * along_y(level, table, T_DY)
        + vel_ref[2 * ROWS : 3 * ROWS] * along_x(level, table, T_DXT)
    )
    lev_ref[...] = fold_in(mass * (level - (2.0 * TIME_STEP) * advect))
    diverge = (
        along_z(vel_ref[0:ROWS], deriv)
        + along_y(vel_ref[ROWS : 2 * ROWS], table, T_DY)
        + along_x(vel_ref[2 * ROWS : 3 * ROWS], table, T_DXT)
    )
    loads[2].wait()
    part_ref[...] = fold_in(mass * (source_ref[...] - (2.0 * TIME_STEP) * diverge))

    pl.semaphore_wait(barrier, n - 1)
    halo_send(0, 3, lev_ref)
    res_ref[...] = part_ref[...]
    loads[3].wait()
    solid = dot(solid_ref[0].astype(F32), mass_ref[ROWS : ROWS + EX])
    solid = jnp.concatenate(
        [jnp.broadcast_to(solid[e : e + 1], (8, 128)) for e in range(EY)], axis=0
    )
    solid = jnp.concatenate([solid] * 8, axis=0)
    halo_wait(0, 3)
    add_rim(0, res_ref, 0, 0, 0)
    add_rim(0, lev_ref, 64, 16, 4)
    outer_halo(0)
    level_new = lev_ref[...] * inv_m / mass
    level_out[...] = level_new
    coef = (GAS_RATIO - (GAS_RATIO - 1.0) * jax.nn.sigmoid(level_new / LEVEL_WIDTH)) * (
        1.0 - (1.0 - SOLID_FACTOR) * solid
    )
    flux_ref[...] = 4.0 * coef * mass
    gather_send(0, (total(coef) / (ROWS * 128.0), total(res_ref[...] * inv_m)))

    def local_solve(v):
        for z in range(8):
            ext_ref[PLANE * (z + 1) : PLANE * (z + 1) + 32] = v[32 * z : 32 * z + 32]
        planes = [ext_ref[PLANE * z : PLANE * z + PLANE] for z in range(10)]
        wide = jnp.concatenate(sine_z(planes, sine, range(10)), axis=0)
        wide = planes_y(wide, table, T_SY, 200, 208)
        wh, wl = split(wide)
        spectral = dot(jnp.concatenate([wh, wl], axis=1), table[T_SX : T_SX + 256, :])
        spectral = spectral + dot(wh, table[T_SX + 256 : T_SX + 384, :])
        sh, sl = split(spectral * den_ref[...])
        back = dot(sh, table[T_BX : T_BX + 256, :])
        back = back[:, :128] + back[:, 128:] + dot(sl, table[T_BX : T_BX + 256, :128])
        back = planes_y(back, table, T_BY, 160, 160)
        planes = [back[32 * z : 32 * z + 32] for z in range(10)]
        return jnp.concatenate(sine_z(planes, sine, range(1, 9)), axis=0)

    def helm(v):
        flux = flux_ref[...]
        out = along_z(flux * along_z(v, deriv), deriv.T)
        out = out + along_y(flux * along_y(v, table, T_DY), table, T_DYT)
        out = out + along_x(flux * along_x(v, table, T_DXT), table, T_DX)
        return out + HELM_COEF * mass_ref[0:ROWS] * v

    npad = a_ref.shape[1]
    sub_n = lax.broadcasted_iota(jnp.int32, (n, npad), 0)
    lane_n = lax.broadcasted_iota(jnp.int32, (n, npad), 1)

    def gathered(g, item):
        got = gbufs[g][:, item, :]
        return got if npad == 128 else jnp.concatenate([got] * (npad // 128), axis=1)

    def invert(k_col):
        diag = lane_n == sub_n
        k_row = jnp.sum(jnp.where(diag, k_col, 0.0), axis=0, keepdims=True)
        gap = lane_n - sub_n
        same = lane_n // ngy == sub_n // ngy
        y_link = jnp.logical_and(jnp.logical_or(gap == 1, gap == -1), same)
        z_link = jnp.logical_or(gap == ngy, gap == -ngy)
        rate = jnp.where(z_link, float(EY * EX) / EZ, 0.0) + jnp.where(
            y_link, float(EZ * EX) / EY, 0.0
        )
        rate = jnp.where(lane_n < n, rate, 0.0)
        link = 2.0 * k_col * k_row / (k_col + k_row) * rate
        diagonal = HELM_COEF * EZ * EY * EX + jnp.sum(link, axis=1, keepdims=True)
        a = jnp.where(diag, diagonal, -link)
        if ngx == 2 and n <= 64:
            left_over = list(range(ngy))
            while left_over:
                now = left_over[1::2] or left_over
                left_over = left_over[0::2] if len(left_over) > 1 else []
                cross = jnp.zeros((n, npad), jnp.bool_)
                change = None
                for j in now:
                    k, m = j, ngy + j
                    c1 = jnp.broadcast_to(a[:, k : k + 1], (n, npad))
                    c2 = jnp.broadcast_to(a[:, m : m + 1], (n, npad))
                    p11, p12, p22 = c1[k : k + 1], c2[k : k + 1], c2[m : m + 1]
                    scale = 1.0 / (p11 * p22 - p12 * p12)
                    at1, at2 = lane_n == k, lane_n == m
                    on1, on2 = sub_n == k, sub_n == m
                    r1 = jnp.where(at1[:1], -1.0, jnp.where(at2[:1], 0.0, a[k : k + 1]))
                    r2 = jnp.where(at2[:1], -1.0, jnp.where(at1[:1], 0.0, a[m : m + 1]))
                    q1 = (p22 * r1 - p12 * r2) * scale
                    q2 = (p11 * r2 - p12 * r1) * scale
                    c1 = jnp.where(on1, -1.0, jnp.where(on2, 0.0, c1))
                    c2 = jnp.where(on2, -1.0, jnp.where(on1, 0.0, c2))
                    cross = cross | at1 | at2 | on1 | on2
                    term = c1 * q1 + c2 * q2
                    change = term if change is None else change + term
                a = jnp.where(cross, 0.0, a) - change
            a_ref[...] = a
        else:
            a_ref[...] = a

            def step(k, carry):
                a = a_ref[...]
                row = a_ref[pl.ds(k, 1), :]
                col = jnp.sum(jnp.where(lane_n == k, a, 0.0), axis=1, keepdims=True)
                a_ref[...] = sweep_step(a, row, col, k, sub_n, lane_n)
                return carry

            lax.fori_loop(0, n, step, 0)

    def coarse(t_col):
        return -jnp.sum(a_ref[...] * t_col, axis=0, keepdims=True)

    def coarse_field(x):
        def value(dz, dy):
            at = me + dz * ngy + dy
            return jnp.sum(jnp.where(lane_n[:1] == at, x, 0.0), axis=1, keepdims=True)

        def along_y(dz):
            return own_y * value(dz, 0) + half_ylo * value(dz, -1) + half_yhi * value(dz, 1)

        return own_z * along_y(0) + half_zlo * along_y(-1) + half_zhi * along_y(1)

    def rows_sum(v):
        return jnp.sum(v, axis=0, keepdims=True)

    loads[6].wait()
    part_ref[...] = fold_in(local_solve(res_ref[...]) * inv_m)
    halo_send(1, 1)
    gather_wait(0)
    invert(gathered(0, 0))
    field = coarse_field(coarse(gathered(0, 1)))
    halo_wait(1, 1)
    search_ref[...] = part_ref[...]
    add_rim(1, search_ref, 0, 0, 0)
    z1 = search_ref[...] + field
    search_ref[...] = z1

    applied = helm(z1)
    part_ref[...] = fold_in(applied)
    halo_send(2, 2)
    sum_rz = rows_sum(res_ref[...] * z1 * inv_m)
    sum_za = rows_sum(z1 * applied)
    app_ref[...] = part_ref[...]
    halo_wait(2, 2)
    add_rim(2, app_ref, 0, 0, 0)
    outer_halo(2)
    gather_send(1, (total(app_ref[...] * invm_ref[...]),))

    part_ref[...] = fold_in(local_solve(app_ref[...]) * invm_ref[...])
    halo_send(3, 1)
    gather_wait(1)
    field = coarse_field(coarse(gathered(1, 0)))
    halo_wait(3, 1)
    add_rim(3, part_ref, 0, 0, 0)
    q = part_ref[...] + field

    q_m = q * invm_ref[...]
    gz, gy, gx = along_z(q, deriv), along_y(q, table, T_DY), along_x(q, table, T_DXT)
    energy = flux_ref[...] * (gz * gz + gy * gy + gx * gx)
    energy = energy + HELM_COEF * mass_ref[0:ROWS] * (q * q)
    sum_rq = rows_sum(res_ref[...] * q_m)
    sum_aq = rows_sum(app_ref[...] * q_m)
    gather_send(2, (sum_rz, sum_za, sum_rq, sum_aq, rows_sum(energy), 0.0, 0.0, 0.0))
    gather_wait(2)
    sums = jnp.sum(jnp.sum(gbuf2[...], axis=0), axis=1, keepdims=True)
    rz, za, rq, aq, qq = (sums[k : k + 1] for k in range(5))

    step1 = rz / za
    rz_next = step1 * (step1 * aq - rq)
    beta1 = 1.0 + rz_next / rz
    norm2 = beta1 * beta1 * za - 2.0 * beta1 * step1 * aq + step1 * step1 * qq
    step2 = rz_next / norm2
    pressure_out[...] = (step1 + step2 * beta1) * search_ref[...] - (step2 * step1) * q

    for r, layers in enumerate((3, 1, 2, 1)):
        halo_drain(r, layers)
    for g in range(3):
        gather_bytes(g, gsend_sem.at[g])


def body(ngx, ngy, level_set, velocity, source, wick_solid):
    n = ngx * ngy
    npad = -(-n // 128) * 128
    consts = [jnp.asarray(t) for t in tables()]
    hbm = pl.BlockSpec(memory_space=pltpu.HBM)
    vmem = pl.BlockSpec(memory_space=pltpu.VMEM)
    shape = level_set.shape
    level_new, pressure = pl.pallas_call(
        functools.partial(kernel, ngx, ngy, gll_tables()[1], sine_table()),
        out_shape=[jax.ShapeDtypeStruct((ROWS, 128), F32)] * 2,
        in_specs=[hbm] * (4 + len(consts)),
        out_specs=[vmem] * 2,
        scratch_shapes=[
            pltpu.VMEM((ROWS, 128), F32),
            pltpu.VMEM((ROWS, 128), F32),
            pltpu.VMEM((ROWS, 128), F32),
            pltpu.VMEM((ROWS, 128), F32),
            pltpu.VMEM((ROWS, 128), F32),
            pltpu.VMEM((ROWS, 128), F32),
            pltpu.VMEM((ROWS, 128), F32),
            pltpu.VMEM((SPEC, 128), F32),
            pltpu.VMEM((n, npad), F32),
            pltpu.VMEM((4, 2, 96, 128), F32),
            pltpu.VMEM((4, 2, 96, 128), F32),
            pltpu.VMEM((4, 2, 24, 128), F32),
            pltpu.VMEM((4, 2, 24, 128), F32),
            pltpu.VMEM((4, 4, 8, 128), F32),
            pltpu.VMEM((4, 4, 8, 128), F32),
            pltpu.VMEM((n, 2, 128), F32),
            pltpu.VMEM((n, 1, 128), F32),
            pltpu.VMEM((n, 8, 128), F32),
            pltpu.VMEM((ROWS, 128), F32),
            pltpu.VMEM((3 * ROWS, 128), F32),
            pltpu.VMEM((ROWS, 128), F32),
            pltpu.VMEM((1, EY, EX), jnp.int32),
            *[pltpu.VMEM(t.shape, t.dtype) for t in consts],
            pltpu.SemaphoreType.DMA((4, 8)),
            pltpu.SemaphoreType.DMA((4, 8)),
            pltpu.SemaphoreType.DMA((3,)),
            pltpu.SemaphoreType.DMA((3,)),
            pltpu.SemaphoreType.DMA((7,)),
        ],
        compiler_params=pltpu.CompilerParams(
            collective_id=0, has_side_effects=True, vmem_limit_bytes=63 * 1024 * 1024
        ),
    )(
        level_set.reshape(ROWS, 128),
        velocity.reshape(3 * ROWS, 128),
        source.reshape(ROWS, 128),
        wick_solid,
        *consts,
    )
    return level_new.reshape(shape), pressure.reshape(shape)


def solution(mesh):
    placed = (
        P("gx", "gy", None),
        P(None, "gx", "gy", None),
        P("gx", "gy", None),
        P("gx", "gy", None),
    )
    return jax.shard_map(
        functools.partial(body, mesh.shape["gx"], mesh.shape["gy"]),
        mesh=mesh,
        in_specs=placed,
        out_specs=(P("gx", "gy", None), P("gx", "gy", None)),
        check_vma=False,
    )
```

```python
import functools

import jax
import jax.numpy as jnp
import ml_dtypes
import numpy as np
from jax import lax
from jax.experimental import pallas as pl
from jax.experimental.pallas import tpu as pltpu
from jax.sharding import PartitionSpec as P

EZ = 1
EY = 4
EX = 16
ROWS = 256
PLANE = 40
SPEC = 400
T_DY, T_DYT, T_DXT, T_DX, T_SX, T_BX = 0, 128, 256, 512, 768, 1152
T_SY, T_BY, T_END = 1408, 1824, 2144

TIME_STEP = 0.02
HELM_COEF = 0.25
LEVEL_WIDTH = 0.25
GAS_RATIO = 10.0
SOLID_FACTOR = 0.25
SCHWARZ_SCALE = 0.5
SCHWARZ_SHIFT = 0.05

MESH = pl.DeviceIdType.MESH
LOGICAL = pl.DeviceIdType.LOGICAL
F32 = jnp.float32
BF16 = jnp.bfloat16

SIDES = ((-1, 0), (1, 0), (0, -1), (0, 1), (-1, -1), (-1, 1), (1, -1), (1, 1))
OPPOSITE = tuple(SIDES.index((-dz, -dy)) for dz, dy in SIDES)


def gll_tables():
    nodes = np.array(
        [
            -1.0,
            -0.8717401485096066,
            -0.5917001814331423,
            -0.2092992179024789,
            0.2092992179024789,
            0.5917001814331423,
            0.8717401485096066,
            1.0,
        ]
    )
    weight = np.array(
        [
            1.0 / 28.0,
            0.21070422714350603,
            0.3411226924835044,
            0.4124587946587038,
            0.4124587946587038,
            0.3411226924835044,
            0.21070422714350603,
            1.0 / 28.0,
        ]
    )
    bary = np.array(
        [1.0 / np.prod([nodes[i] - nodes[j] for j in range(8) if j != i]) for i in range(8)]
    )
    deriv = np.zeros((8, 8))
    for i in range(8):
        for j in range(8):
            if i != j:
                deriv[i, j] = bary[j] / bary[i] / (nodes[i] - nodes[j])
        deriv[i, i] = -np.sum(deriv[i])
    return weight, deriv


def halves(table):
    table = np.asarray(table, np.float32)
    high = table.astype(ml_dtypes.bfloat16)
    low = (table - high.astype(np.float32)).astype(ml_dtypes.bfloat16)
    return high, low


def tables():
    weight, deriv = gll_tables()
    ids = np.arange(10) + 1.0
    sine = sine_table()
    eig = 2.0 - 2.0 * np.cos(np.pi * ids / 11.0)
    dy = np.kron(np.eye(16), deriv)
    dx_t = np.kron(np.eye(EX), deriv.T)
    dx = np.kron(np.eye(EX), deriv)

    widen_y = np.zeros((PLANE, PLANE))
    for e in range(EY):
        for yi in range(10):
            y = 8 * e - 2 if yi == 0 else (8 * e + 9 if yi == 9 else 8 * e + yi - 1)
            widen_y[e * 10 + yi, 32 if y < 0 else (33 if y > 31 else y)] = 1.0
    spec_y = np.kron(np.eye(5), np.kron(np.eye(EY), sine) @ widen_y)
    widen_x = np.zeros((160, 128))
    for e in range(EX):
        for xi in range(10):
            x = 8 * e - 2 if xi == 0 else (8 * e + 9 if xi == 9 else 8 * e + xi - 1)
            if 0 <= x < 128:
                widen_x[e * 10 + xi, x] = 1.0
    spec_x = np.zeros((128, 256))
    spec_x[:, :160] = (np.kron(np.eye(EX), sine) @ widen_x).T
    back_y = np.kron(np.eye(5), np.kron(np.eye(EY), sine[1:9]))
    back_x = np.zeros((256, 128))
    back_x[:160] = np.kron(np.eye(EX), sine[1:9]).T
    lam_zy = (eig[:, None] + np.tile(eig, EY)[None, :]).reshape(SPEC)
    inv_den = np.zeros((SPEC, 256))
    inv_den[:, :160] = 1.0 / (
        SCHWARZ_SCALE * (lam_zy[:, None] + np.tile(eig, EX)[None, :]) + SCHWARZ_SHIFT
    )
    mass = 0.125 * (
        np.kron(weight, np.tile(weight, EY))[:, None] * np.tile(weight, EX)[None, :]
    )
    spread = np.zeros((16, 128))
    spread[:EX] = np.kron(np.eye(EX), np.ones((1, 8)))

    def beside(table):
        high, low = halves(table)
        return np.concatenate([high, low], axis=1)

    def both(table):
        high, low = halves(table)
        zero = np.zeros_like(low)
        return np.concatenate(
            [np.concatenate([high, low], axis=1), np.concatenate([high, zero], axis=1)], axis=0
        )

    def under(table):
        high, low = halves(table)
        return np.concatenate([high, high, low], axis=0)

    def padded(table, rows, cols):
        out = np.zeros((rows, cols))
        out[: table.shape[0], : table.shape[1]] = table
        return out

    return (
        np.concatenate(
            [
                beside(dy), beside(dy.T), both(dx_t), both(dx), under(spec_x), beside(back_x),
                *halves(padded(spec_y, 208, 256)), *halves(padded(back_y, 160, 256)),
            ],
            axis=0,
        ),
        np.concatenate([mass, spread], axis=0).astype(np.float32),
        inv_den.astype(np.float32),
    )


def sine_table():
    ids = np.arange(10) + 1.0
    return np.sqrt(2.0 / 11.0) * np.sin(np.pi * np.outer(ids, ids) / 11.0)


def split(v):
    high = v.astype(BF16)
    low = (v - high.astype(F32)).astype(BF16)
    return high, low


def dot(a, b):
    return jnp.dot(a, b, preferred_element_type=F32)


def along_y(v, ref, base):
    vh, vl = split(jnp.concatenate([v[:128], v[128:]], axis=1))
    table = ref[base : base + 128, :]
    out = dot(table, jnp.concatenate([vh, vh], axis=0)) + dot(table[:, :128], vl)
    return jnp.concatenate([out[:, :128], out[:, 128:]], axis=0)


def along_x(v, ref, base):
    vh, vl = split(v)
    out = dot(jnp.concatenate([vh, vl], axis=1), ref[base : base + 256, :])
    return out[:, :128] + out[:, 128:]


def planes_y(v, ref, base, rows, pad):
    vh, vl = split(jnp.concatenate([v[:200], v[200:]], axis=1))
    high = ref[base : base + pad, :200]
    low = ref[base + pad : base + 2 * pad, :200]
    out = dot(high, vh) + dot(high, vl) + dot(low, vh)
    return jnp.concatenate([out[:rows, :128], out[:rows, 128:]], axis=0)


def sine_z(planes, sine, keep):
    even = [planes[k] + planes[9 - k] for k in range(5)]
    odd = [planes[k] - planes[9 - k] for k in range(5)]
    out = []
    for j in keep:
        terms = [float(sine[j, k]) * (odd if j % 2 else even)[k] for k in range(5)]
        out.append(functools.reduce(lambda a, b: a + b, terms))
    return out


def along_z(v, table):
    planes = [v[32 * i : 32 * i + 32] for i in range(8)]
    even = [planes[j] + planes[7 - j] for j in range(4)]
    odd = [planes[j] - planes[7 - j] for j in range(4)]
    low, high = [], []
    for i in range(4):
        a = b = None
        for j in range(4):
            p = float(table[i, j] + table[i, 7 - j]) / 2.0 * even[j]
            q = float(table[i, j] - table[i, 7 - j]) / 2.0 * odd[j]
            a, b = (p, q) if a is None else (a + p, b + q)
        low.append(a + b)
        high.insert(0, b - a)
    return jnp.concatenate(low + high, axis=0)


def total(v):
    return jnp.sum(jnp.sum(v, axis=0, keepdims=True), axis=1, keepdims=True)


def sweep_step(a, row, col, k, sub, lane):
    pivot = jnp.sum(jnp.where(lane[:1] == k, row, 0.0), axis=1, keepdims=True)
    row_m = jnp.where(lane[:1] == k, -1.0, row) / pivot
    col_m = jnp.where(sub == k, -1.0, col)
    return jnp.where(jnp.logical_or(lane == k, sub == k), 0.0, a) - col_m * row_m


def kernel(
    ngx, ngy, deriv, sine,
    level_hbm, vel_hbm, source_hbm, solid_hbm, *refs
):
    tables_hbm, refs = refs[:3], refs[3:]
    level_out, pressure_out = refs[:2]
    (
        flux_ref, invm_ref, part_ref, lev_ref, app_ref, res_ref, search_ref, ext_ref, a_ref,
        zs, zr, ys, yr, cs, cr, gbuf0, gbuf1, gbuf2,
        level_ref, vel_ref, source_ref, solid_ref,
        table, mass_ref, den_ref,
        send_sem, recv_sem, gsend_sem, grecv_sem, load_sem,
    ) = refs[2:]
    loads = [
        pltpu.make_async_copy(src, dst, load_sem.at[i])
        for i, (src, dst) in enumerate(
            zip(
                (level_hbm, vel_hbm, source_hbm, solid_hbm) + tables_hbm,
                (level_ref, vel_ref, source_ref, solid_ref)
                + (table, mass_ref, den_ref),
            )
        )
    ]
    for i in (4, 0, 1, 5, 2, 3, 6):
        loads[i].start()
    gbufs = (gbuf0, gbuf1, gbuf2)
    n = ngx * ngy
    ix = lax.axis_index("gx")
    iy = lax.axis_index("gy")
    me = ix * ngy + iy

    def other(i):
        at = me + i
        return jnp.where(at >= n, at - n, at)

    zr[...] = jnp.zeros_like(zr)
    yr[...] = jnp.zeros_like(yr)
    cr[...] = jnp.zeros_like(cr)
    ext_ref[...] = jnp.zeros_like(ext_ref)

    barrier = pltpu.get_barrier_semaphore()

    def greet(i, carry):
        pl.semaphore_signal(barrier, inc=1, device_id=other(i), device_id_type=LOGICAL)
        return carry

    lax.fori_loop(1, n, greet, 0, unroll=n <= 64)

    has_zlo, has_zhi = ix > 0, ix < ngx - 1
    has_ylo, has_yhi = iy > 0, iy < ngy - 1

    def exists(d):
        dz, dy = SIDES[d]
        conds = []
        if dz:
            conds.append(has_zlo if dz < 0 else has_zhi)
        if dy:
            conds.append(has_ylo if dy < 0 else has_yhi)
        return conds[0] if len(conds) == 1 else jnp.logical_and(*conds)

    def buffers(r, d, layers):
        if d < 2:
            return zs.at[r, d, pl.ds(0, 32 * layers)], zr.at[r, OPPOSITE[d], pl.ds(0, 32 * layers)]
        if d < 4:
            return (
                ys.at[r, d - 2, pl.ds(0, 8 * layers)],
                yr.at[r, OPPOSITE[d] - 2, pl.ds(0, 8 * layers)],
            )
        return cs.at[r, d - 4], cr.at[r, OPPOSITE[d] - 4]

    def halo_copy(r, d, layers):
        src, dst = buffers(r, d, layers)
        dz, dy = SIDES[d]
        return pltpu.make_async_remote_copy(
            src_ref=src,
            dst_ref=dst,
            send_sem=send_sem.at[r, d],
            recv_sem=recv_sem.at[r, OPPOSITE[d]],
            device_id=(ix + dz, iy + dy),
            device_id_type=MESH,
        )

    def halo_send(r, layers, second=None):
        for s in range(2):
            zo, zi = ((0, 32), (224, 192))[s]
            zs[r, s, 0:32] = part_ref[zo : zo + 32]
            yo, yi = ((0, 1), (31, 30))[s]
            ys[r, s, 0:8] = part_ref[pl.ds(yo, 8, stride=32), :]
            if layers > 1:
                zs[r, s, 32:64] = part_ref[zi : zi + 32]
                ys[r, s, 8:16] = part_ref[pl.ds(yi, 8, stride=32), :]
            if second is not None:
                zs[r, s, 64:96] = second[zo : zo + 32]
                ys[r, s, 16:24] = second[pl.ds(yo, 8, stride=32), :]
        for c in range(4):
            dz, dy = SIDES[4 + c]
            zo, zi = (0, 32) if dz < 0 else (224, 192)
            yo, yi = (0, 1) if dy < 0 else (31, 30)
            cs[r, c, 0:1] = part_ref[zo + yo : zo + yo + 1]
            if layers > 1:
                cs[r, c, 1:2] = part_ref[zo + yi : zo + yi + 1]
                cs[r, c, 2:3] = part_ref[zi + yo : zi + yo + 1]
                cs[r, c, 3:4] = part_ref[zi + yi : zi + yi + 1]
            if second is not None:
                cs[r, c, 4:5] = second[zo + yo : zo + yo + 1]
        for d in range(8):

            @pl.when(exists(d))
            def _():
                halo_copy(r, d, layers).start()

    def halo_wait(r, layers):
        for d in range(8):

            @pl.when(exists(d))
            def _():
                src, _ = buffers(r, d, layers)
                _, dst = buffers(r, OPPOSITE[d], layers)
                dz, dy = SIDES[d]
                pltpu.make_async_remote_copy(
                    src_ref=src,
                    dst_ref=dst,
                    send_sem=send_sem.at[r, d],
                    recv_sem=recv_sem.at[r, d],
                    device_id=(ix + dz, iy + dy),
                    device_id_type=MESH,
                ).wait_recv()

    def halo_drain(r, layers):
        for d in range(8):

            @pl.when(exists(d))
            def _():
                halo_copy(r, d, layers).wait_send()

    def add_rim(r, ref, zoff, yoff, crow):
        ref[0:32] = ref[0:32] + zr[r, 0, zoff : zoff + 32]
        ref[224:256] = ref[224:256] + zr[r, 1, zoff : zoff + 32]
        for s, yo in ((0, 0), (1, 31)):
            at = pl.ds(yo, 8, stride=32)
            ref[at, :] = ref[at, :] + yr[r, s, yoff : yoff + 8]
        for c, row in enumerate((0, 31, 224, 255)):
            ref[row : row + 1] = ref[row : row + 1] + cr[r, c, crow : crow + 1]

    def outer_halo(r):
        for s in range(2):
            base = 9 * PLANE * s
            ext_ref[base : base + 32] = zr[r, s, 32:64]
            ext_ref[base : base + 1] = ext_ref[base : base + 1] + cr[r, 2 * s, 2:3]
            at = base + 31
            ext_ref[at : at + 1] = ext_ref[at : at + 1] + cr[r, 2 * s + 1, 2:3]
            ext_ref[pl.ds(PLANE + 32 + s, 8, stride=PLANE), :] = yr[r, s, 8:16]
            for at, c in ((PLANE + 32 + s, s), (8 * PLANE + 32 + s, 2 + s)):
                ext_ref[at : at + 1] = ext_ref[at : at + 1] + cr[r, c, 1:2]
        for c in range(4):
            at = 9 * PLANE * (c // 2) + 32 + c % 2
            ext_ref[at : at + 1] = cr[r, c, 3:4]

    def gather_copy(g, dst):
        ref = gbufs[g].at[me]
        return pltpu.make_async_remote_copy(
            src_ref=ref,
            dst_ref=ref,
            send_sem=gsend_sem.at[g],
            recv_sem=grecv_sem.at[g],
            device_id=dst,
            device_id_type=LOGICAL,
        )

    def gather_send(g, rows):
        for k, value in enumerate(rows):
            gbufs[g][me, k : k + 1] = jnp.broadcast_to(value, (1, 128))

        def send(i, carry):
            gather_copy(g, other(i)).start()
            return carry

        lax.fori_loop(1, n, send, 0, unroll=n <= 64)

    def gather_bytes(g, sem):
        ref = gbufs[g].at[pl.ds(0, n - 1)]
        pltpu.make_async_copy(ref, ref, sem).wait()

    def gather_wait(g):
        gather_bytes(g, grecv_sem.at[g])

    row = lax.broadcasted_iota(jnp.int32, (ROWS, 128), 0)
    lane = lax.broadcasted_iota(jnp.int32, (ROWS, 128), 1)
    zpos, ypos = row // 32, row % 32
    y8, x8 = row % 8, lane % 8
    y_first = jnp.logical_and(y8 == 0, ypos > 0).astype(F32)
    y_last = jnp.logical_and(y8 == 7, ypos < 31).astype(F32)
    x_first = jnp.logical_and(x8 == 0, lane > 0).astype(F32)
    x_last = jnp.logical_and(x8 == 7, lane < 127).astype(F32)

    def flag(c):
        return c.astype(jnp.int32).astype(F32)

    zlo_f, zhi_f, ylo_f, yhi_f = flag(has_zlo), flag(has_zhi), flag(has_ylo), flag(has_yhi)
    z0, z7 = (zpos == 0).astype(F32), (zpos == 7).astype(F32)
    yb0, yb31 = (ypos == 0).astype(F32), (ypos == 31).astype(F32)
    half_zlo, half_zhi = 0.5 * zlo_f * z0, 0.5 * zhi_f * z7
    half_ylo, half_yhi = 0.5 * ylo_f * yb0, 0.5 * yhi_f * yb31
    own_z, own_y = 1.0 - half_zlo - half_zhi, 1.0 - half_ylo - half_yhi
    inv_m = (
        own_z
        * (own_y - 0.5 * (y_first + y_last))
        * (1.0 - 0.5 * (x_first + x_last))
    )
    invm_ref[...] = inv_m

    def fold_in(v):
        v = v + x_first * pltpu.roll(v, 1, 1) + x_last * pltpu.roll(v, 127, 1)
        return v + y_first * pltpu.roll(v, 1, 0) + y_last * pltpu.roll(v, ROWS - 1, 0)

    for i in (4, 0, 1, 5):
        loads[i].wait()
    mass = mass_ref[0:ROWS]
    level = level_ref[...]
    advect = (
        vel_ref[0:ROWS] * along_z(level, deriv)
        + vel_ref[ROWS : 2 * ROWS] * along_y(level, table, T_DY)
        + vel_ref[2 * ROWS : 3 * ROWS] * along_x(level, table, T_DXT)
    )
    lev_ref[...] = fold_in(mass * (level - (2.0 * TIME_STEP) * advect))
    diverge = (
        along_z(vel_ref[0:ROWS], deriv)
        + along_y(vel_ref[ROWS : 2 * ROWS], table, T_DY)
        + along_x(vel_ref[2 * ROWS : 3 * ROWS], table, T_DXT)
    )
    loads[2].wait()
    part_ref[...] = fold_in(mass * (source_ref[...] - (2.0 * TIME_STEP) * diverge))

    pl.semaphore_wait(barrier, n - 1)
    halo_send(0, 3, lev_ref)
    res_ref[...] = part_ref[...]
    loads[3].wait()
    solid = dot(solid_ref[0].astype(F32), mass_ref[ROWS : ROWS + EX])
    solid = jnp.concatenate(
        [jnp.broadcast_to(solid[e : e + 1], (8, 128)) for e in range(EY)], axis=0
    )
    solid = jnp.concatenate([solid] * 8, axis=0)
    halo_wait(0, 3)
    add_rim(0, res_ref, 0, 0, 0)
    add_rim(0, lev_ref, 64, 16, 4)
    outer_halo(0)
    level_new = lev_ref[...] * inv_m / mass
    level_out[...] = level_new
    coef = (GAS_RATIO - (GAS_RATIO - 1.0) * jax.nn.sigmoid(level_new / LEVEL_WIDTH)) * (
        1.0 - (1.0 - SOLID_FACTOR) * solid
    )
    flux_ref[...] = 4.0 * coef * mass
    gather_send(0, (total(coef) / (ROWS * 128.0), total(res_ref[...] * inv_m)))

    def local_solve(v):
        for z in range(8):
            ext_ref[PLANE * (z + 1) : PLANE * (z + 1) + 32] = v[32 * z : 32 * z + 32]
        planes = [ext_ref[PLANE * z : PLANE * z + PLANE] for z in range(10)]
        wide = jnp.concatenate(sine_z(planes, sine, range(10)), axis=0)
        wide = planes_y(wide, table, T_SY, 200, 208)
        wh, wl = split(wide)
        spectral = dot(jnp.concatenate([wh, wl], axis=1), table[T_SX : T_SX + 256, :])
        spectral = spectral + dot(wh, table[T_SX + 256 : T_SX + 384, :])
        sh, sl = split(spectral * den_ref[...])
        back = dot(sh, table[T_BX : T_BX + 256, :])
        back = back[:, :128] + back[:, 128:] + dot(sl, table[T_BX : T_BX + 256, :128])
        back = planes_y(back, table, T_BY, 160, 160)
        planes = [back[32 * z : 32 * z + 32] for z in range(10)]
        return jnp.concatenate(sine_z(planes, sine, range(1, 9)), axis=0)

    def helm(v):
        flux = flux_ref[...]
        out = along_z(flux * along_z(v, deriv), deriv.T)
        out = out + along_y(flux * along_y(v, table, T_DY), table, T_DYT)
        out = out + along_x(flux * along_x(v, table, T_DXT), table, T_DX)
        return out + HELM_COEF * mass_ref[0:ROWS] * v

    npad = a_ref.shape[1]
    sub_n = lax.broadcasted_iota(jnp.int32, (n, npad), 0)
    lane_n = lax.broadcasted_iota(jnp.int32, (n, npad), 1)

    def gathered(g, item):
        got = gbufs[g][:, item, :]
        return got if npad == 128 else jnp.concatenate([got] * (npad // 128), axis=1)

    def invert(k_col):
        diag = lane_n == sub_n
        k_row = jnp.sum(jnp.where(diag, k_col, 0.0), axis=0, keepdims=True)
        gap = lane_n - sub_n
        same = lane_n // ngy == sub_n // ngy
        y_link = jnp.logical_and(jnp.logical_or(gap == 1, gap == -1), same)
        z_link = jnp.logical_or(gap == ngy, gap == -ngy)
        rate = jnp.where(z_link, float(EY * EX) / EZ, 0.0) + jnp.where(
            y_link, float(EZ * EX) / EY, 0.0
        )
        rate = jnp.where(lane_n < n, rate, 0.0)
        link = 2.0 * k_col * k_row / (k_col + k_row) * rate
        diagonal = HELM_COEF * EZ * EY * EX + jnp.sum(link, axis=1, keepdims=True)
        a = jnp.where(diag, diagonal, -link)
        if ngx == 2 and n <= 64:
            left_over = list(range(ngy))
            while left_over:
                now = left_over[1::2] or left_over
                left_over = left_over[0::2] if len(left_over) > 1 else []
                cross = jnp.zeros((n, npad), jnp.bool_)
                change = None
                for j in now:
                    k, m = j, ngy + j
                    c1 = jnp.broadcast_to(a[:, k : k + 1], (n, npad))
                    c2 = jnp.broadcast_to(a[:, m : m + 1], (n, npad))
                    p11, p12, p22 = c1[k : k + 1], c2[k : k + 1], c2[m : m + 1]
                    scale = 1.0 / (p11 * p22 - p12 * p12)
                    at1, at2 = lane_n == k, lane_n == m
                    on1, on2 = sub_n == k, sub_n == m
                    r1 = jnp.where(at1[:1], -1.0, jnp.where(at2[:1], 0.0, a[k : k + 1]))
                    r2 = jnp.where(at2[:1], -1.0, jnp.where(at1[:1], 0.0, a[m : m + 1]))
                    q1 = (p22 * r1 - p12 * r2) * scale
                    q2 = (p11 * r2 - p12 * r1) * scale
                    c1 = jnp.where(on1, -1.0, jnp.where(on2, 0.0, c1))
                    c2 = jnp.where(on2, -1.0, jnp.where(on1, 0.0, c2))
                    cross = cross | at1 | at2 | on1 | on2
                    term = c1 * q1 + c2 * q2
                    change = term if change is None else change + term
                a = jnp.where(cross, 0.0, a) - change
            a_ref[...] = a
        else:
            a_ref[...] = a

            def step(k, carry):
                a = a_ref[...]
                row = a_ref[pl.ds(k, 1), :]
                col = jnp.sum(jnp.where(lane_n == k, a, 0.0), axis=1, keepdims=True)
                a_ref[...] = sweep_step(a, row, col, k, sub_n, lane_n)
                return carry

            lax.fori_loop(0, n, step, 0)

    def coarse(t_col):
        return -jnp.sum(a_ref[...] * t_col, axis=0, keepdims=True)

    def coarse_field(x):
        def value(dz, dy):
            at = me + dz * ngy + dy
            return jnp.sum(jnp.where(lane_n[:1] == at, x, 0.0), axis=1, keepdims=True)

        def along_y(dz):
            return own_y * value(dz, 0) + half_ylo * value(dz, -1) + half_yhi * value(dz, 1)

        return own_z * along_y(0) + half_zlo * along_y(-1) + half_zhi * along_y(1)

    def rows_sum(v):
        return jnp.sum(v, axis=0, keepdims=True)

    loads[6].wait()
    part_ref[...] = fold_in(local_solve(res_ref[...]) * inv_m)
    halo_send(1, 1)
    gather_wait(0)
    invert(gathered(0, 0))
    field = coarse_field(coarse(gathered(0, 1)))
    halo_wait(1, 1)
    search_ref[...] = part_ref[...]
    add_rim(1, search_ref, 0, 0, 0)
    z1 = search_ref[...] + field
    search_ref[...] = z1

    applied = helm(z1)
    part_ref[...] = fold_in(applied)
    halo_send(2, 2)
    sum_rz = rows_sum(res_ref[...] * z1 * inv_m)
    sum_za = rows_sum(z1 * applied)
    app_ref[...] = part_ref[...]
    halo_wait(2, 2)
    add_rim(2, app_ref, 0, 0, 0)
    outer_halo(2)
    gather_send(1, (total(app_ref[...] * invm_ref[...]),))

    part_ref[...] = fold_in(local_solve(app_ref[...]) * invm_ref[...])
    halo_send(3, 1)
    gather_wait(1)
    field = coarse_field(coarse(gathered(1, 0)))
    halo_wait(3, 1)
    add_rim(3, part_ref, 0, 0, 0)
    q = part_ref[...] + field

    q_m = q * invm_ref[...]
    gz, gy, gx = along_z(q, deriv), along_y(q, table, T_DY), along_x(q, table, T_DXT)
    energy = flux_ref[...] * (gz * gz + gy * gy + gx * gx)
    energy = energy + HELM_COEF * mass_ref[0:ROWS] * (q * q)
    sum_rq = rows_sum(res_ref[...] * q_m)
    sum_aq = rows_sum(app_ref[...] * q_m)
    gather_send(2, (sum_rz, sum_za, sum_rq, sum_aq, rows_sum(energy), 0.0, 0.0, 0.0))
    gather_wait(2)
    sums = jnp.sum(jnp.sum(gbuf2[...], axis=0), axis=1, keepdims=True)
    rz, za, rq, aq, qq = (sums[k : k + 1] for k in range(5))

    step1 = rz / za
    rz_next = step1 * (step1 * aq - rq)
    beta1 = 1.0 + rz_next / rz
    norm2 = beta1 * beta1 * za - 2.0 * beta1 * step1 * aq + step1 * step1 * qq
    step2 = rz_next / norm2
    pressure_out[...] = (step1 + step2 * beta1) * search_ref[...] - (step2 * step1) * q

    for r, layers in enumerate((3, 1, 2, 1)):
        halo_drain(r, layers)
    for g in range(3):
        gather_bytes(g, gsend_sem.at[g])


def body(ngx, ngy, level_set, velocity, source, wick_solid):
    n = ngx * ngy
    npad = -(-n // 128) * 128
    consts = [jnp.asarray(t) for t in tables()]
    hbm = pl.BlockSpec(memory_space=pltpu.HBM)
    vmem = pl.BlockSpec(memory_space=pltpu.VMEM)
    shape = level_set.shape
    level_new, pressure = pl.pallas_call(
        functools.partial(kernel, ngx, ngy, gll_tables()[1], sine_table()),
        out_shape=[jax.ShapeDtypeStruct((ROWS, 128), F32)] * 2,
        in_specs=[hbm] * (4 + len(consts)),
        out_specs=[vmem] * 2,
        scratch_shapes=[
            pltpu.VMEM((ROWS, 128), F32),
            pltpu.VMEM((ROWS, 128), F32),
            pltpu.VMEM((ROWS, 128), F32),
            pltpu.VMEM((ROWS, 128), F32),
            pltpu.VMEM((ROWS, 128), F32),
            pltpu.VMEM((ROWS, 128), F32),
            pltpu.VMEM((ROWS, 128), F32),
            pltpu.VMEM((SPEC, 128), F32),
            pltpu.VMEM((n, npad), F32),
            pltpu.VMEM((4, 2, 96, 128), F32),
            pltpu.VMEM((4, 2, 96, 128), F32),
            pltpu.VMEM((4, 2, 24, 128), F32),
            pltpu.VMEM((4, 2, 24, 128), F32),
            pltpu.VMEM((4, 4, 8, 128), F32),
            pltpu.VMEM((4, 4, 8, 128), F32),
            pltpu.VMEM((n, 2, 128), F32),
            pltpu.VMEM((n, 1, 128), F32),
            pltpu.VMEM((n, 8, 128), F32),
            pltpu.VMEM((ROWS, 128), F32),
            pltpu.VMEM((3 * ROWS, 128), F32),
            pltpu.VMEM((ROWS, 128), F32),
            pltpu.VMEM((1, EY, EX), jnp.int32),
            *[pltpu.VMEM(t.shape, t.dtype) for t in consts],
            pltpu.SemaphoreType.DMA((4, 8)),
            pltpu.SemaphoreType.DMA((4, 8)),
            pltpu.SemaphoreType.DMA((3,)),
            pltpu.SemaphoreType.DMA((3,)),
            pltpu.SemaphoreType.DMA((7,)),
        ],
        compiler_params=pltpu.CompilerParams(
            collective_id=0, has_side_effects=True, vmem_limit_bytes=54848 * 1024
        ),
    )(
        level_set.reshape(ROWS, 128),
        velocity.reshape(3 * ROWS, 128),
        source.reshape(ROWS, 128),
        wick_solid,
        *consts,
    )
    return level_new.reshape(shape), pressure.reshape(shape)


def solution(mesh):
    placed = (
        P("gx", "gy", None),
        P(None, "gx", "gy", None),
        P("gx", "gy", None),
        P("gx", "gy", None),
    )
    return jax.shard_map(
        functools.partial(body, mesh.shape["gx"], mesh.shape["gy"]),
        mesh=mesh,
        in_specs=placed,
        out_specs=(P("gx", "gy", None), P("gx", "gy", None)),
        check_vma=False,
    )
```

```python
import functools

import jax
import jax.numpy as jnp
import ml_dtypes
import numpy as np
from jax import lax
from jax.experimental import pallas as pl
from jax.experimental.pallas import tpu as pltpu
from jax.sharding import PartitionSpec as P

EZ = 1
EY = 4
EX = 16
ROWS = 256
PLANE = 40
SPEC = 400
T_DY, T_DYT, T_DXT, T_DX, T_SX, T_BX = 0, 128, 256, 512, 768, 1152
T_SY, T_BY, T_END = 1408, 1824, 2144

TIME_STEP = 0.02
HELM_COEF = 0.25
LEVEL_WIDTH = 0.25
GAS_RATIO = 10.0
SOLID_FACTOR = 0.25
SCHWARZ_SCALE = 0.5
SCHWARZ_SHIFT = 0.05

MESH = pl.DeviceIdType.MESH
LOGICAL = pl.DeviceIdType.LOGICAL
F32 = jnp.float32
BF16 = jnp.bfloat16

SIDES = ((-1, 0), (1, 0), (0, -1), (0, 1), (-1, -1), (-1, 1), (1, -1), (1, 1))
OPPOSITE = tuple(SIDES.index((-dz, -dy)) for dz, dy in SIDES)


def gll_tables():
    nodes = np.array(
        [
            -1.0,
            -0.8717401485096066,
            -0.5917001814331423,
            -0.2092992179024789,
            0.2092992179024789,
            0.5917001814331423,
            0.8717401485096066,
            1.0,
        ]
    )
    weight = np.array(
        [
            1.0 / 28.0,
            0.21070422714350603,
            0.3411226924835044,
            0.4124587946587038,
            0.4124587946587038,
            0.3411226924835044,
            0.21070422714350603,
            1.0 / 28.0,
        ]
    )
    bary = np.array(
        [1.0 / np.prod([nodes[i] - nodes[j] for j in range(8) if j != i]) for i in range(8)]
    )
    deriv = np.zeros((8, 8))
    for i in range(8):
        for j in range(8):
            if i != j:
                deriv[i, j] = bary[j] / bary[i] / (nodes[i] - nodes[j])
        deriv[i, i] = -np.sum(deriv[i])
    return weight, deriv


def halves(table):
    table = np.asarray(table, np.float32)
    high = table.astype(ml_dtypes.bfloat16)
    low = (table - high.astype(np.float32)).astype(ml_dtypes.bfloat16)
    return high, low


def tables():
    weight, deriv = gll_tables()
    ids = np.arange(10) + 1.0
    sine = sine_table()
    eig = 2.0 - 2.0 * np.cos(np.pi * ids / 11.0)
    dy = np.kron(np.eye(16), deriv)
    dx_t = np.kron(np.eye(EX), deriv.T)
    dx = np.kron(np.eye(EX), deriv)

    widen_y = np.zeros((PLANE, PLANE))
    for e in range(EY):
        for yi in range(10):
            y = 8 * e - 2 if yi == 0 else (8 * e + 9 if yi == 9 else 8 * e + yi - 1)
            widen_y[e * 10 + yi, 32 if y < 0 else (33 if y > 31 else y)] = 1.0
    spec_y = np.kron(np.eye(5), np.kron(np.eye(EY), sine) @ widen_y)
    widen_x = np.zeros((160, 128))
    for e in range(EX):
        for xi in range(10):
            x = 8 * e - 2 if xi == 0 else (8 * e + 9 if xi == 9 else 8 * e + xi - 1)
            if 0 <= x < 128:
                widen_x[e * 10 + xi, x] = 1.0
    spec_x = np.zeros((128, 256))
    spec_x[:, :160] = (np.kron(np.eye(EX), sine) @ widen_x).T
    back_y = np.kron(np.eye(5), np.kron(np.eye(EY), sine[1:9]))
    back_x = np.zeros((256, 128))
    back_x[:160] = np.kron(np.eye(EX), sine[1:9]).T
    lam_zy = (eig[:, None] + np.tile(eig, EY)[None, :]).reshape(SPEC)
    inv_den = np.zeros((SPEC, 256))
    inv_den[:, :160] = 1.0 / (
        SCHWARZ_SCALE * (lam_zy[:, None] + np.tile(eig, EX)[None, :]) + SCHWARZ_SHIFT
    )
    mass = 0.125 * (
        np.kron(weight, np.tile(weight, EY))[:, None] * np.tile(weight, EX)[None, :]
    )
    spread = np.zeros((16, 128))
    spread[:EX] = np.kron(np.eye(EX), np.ones((1, 8)))

    def beside(table):
        high, low = halves(table)
        return np.concatenate([high, low], axis=1)

    def both(table):
        high, low = halves(table)
        zero = np.zeros_like(low)
        return np.concatenate(
            [np.concatenate([high, low], axis=1), np.concatenate([high, zero], axis=1)], axis=0
        )

    def under(table):
        high, low = halves(table)
        return np.concatenate([high, high, low], axis=0)

    def padded(table, rows, cols):
        out = np.zeros((rows, cols))
        out[: table.shape[0], : table.shape[1]] = table
        return out

    return (
        np.concatenate(
            [
                beside(dy), beside(dy.T), both(dx_t), both(dx), under(spec_x), beside(back_x),
                *halves(padded(spec_y, 208, 256)), *halves(padded(back_y, 160, 256)),
            ],
            axis=0,
        ),
        np.concatenate([mass, spread], axis=0).astype(np.float32),
        inv_den.astype(np.float32),
    )


def sine_table():
    ids = np.arange(10) + 1.0
    return np.sqrt(2.0 / 11.0) * np.sin(np.pi * np.outer(ids, ids) / 11.0)


def split(v):
    high = v.astype(BF16)
    low = (v - high.astype(F32)).astype(BF16)
    return high, low


def dot(a, b):
    return jnp.dot(a, b, preferred_element_type=F32)


def along_y(v, ref, base):
    vh, vl = split(jnp.concatenate([v[:128], v[128:]], axis=1))
    table = ref[base : base + 128, :]
    out = dot(table, jnp.concatenate([vh, vh], axis=0)) + dot(table[:, :128], vl)
    return jnp.concatenate([out[:, :128], out[:, 128:]], axis=0)


def along_x(v, ref, base):
    vh, vl = split(v)
    out = dot(jnp.concatenate([vh, vl], axis=1), ref[base : base + 256, :])
    return out[:, :128] + out[:, 128:]


def planes_y(v, ref, base, rows, pad):
    vh, vl = split(jnp.concatenate([v[:200], v[200:]], axis=1))
    high = ref[base : base + pad, :200]
    low = ref[base + pad : base + 2 * pad, :200]
    out = dot(high, vh) + dot(high, vl) + dot(low, vh)
    return jnp.concatenate([out[:rows, :128], out[:rows, 128:]], axis=0)


def sine_z(planes, sine, keep):
    even = [planes[k] + planes[9 - k] for k in range(5)]
    odd = [planes[k] - planes[9 - k] for k in range(5)]
    out = []
    for j in keep:
        terms = [float(sine[j, k]) * (odd if j % 2 else even)[k] for k in range(5)]
        out.append(functools.reduce(lambda a, b: a + b, terms))
    return out


def along_z(v, table):
    planes = [v[32 * i : 32 * i + 32] for i in range(8)]
    even = [planes[j] + planes[7 - j] for j in range(4)]
    odd = [planes[j] - planes[7 - j] for j in range(4)]
    low, high = [], []
    for i in range(4):
        a = b = None
        for j in range(4):
            p = float(table[i, j] + table[i, 7 - j]) / 2.0 * even[j]
            q = float(table[i, j] - table[i, 7 - j]) / 2.0 * odd[j]
            a, b = (p, q) if a is None else (a + p, b + q)
        low.append(a + b)
        high.insert(0, b - a)
    return jnp.concatenate(low + high, axis=0)


def total(v):
    return jnp.sum(jnp.sum(v, axis=0, keepdims=True), axis=1, keepdims=True)


def sweep_step(a, row, col, k, sub, lane):
    pivot = jnp.sum(jnp.where(lane[:1] == k, row, 0.0), axis=1, keepdims=True)
    row_m = jnp.where(lane[:1] == k, -1.0, row) / pivot
    col_m = jnp.where(sub == k, -1.0, col)
    return jnp.where(jnp.logical_or(lane == k, sub == k), 0.0, a) - col_m * row_m


def kernel(
    ngx, ngy, deriv, sine,
    level_hbm, vel_hbm, source_hbm, solid_hbm, *refs
):
    tables_hbm, refs = refs[:3], refs[3:]
    level_out, pressure_out = refs[:2]
    (
        flux_ref, invm_ref, part_ref, lev_ref, app_ref, res_ref, search_ref, ext_ref, a_ref,
        zs, zr, ys, yr, cs, cr, gbuf0, gbuf1, gbuf2,
        level_ref, vel_ref, source_ref, solid_ref,
        table, mass_ref, den_ref,
        send_sem, recv_sem, gsend_sem, grecv_sem, load_sem,
    ) = refs[2:]
    first, later = pl.ds(0, T_SX), pl.ds(T_SX, T_END - T_SX)
    pairs = (
        (level_hbm, level_ref),
        (vel_hbm, vel_ref),
        (source_hbm, source_ref),
        (solid_hbm, solid_ref),
        (tables_hbm[0].at[first], table.at[first]),
        (tables_hbm[1], mass_ref),
        (tables_hbm[2], den_ref),
        (tables_hbm[0].at[later], table.at[later]),
    )
    loads = [
        pltpu.make_async_copy(src, dst, load_sem.at[i]) for i, (src, dst) in enumerate(pairs)
    ]
    for i in (0, 4, 1, 5, 2, 3, 7, 6):
        loads[i].start()
    gbufs = (gbuf0, gbuf1, gbuf2)
    n = ngx * ngy
    ix = lax.axis_index("gx")
    iy = lax.axis_index("gy")
    me = ix * ngy + iy

    def other(i):
        at = me + i
        return jnp.where(at >= n, at - n, at)

    zr[...] = jnp.zeros_like(zr)
    yr[...] = jnp.zeros_like(yr)
    cr[...] = jnp.zeros_like(cr)
    ext_ref[...] = jnp.zeros_like(ext_ref)

    barrier = pltpu.get_barrier_semaphore()

    def greet(i, carry):
        pl.semaphore_signal(barrier, inc=1, device_id=other(i), device_id_type=LOGICAL)
        return carry

    lax.fori_loop(1, n, greet, 0, unroll=n <= 64)

    has_zlo, has_zhi = ix > 0, ix < ngx - 1
    has_ylo, has_yhi = iy > 0, iy < ngy - 1

    def exists(d):
        dz, dy = SIDES[d]
        conds = []
        if dz:
            conds.append(has_zlo if dz < 0 else has_zhi)
        if dy:
            conds.append(has_ylo if dy < 0 else has_yhi)
        return conds[0] if len(conds) == 1 else jnp.logical_and(*conds)

    def buffers(r, d, layers):
        if d < 2:
            return zs.at[r, d, pl.ds(0, 32 * layers)], zr.at[r, OPPOSITE[d], pl.ds(0, 32 * layers)]
        if d < 4:
            return (
                ys.at[r, d - 2, pl.ds(0, 8 * layers)],
                yr.at[r, OPPOSITE[d] - 2, pl.ds(0, 8 * layers)],
            )
        return cs.at[r, d - 4], cr.at[r, OPPOSITE[d] - 4]

    def halo_copy(r, d, layers):
        src, dst = buffers(r, d, layers)
        dz, dy = SIDES[d]
        return pltpu.make_async_remote_copy(
            src_ref=src,
            dst_ref=dst,
            send_sem=send_sem.at[r, d],
            recv_sem=recv_sem.at[r, OPPOSITE[d]],
            device_id=(ix + dz, iy + dy),
            device_id_type=MESH,
        )

    def halo_send(r, layers, second=None):
        for s in range(2):
            zo, zi = ((0, 32), (224, 192))[s]
            zs[r, s, 0:32] = part_ref[zo : zo + 32]
            yo, yi = ((0, 1), (31, 30))[s]
            ys[r, s, 0:8] = part_ref[pl.ds(yo, 8, stride=32), :]
            if layers > 1:
                zs[r, s, 32:64] = part_ref[zi : zi + 32]
                ys[r, s, 8:16] = part_ref[pl.ds(yi, 8, stride=32), :]
            if second is not None:
                zs[r, s, 64:96] = second[zo : zo + 32]
                ys[r, s, 16:24] = second[pl.ds(yo, 8, stride=32), :]
        for c in range(4):
            dz, dy = SIDES[4 + c]
            zo, zi = (0, 32) if dz < 0 else (224, 192)
            yo, yi = (0, 1) if dy < 0 else (31, 30)
            cs[r, c, 0:1] = part_ref[zo + yo : zo + yo + 1]
            if layers > 1:
                cs[r, c, 1:2] = part_ref[zo + yi : zo + yi + 1]
                cs[r, c, 2:3] = part_ref[zi + yo : zi + yo + 1]
                cs[r, c, 3:4] = part_ref[zi + yi : zi + yi + 1]
            if second is not None:
                cs[r, c, 4:5] = second[zo + yo : zo + yo + 1]
        for d in range(8):

            @pl.when(exists(d))
            def _():
                halo_copy(r, d, layers).start()

    def halo_wait(r, layers):
        for d in range(8):

            @pl.when(exists(d))
            def _():
                src, _ = buffers(r, d, layers)
                _, dst = buffers(r, OPPOSITE[d], layers)
                dz, dy = SIDES[d]
                pltpu.make_async_remote_copy(
                    src_ref=src,
                    dst_ref=dst,
                    send_sem=send_sem.at[r, d],
                    recv_sem=recv_sem.at[r, d],
                    device_id=(ix + dz, iy + dy),
                    device_id_type=MESH,
                ).wait_recv()

    def halo_drain(r, layers):
        for d in range(8):

            @pl.when(exists(d))
            def _():
                halo_copy(r, d, layers).wait_send()

    def add_rim(r, ref, zoff, yoff, crow):
        ref[0:32] = ref[0:32] + zr[r, 0, zoff : zoff + 32]
        ref[224:256] = ref[224:256] + zr[r, 1, zoff : zoff + 32]
        for s, yo in ((0, 0), (1, 31)):
            at = pl.ds(yo, 8, stride=32)
            ref[at, :] = ref[at, :] + yr[r, s, yoff : yoff + 8]
        for c, row in enumerate((0, 31, 224, 255)):
            ref[row : row + 1] = ref[row : row + 1] + cr[r, c, crow : crow + 1]

    def outer_halo(r):
        for s in range(2):
            base = 9 * PLANE * s
            ext_ref[base : base + 32] = zr[r, s, 32:64]
            ext_ref[base : base + 1] = ext_ref[base : base + 1] + cr[r, 2 * s, 2:3]
            at = base + 31
            ext_ref[at : at + 1] = ext_ref[at : at + 1] + cr[r, 2 * s + 1, 2:3]
            ext_ref[pl.ds(PLANE + 32 + s, 8, stride=PLANE), :] = yr[r, s, 8:16]
            for at, c in ((PLANE + 32 + s, s), (8 * PLANE + 32 + s, 2 + s)):
                ext_ref[at : at + 1] = ext_ref[at : at + 1] + cr[r, c, 1:2]
        for c in range(4):
            at = 9 * PLANE * (c // 2) + 32 + c % 2
            ext_ref[at : at + 1] = cr[r, c, 3:4]

    def gather_copy(g, dst):
        ref = gbufs[g].at[me]
        return pltpu.make_async_remote_copy(
            src_ref=ref,
            dst_ref=ref,
            send_sem=gsend_sem.at[g],
            recv_sem=grecv_sem.at[g],
            device_id=dst,
            device_id_type=LOGICAL,
        )

    def gather_send(g, rows):
        for k, value in enumerate(rows):
            gbufs[g][me, k : k + 1] = jnp.broadcast_to(value, (1, 128))

        def send(i, carry):
            gather_copy(g, other(i)).start()
            return carry

        lax.fori_loop(1, n, send, 0, unroll=n <= 64)

    def gather_bytes(g, sem):
        ref = gbufs[g].at[pl.ds(0, n - 1)]
        pltpu.make_async_copy(ref, ref, sem).wait()

    def gather_wait(g):
        gather_bytes(g, grecv_sem.at[g])

    row = lax.broadcasted_iota(jnp.int32, (ROWS, 128), 0)
    lane = lax.broadcasted_iota(jnp.int32, (ROWS, 128), 1)
    zpos, ypos = row // 32, row % 32
    y8, x8 = row % 8, lane % 8
    y_first = jnp.logical_and(y8 == 0, ypos > 0).astype(F32)
    y_last = jnp.logical_and(y8 == 7, ypos < 31).astype(F32)
    x_first = jnp.logical_and(x8 == 0, lane > 0).astype(F32)
    x_last = jnp.logical_and(x8 == 7, lane < 127).astype(F32)

    def flag(c):
        return c.astype(jnp.int32).astype(F32)

    zlo_f, zhi_f, ylo_f, yhi_f = flag(has_zlo), flag(has_zhi), flag(has_ylo), flag(has_yhi)
    z0, z7 = (zpos == 0).astype(F32), (zpos == 7).astype(F32)
    yb0, yb31 = (ypos == 0).astype(F32), (ypos == 31).astype(F32)
    half_zlo, half_zhi = 0.5 * zlo_f * z0, 0.5 * zhi_f * z7
    half_ylo, half_yhi = 0.5 * ylo_f * yb0, 0.5 * yhi_f * yb31
    own_z, own_y = 1.0 - half_zlo - half_zhi, 1.0 - half_ylo - half_yhi
    inv_m = (
        own_z
        * (own_y - 0.5 * (y_first + y_last))
        * (1.0 - 0.5 * (x_first + x_last))
    )
    invm_ref[...] = inv_m

    def fold_in(v):
        v = v + x_first * pltpu.roll(v, 1, 1) + x_last * pltpu.roll(v, 127, 1)
        return v + y_first * pltpu.roll(v, 1, 0) + y_last * pltpu.roll(v, ROWS - 1, 0)

    for i in (4, 0, 1, 5):
        loads[i].wait()
    mass = mass_ref[0:ROWS]
    level = level_ref[...]
    advect = (
        vel_ref[0:ROWS] * along_z(level, deriv)
        + vel_ref[ROWS : 2 * ROWS] * along_y(level, table, T_DY)
        + vel_ref[2 * ROWS : 3 * ROWS] * along_x(level, table, T_DXT)
    )
    lev_ref[...] = fold_in(mass * (level - (2.0 * TIME_STEP) * advect))
    diverge = (
        along_z(vel_ref[0:ROWS], deriv)
        + along_y(vel_ref[ROWS : 2 * ROWS], table, T_DY)
        + along_x(vel_ref[2 * ROWS : 3 * ROWS], table, T_DXT)
    )
    loads[2].wait()
    part_ref[...] = fold_in(mass * (source_ref[...] - (2.0 * TIME_STEP) * diverge))

    pl.semaphore_wait(barrier, n - 1)
    halo_send(0, 3, lev_ref)
    res_ref[...] = part_ref[...]
    loads[3].wait()
    solid = dot(solid_ref[0].astype(F32), mass_ref[ROWS : ROWS + EX])
    solid = jnp.concatenate(
        [jnp.broadcast_to(solid[e : e + 1], (8, 128)) for e in range(EY)], axis=0
    )
    solid = jnp.concatenate([solid] * 8, axis=0)
    halo_wait(0, 3)
    add_rim(0, res_ref, 0, 0, 0)
    add_rim(0, lev_ref, 64, 16, 4)
    outer_halo(0)
    level_new = lev_ref[...] * inv_m / mass
    level_out[...] = level_new
    coef = (GAS_RATIO - (GAS_RATIO - 1.0) * jax.nn.sigmoid(level_new / LEVEL_WIDTH)) * (
        1.0 - (1.0 - SOLID_FACTOR) * solid
    )
    flux_ref[...] = 4.0 * coef * mass
    gather_send(0, (total(coef) / (ROWS * 128.0), total(res_ref[...] * inv_m)))

    def local_solve(v):
        for z in range(8):
            ext_ref[PLANE * (z + 1) : PLANE * (z + 1) + 32] = v[32 * z : 32 * z + 32]
        planes = [ext_ref[PLANE * z : PLANE * z + PLANE] for z in range(10)]
        wide = jnp.concatenate(sine_z(planes, sine, range(10)), axis=0)
        wide = planes_y(wide, table, T_SY, 200, 208)
        wh, wl = split(wide)
        spectral = dot(jnp.concatenate([wh, wl], axis=1), table[T_SX : T_SX + 256, :])
        spectral = spectral + dot(wh, table[T_SX + 256 : T_SX + 384, :])
        sh, sl = split(spectral * den_ref[...])
        back = dot(sh, table[T_BX : T_BX + 256, :])
        back = back[:, :128] + back[:, 128:] + dot(sl, table[T_BX : T_BX + 256, :128])
        back = planes_y(back, table, T_BY, 160, 160)
        planes = [back[32 * z : 32 * z + 32] for z in range(10)]
        return jnp.concatenate(sine_z(planes, sine, range(1, 9)), axis=0)

    def helm(v):
        flux = flux_ref[...]
        out = along_z(flux * along_z(v, deriv), deriv.T)
        out = out + along_y(flux * along_y(v, table, T_DY), table, T_DYT)
        out = out + along_x(flux * along_x(v, table, T_DXT), table, T_DX)
        return out + HELM_COEF * mass_ref[0:ROWS] * v

    npad = a_ref.shape[1]
    sub_n = lax.broadcasted_iota(jnp.int32, (n, npad), 0)
    lane_n = lax.broadcasted_iota(jnp.int32, (n, npad), 1)

    def gathered(g, item):
        got = gbufs[g][:, item, :]
        return got if npad == 128 else jnp.concatenate([got] * (npad // 128), axis=1)

    def invert(k_col):
        diag = lane_n == sub_n
        k_row = jnp.sum(jnp.where(diag, k_col, 0.0), axis=0, keepdims=True)
        gap = lane_n - sub_n
        same = lane_n // ngy == sub_n // ngy
        y_link = jnp.logical_and(jnp.logical_or(gap == 1, gap == -1), same)
        z_link = jnp.logical_or(gap == ngy, gap == -ngy)
        rate = jnp.where(z_link, float(EY * EX) / EZ, 0.0) + jnp.where(
            y_link, float(EZ * EX) / EY, 0.0
        )
        rate = jnp.where(lane_n < n, rate, 0.0)
        link = 2.0 * k_col * k_row / (k_col + k_row) * rate
        diagonal = HELM_COEF * EZ * EY * EX + jnp.sum(link, axis=1, keepdims=True)
        a = jnp.where(diag, diagonal, -link)
        if ngx == 2 and n <= 64:
            left_over = list(range(ngy))
            while left_over:
                now = left_over[1::2] or left_over
                left_over = left_over[0::2] if len(left_over) > 1 else []
                cross = jnp.zeros((n, npad), jnp.bool_)
                change = None
                for j in now:
                    k, m = j, ngy + j
                    c1 = jnp.broadcast_to(a[:, k : k + 1], (n, npad))
                    c2 = jnp.broadcast_to(a[:, m : m + 1], (n, npad))
                    p11, p12, p22 = c1[k : k + 1], c2[k : k + 1], c2[m : m + 1]
                    scale = 1.0 / (p11 * p22 - p12 * p12)
                    at1, at2 = lane_n == k, lane_n == m
                    on1, on2 = sub_n == k, sub_n == m
                    r1 = jnp.where(at1[:1], -1.0, jnp.where(at2[:1], 0.0, a[k : k + 1]))
                    r2 = jnp.where(at2[:1], -1.0, jnp.where(at1[:1], 0.0, a[m : m + 1]))
                    q1 = (p22 * r1 - p12 * r2) * scale
                    q2 = (p11 * r2 - p12 * r1) * scale
                    c1 = jnp.where(on1, -1.0, jnp.where(on2, 0.0, c1))
                    c2 = jnp.where(on2, -1.0, jnp.where(on1, 0.0, c2))
                    cross = cross | at1 | at2 | on1 | on2
                    term = c1 * q1 + c2 * q2
                    change = term if change is None else change + term
                a = jnp.where(cross, 0.0, a) - change
            a_ref[...] = a
        else:
            a_ref[...] = a

            def step(k, carry):
                a = a_ref[...]
                row = a_ref[pl.ds(k, 1), :]
                col = jnp.sum(jnp.where(lane_n == k, a, 0.0), axis=1, keepdims=True)
                a_ref[...] = sweep_step(a, row, col, k, sub_n, lane_n)
                return carry

            lax.fori_loop(0, n, step, 0)

    def coarse(t_col):
        return -jnp.sum(a_ref[...] * t_col, axis=0, keepdims=True)

    def coarse_field(x):
        def value(dz, dy):
            at = me + dz * ngy + dy
            return jnp.sum(jnp.where(lane_n[:1] == at, x, 0.0), axis=1, keepdims=True)

        def along_y(dz):
            return own_y * value(dz, 0) + half_ylo * value(dz, -1) + half_yhi * value(dz, 1)

        return own_z * along_y(0) + half_zlo * along_y(-1) + half_zhi * along_y(1)

    def rows_sum(v):
        return jnp.sum(v, axis=0, keepdims=True)

    loads[6].wait()
    loads[7].wait()
    part_ref[...] = fold_in(local_solve(res_ref[...]) * inv_m)
    halo_send(1, 1)
    gather_wait(0)
    invert(gathered(0, 0))
    field = coarse_field(coarse(gathered(0, 1)))
    halo_wait(1, 1)
    search_ref[...] = part_ref[...]
    add_rim(1, search_ref, 0, 0, 0)
    z1 = search_ref[...] + field
    search_ref[...] = z1

    applied = helm(z1)
    part_ref[...] = fold_in(applied)
    halo_send(2, 2)
    sum_rz = rows_sum(res_ref[...] * z1 * inv_m)
    sum_za = rows_sum(z1 * applied)
    app_ref[...] = part_ref[...]
    halo_wait(2, 2)
    add_rim(2, app_ref, 0, 0, 0)
    outer_halo(2)
    gather_send(1, (total(app_ref[...] * invm_ref[...]),))

    part_ref[...] = fold_in(local_solve(app_ref[...]) * invm_ref[...])
    halo_send(3, 1)
    gather_wait(1)
    field = coarse_field(coarse(gathered(1, 0)))
    halo_wait(3, 1)
    add_rim(3, part_ref, 0, 0, 0)
    q = part_ref[...] + field

    q_m = q * invm_ref[...]
    gz, gy, gx = along_z(q, deriv), along_y(q, table, T_DY), along_x(q, table, T_DXT)
    energy = flux_ref[...] * (gz * gz + gy * gy + gx * gx)
    energy = energy + HELM_COEF * mass_ref[0:ROWS] * (q * q)
    sum_rq = rows_sum(res_ref[...] * q_m)
    sum_aq = rows_sum(app_ref[...] * q_m)
    gather_send(2, (sum_rz, sum_za, sum_rq, sum_aq, rows_sum(energy), 0.0, 0.0, 0.0))
    for r, layers in enumerate((3, 1, 2, 1)):
        halo_drain(r, layers)
    for g in range(2):
        gather_bytes(g, gsend_sem.at[g])
    gather_wait(2)
    sums = jnp.sum(jnp.sum(gbuf2[...], axis=0), axis=1, keepdims=True)
    rz, za, rq, aq, qq = (sums[k : k + 1] for k in range(5))

    step1 = rz / za
    rz_next = step1 * (step1 * aq - rq)
    beta1 = 1.0 + rz_next / rz
    norm2 = beta1 * beta1 * za - 2.0 * beta1 * step1 * aq + step1 * step1 * qq
    step2 = rz_next / norm2
    pressure_out[...] = (step1 + step2 * beta1) * search_ref[...] - (step2 * step1) * q

    gather_bytes(2, gsend_sem.at[2])


def body(ngx, ngy, level_set, velocity, source, wick_solid):
    n = ngx * ngy
    npad = -(-n // 128) * 128
    consts = [jnp.asarray(t) for t in tables()]
    hbm = pl.BlockSpec(memory_space=pltpu.HBM)
    vmem = pl.BlockSpec(memory_space=pltpu.VMEM)
    shape = level_set.shape
    level_new, pressure = pl.pallas_call(
        functools.partial(kernel, ngx, ngy, gll_tables()[1], sine_table()),
        out_shape=[jax.ShapeDtypeStruct((ROWS, 128), F32)] * 2,
        in_specs=[hbm] * (4 + len(consts)),
        out_specs=[vmem] * 2,
        scratch_shapes=[
            pltpu.VMEM((ROWS, 128), F32),
            pltpu.VMEM((ROWS, 128), F32),
            pltpu.VMEM((ROWS, 128), F32),
            pltpu.VMEM((ROWS, 128), F32),
            pltpu.VMEM((ROWS, 128), F32),
            pltpu.VMEM((ROWS, 128), F32),
            pltpu.VMEM((ROWS, 128), F32),
            pltpu.VMEM((SPEC, 128), F32),
            pltpu.VMEM((n, npad), F32),
            pltpu.VMEM((4, 2, 96, 128), F32),
            pltpu.VMEM((4, 2, 96, 128), F32),
            pltpu.VMEM((4, 2, 24, 128), F32),
            pltpu.VMEM((4, 2, 24, 128), F32),
            pltpu.VMEM((4, 4, 8, 128), F32),
            pltpu.VMEM((4, 4, 8, 128), F32),
            pltpu.VMEM((n, 2, 128), F32),
            pltpu.VMEM((n, 1, 128), F32),
            pltpu.VMEM((n, 8, 128), F32),
            pltpu.VMEM((ROWS, 128), F32),
            pltpu.VMEM((3 * ROWS, 128), F32),
            pltpu.VMEM((ROWS, 128), F32),
            pltpu.VMEM((1, EY, EX), jnp.int32),
            *[pltpu.VMEM(t.shape, t.dtype) for t in consts],
            pltpu.SemaphoreType.DMA((4, 8)),
            pltpu.SemaphoreType.DMA((4, 8)),
            pltpu.SemaphoreType.DMA((3,)),
            pltpu.SemaphoreType.DMA((3,)),
            pltpu.SemaphoreType.DMA((8,)),
        ],
        compiler_params=pltpu.CompilerParams(
            collective_id=0, has_side_effects=True, vmem_limit_bytes=54848 * 1024
        ),
    )(
        level_set.reshape(ROWS, 128),
        velocity.reshape(3 * ROWS, 128),
        source.reshape(ROWS, 128),
        wick_solid,
        *consts,
    )
    return level_new.reshape(shape), pressure.reshape(shape)


def solution(mesh):
    placed = (
        P("gx", "gy", None),
        P(None, "gx", "gy", None),
        P("gx", "gy", None),
        P("gx", "gy", None),
    )
    return jax.shard_map(
        functools.partial(body, mesh.shape["gx"], mesh.shape["gy"]),
        mesh=mesh,
        in_specs=placed,
        out_specs=(P("gx", "gy", None), P("gx", "gy", None)),
        check_vma=False,
    )
```

```python
import functools

import jax
import jax.numpy as jnp
import ml_dtypes
import numpy as np
from jax import lax
from jax.experimental import pallas as pl
from jax.experimental.pallas import tpu as pltpu
from jax.sharding import PartitionSpec as P

EZ = 1
EY = 4
EX = 16
ROWS = 256
PLANE = 40
SPEC = 400
T_DY, T_DYT, T_DXT, T_DX, T_SX, T_BX = 0, 128, 256, 512, 768, 1152
T_SY, T_BY, T_END = 1408, 1824, 2144

TIME_STEP = 0.02
HELM_COEF = 0.25
LEVEL_WIDTH = 0.25
GAS_RATIO = 10.0
SOLID_FACTOR = 0.25
SCHWARZ_SCALE = 0.5
SCHWARZ_SHIFT = 0.05

MESH = pl.DeviceIdType.MESH
LOGICAL = pl.DeviceIdType.LOGICAL
F32 = jnp.float32
BF16 = jnp.bfloat16

SIDES = ((-1, 0), (1, 0), (0, -1), (0, 1), (-1, -1), (-1, 1), (1, -1), (1, 1))
OPPOSITE = tuple(SIDES.index((-dz, -dy)) for dz, dy in SIDES)


def gll_tables():
    nodes = np.array(
        [
            -1.0,
            -0.8717401485096066,
            -0.5917001814331423,
            -0.2092992179024789,
            0.2092992179024789,
            0.5917001814331423,
            0.8717401485096066,
            1.0,
        ]
    )
    weight = np.array(
        [
            1.0 / 28.0,
            0.21070422714350603,
            0.3411226924835044,
            0.4124587946587038,
            0.4124587946587038,
            0.3411226924835044,
            0.21070422714350603,
            1.0 / 28.0,
        ]
    )
    bary = np.array(
        [1.0 / np.prod([nodes[i] - nodes[j] for j in range(8) if j != i]) for i in range(8)]
    )
    deriv = np.zeros((8, 8))
    for i in range(8):
        for j in range(8):
            if i != j:
                deriv[i, j] = bary[j] / bary[i] / (nodes[i] - nodes[j])
        deriv[i, i] = -np.sum(deriv[i])
    return weight, deriv


def halves(table):
    table = np.asarray(table, np.float32)
    high = table.astype(ml_dtypes.bfloat16)
    low = (table - high.astype(np.float32)).astype(ml_dtypes.bfloat16)
    return high, low


def tables():
    weight, deriv = gll_tables()
    ids = np.arange(10) + 1.0
    sine = sine_table()
    eig = 2.0 - 2.0 * np.cos(np.pi * ids / 11.0)
    dy = np.kron(np.eye(16), deriv)
    dx_t = np.kron(np.eye(EX), deriv.T)
    dx = np.kron(np.eye(EX), deriv)

    widen_y = np.zeros((PLANE, PLANE))
    for e in range(EY):
        for yi in range(10):
            y = 8 * e - 2 if yi == 0 else (8 * e + 9 if yi == 9 else 8 * e + yi - 1)
            widen_y[e * 10 + yi, 32 if y < 0 else (33 if y > 31 else y)] = 1.0
    spec_y = np.kron(np.eye(5), np.kron(np.eye(EY), sine) @ widen_y)
    widen_x = np.zeros((160, 128))
    for e in range(EX):
        for xi in range(10):
            x = 8 * e - 2 if xi == 0 else (8 * e + 9 if xi == 9 else 8 * e + xi - 1)
            if 0 <= x < 128:
                widen_x[e * 10 + xi, x] = 1.0
    spec_x = np.zeros((128, 256))
    spec_x[:, :160] = (np.kron(np.eye(EX), sine) @ widen_x).T
    back_y = np.kron(np.eye(5), np.kron(np.eye(EY), sine[1:9]))
    back_x = np.zeros((256, 128))
    back_x[:160] = np.kron(np.eye(EX), sine[1:9]).T
    lam_zy = (eig[:, None] + np.tile(eig, EY)[None, :]).reshape(SPEC)
    inv_den = np.zeros((SPEC, 256))
    inv_den[:, :160] = 1.0 / (
        SCHWARZ_SCALE * (lam_zy[:, None] + np.tile(eig, EX)[None, :]) + SCHWARZ_SHIFT
    )
    mass = 0.125 * (
        np.kron(weight, np.tile(weight, EY))[:, None] * np.tile(weight, EX)[None, :]
    )
    spread = np.zeros((16, 128))
    spread[:EX] = np.kron(np.eye(EX), np.ones((1, 8)))

    def beside(table):
        high, low = halves(table)
        return np.concatenate([high, low], axis=1)

    def both(table):
        high, low = halves(table)
        zero = np.zeros_like(low)
        return np.concatenate(
            [np.concatenate([high, low], axis=1), np.concatenate([high, zero], axis=1)], axis=0
        )

    def under(table):
        high, low = halves(table)
        return np.concatenate([high, high, low], axis=0)

    def padded(table, rows, cols):
        out = np.zeros((rows, cols))
        out[: table.shape[0], : table.shape[1]] = table
        return out

    return (
        np.concatenate(
            [
                beside(dy), beside(dy.T), both(dx_t), both(dx), under(spec_x), beside(back_x),
                *halves(padded(spec_y, 208, 256)), *halves(padded(back_y, 160, 256)),
            ],
            axis=0,
        ),
        np.concatenate([mass, spread], axis=0).astype(np.float32),
        inv_den.astype(np.float32),
    )


def sine_table():
    ids = np.arange(10) + 1.0
    return np.sqrt(2.0 / 11.0) * np.sin(np.pi * np.outer(ids, ids) / 11.0)


def split(v):
    high = v.astype(BF16)
    low = (v - high.astype(F32)).astype(BF16)
    return high, low


def dot(a, b):
    return jnp.dot(a, b, preferred_element_type=F32)


def along_y(v, ref, base):
    vh, vl = split(jnp.concatenate([v[:128], v[128:]], axis=1))
    table = ref[base : base + 128, :]
    out = dot(table, jnp.concatenate([vh, vh], axis=0)) + dot(table[:, :128], vl)
    return jnp.concatenate([out[:, :128], out[:, 128:]], axis=0)


def along_x(v, ref, base):
    vh, vl = split(v)
    out = dot(jnp.concatenate([vh, vl], axis=1), ref[base : base + 256, :])
    return out[:, :128] + out[:, 128:]


def planes_y(v, ref, base, rows, pad):
    vh, vl = split(jnp.concatenate([v[:200], v[200:]], axis=1))
    high = ref[base : base + pad, :200]
    low = ref[base + pad : base + 2 * pad, :200]
    out = dot(high, vh) + dot(high, vl) + dot(low, vh)
    return jnp.concatenate([out[:rows, :128], out[:rows, 128:]], axis=0)


def sine_z(planes, sine, keep):
    even = [planes[k] + planes[9 - k] for k in range(5)]
    odd = [planes[k] - planes[9 - k] for k in range(5)]
    out = []
    for j in keep:
        terms = [float(sine[j, k]) * (odd if j % 2 else even)[k] for k in range(5)]
        out.append(functools.reduce(lambda a, b: a + b, terms))
    return out


def along_z(v, table):
    planes = [v[32 * i : 32 * i + 32] for i in range(8)]
    even = [planes[j] + planes[7 - j] for j in range(4)]
    odd = [planes[j] - planes[7 - j] for j in range(4)]
    low, high = [], []
    for i in range(4):
        a = b = None
        for j in range(4):
            p = float(table[i, j] + table[i, 7 - j]) / 2.0 * even[j]
            q = float(table[i, j] - table[i, 7 - j]) / 2.0 * odd[j]
            a, b = (p, q) if a is None else (a + p, b + q)
        low.append(a + b)
        high.insert(0, b - a)
    return jnp.concatenate(low + high, axis=0)


def total(v):
    return jnp.sum(jnp.sum(v, axis=0, keepdims=True), axis=1, keepdims=True)


def sweep_step(a, row, col, k, sub, lane):
    pivot = jnp.sum(jnp.where(lane[:1] == k, row, 0.0), axis=1, keepdims=True)
    row_m = jnp.where(lane[:1] == k, -1.0, row) / pivot
    col_m = jnp.where(sub == k, -1.0, col)
    return jnp.where(jnp.logical_or(lane == k, sub == k), 0.0, a) - col_m * row_m


def kernel(
    ngx, ngy, deriv, sine,
    level_hbm, vel_hbm, source_hbm, solid_hbm, *refs
):
    tables_hbm, refs = refs[:3], refs[3:]
    level_out, pressure_out = refs[:2]
    (
        flux_ref, invm_ref, part_ref, lev_ref, app_ref, res_ref, search_ref, ext_ref, a_ref,
        zs, zr, ys, yr, cs, cr, gbuf0, gbuf1, gbuf2,
        level_ref, vel_ref, source_ref, solid_ref,
        table, mass_ref, den_ref,
        send_sem, recv_sem, gsend_sem, grecv_sem, load_sem,
    ) = refs[2:]
    first, later = pl.ds(0, T_SX), pl.ds(T_SX, T_END - T_SX)
    pairs = (
        (level_hbm, level_ref),
        (vel_hbm, vel_ref),
        (source_hbm, source_ref),
        (solid_hbm, solid_ref),
        (tables_hbm[0].at[first], table.at[first]),
        (tables_hbm[1], mass_ref),
        (tables_hbm[2], den_ref),
        (tables_hbm[0].at[later], table.at[later]),
    )
    loads = [
        pltpu.make_async_copy(src, dst, load_sem.at[i]) for i, (src, dst) in enumerate(pairs)
    ]
    for i in (0, 4, 1, 5, 2, 3, 7, 6):
        loads[i].start()
    gbufs = (gbuf0, gbuf1, gbuf2)
    n = ngx * ngy
    ix = lax.axis_index("gx")
    iy = lax.axis_index("gy")
    me = ix * ngy + iy

    def other(i):
        at = me + i
        return jnp.where(at >= n, at - n, at)

    zr[...] = jnp.zeros_like(zr)
    yr[...] = jnp.zeros_like(yr)
    cr[...] = jnp.zeros_like(cr)
    ext_ref[...] = jnp.zeros_like(ext_ref)

    barrier = pltpu.get_barrier_semaphore()

    def greet(i, carry):
        pl.semaphore_signal(barrier, inc=1, device_id=other(i), device_id_type=LOGICAL)
        return carry

    lax.fori_loop(1, n, greet, 0, unroll=n <= 64)

    has_zlo, has_zhi = ix > 0, ix < ngx - 1
    has_ylo, has_yhi = iy > 0, iy < ngy - 1

    def exists(d):
        dz, dy = SIDES[d]
        conds = []
        if dz:
            conds.append(has_zlo if dz < 0 else has_zhi)
        if dy:
            conds.append(has_ylo if dy < 0 else has_yhi)
        return conds[0] if len(conds) == 1 else jnp.logical_and(*conds)

    def buffers(r, d, layers):
        if d < 2:
            return zs.at[r, d, pl.ds(0, 32 * layers)], zr.at[r, OPPOSITE[d], pl.ds(0, 32 * layers)]
        if d < 4:
            return (
                ys.at[r, d - 2, pl.ds(0, 8 * layers)],
                yr.at[r, OPPOSITE[d] - 2, pl.ds(0, 8 * layers)],
            )
        return cs.at[r, d - 4], cr.at[r, OPPOSITE[d] - 4]

    def halo_copy(r, d, layers):
        src, dst = buffers(r, d, layers)
        dz, dy = SIDES[d]
        return pltpu.make_async_remote_copy(
            src_ref=src,
            dst_ref=dst,
            send_sem=send_sem.at[r, d],
            recv_sem=recv_sem.at[r, OPPOSITE[d]],
            device_id=(ix + dz, iy + dy),
            device_id_type=MESH,
        )

    def halo_send(r, layers, second=None):
        for s in range(2):
            zo, zi = ((0, 32), (224, 192))[s]
            zs[r, s, 0:32] = part_ref[zo : zo + 32]
            yo, yi = ((0, 1), (31, 30))[s]
            ys[r, s, 0:8] = part_ref[pl.ds(yo, 8, stride=32), :]
            if layers > 1:
                zs[r, s, 32:64] = part_ref[zi : zi + 32]
                ys[r, s, 8:16] = part_ref[pl.ds(yi, 8, stride=32), :]
            if second is not None:
                zs[r, s, 64:96] = second[zo : zo + 32]
                ys[r, s, 16:24] = second[pl.ds(yo, 8, stride=32), :]
        for c in range(4):
            dz, dy = SIDES[4 + c]
            zo, zi = (0, 32) if dz < 0 else (224, 192)
            yo, yi = (0, 1) if dy < 0 else (31, 30)
            cs[r, c, 0:1] = part_ref[zo + yo : zo + yo + 1]
            if layers > 1:
                cs[r, c, 1:2] = part_ref[zo + yi : zo + yi + 1]
                cs[r, c, 2:3] = part_ref[zi + yo : zi + yo + 1]
                cs[r, c, 3:4] = part_ref[zi + yi : zi + yi + 1]
            if second is not None:
                cs[r, c, 4:5] = second[zo + yo : zo + yo + 1]
        for d in range(8):

            @pl.when(exists(d))
            def _():
                halo_copy(r, d, layers).start()

    def halo_wait(r, layers):
        for d in range(8):

            @pl.when(exists(d))
            def _():
                src, _ = buffers(r, d, layers)
                _, dst = buffers(r, OPPOSITE[d], layers)
                dz, dy = SIDES[d]
                pltpu.make_async_remote_copy(
                    src_ref=src,
                    dst_ref=dst,
                    send_sem=send_sem.at[r, d],
                    recv_sem=recv_sem.at[r, d],
                    device_id=(ix + dz, iy + dy),
                    device_id_type=MESH,
                ).wait_recv()

    def halo_drain(r, layers):
        for d in range(8):

            @pl.when(exists(d))
            def _():
                halo_copy(r, d, layers).wait_send()

    def add_rim(r, ref, zoff, yoff, crow):
        ref[0:32] = ref[0:32] + zr[r, 0, zoff : zoff + 32]
        ref[224:256] = ref[224:256] + zr[r, 1, zoff : zoff + 32]
        for s, yo in ((0, 0), (1, 31)):
            at = pl.ds(yo, 8, stride=32)
            ref[at, :] = ref[at, :] + yr[r, s, yoff : yoff + 8]
        for c, row in enumerate((0, 31, 224, 255)):
            ref[row : row + 1] = ref[row : row + 1] + cr[r, c, crow : crow + 1]

    def outer_halo(r):
        for s in range(2):
            base = 9 * PLANE * s
            ext_ref[base : base + 32] = zr[r, s, 32:64]
            ext_ref[base : base + 1] = ext_ref[base : base + 1] + cr[r, 2 * s, 2:3]
            at = base + 31
            ext_ref[at : at + 1] = ext_ref[at : at + 1] + cr[r, 2 * s + 1, 2:3]
            ext_ref[pl.ds(PLANE + 32 + s, 8, stride=PLANE), :] = yr[r, s, 8:16]
            for at, c in ((PLANE + 32 + s, s), (8 * PLANE + 32 + s, 2 + s)):
                ext_ref[at : at + 1] = ext_ref[at : at + 1] + cr[r, c, 1:2]
        for c in range(4):
            at = 9 * PLANE * (c // 2) + 32 + c % 2
            ext_ref[at : at + 1] = cr[r, c, 3:4]

    def gather_copy(g, dst):
        ref = gbufs[g].at[me]
        return pltpu.make_async_remote_copy(
            src_ref=ref,
            dst_ref=ref,
            send_sem=gsend_sem.at[g],
            recv_sem=grecv_sem.at[g],
            device_id=dst,
            device_id_type=LOGICAL,
        )

    def gather_send(g, rows):
        for k, value in enumerate(rows):
            gbufs[g][me, k : k + 1] = jnp.broadcast_to(value, (1, 128))

        def send(i, carry):
            gather_copy(g, other(i)).start()
            return carry

        lax.fori_loop(1, n, send, 0, unroll=n <= 64)

    def gather_bytes(g, sem):
        ref = gbufs[g].at[pl.ds(0, n - 1)]
        pltpu.make_async_copy(ref, ref, sem).wait()

    def gather_wait(g):
        gather_bytes(g, grecv_sem.at[g])

    row = lax.broadcasted_iota(jnp.int32, (ROWS, 128), 0)
    lane = lax.broadcasted_iota(jnp.int32, (ROWS, 128), 1)
    zpos, ypos = row // 32, row % 32
    y8, x8 = row % 8, lane % 8
    y_first = jnp.logical_and(y8 == 0, ypos > 0).astype(F32)
    y_last = jnp.logical_and(y8 == 7, ypos < 31).astype(F32)
    x_first = jnp.logical_and(x8 == 0, lane > 0).astype(F32)
    x_last = jnp.logical_and(x8 == 7, lane < 127).astype(F32)

    def flag(c):
        return c.astype(jnp.int32).astype(F32)

    zlo_f, zhi_f, ylo_f, yhi_f = flag(has_zlo), flag(has_zhi), flag(has_ylo), flag(has_yhi)
    z0, z7 = (zpos == 0).astype(F32), (zpos == 7).astype(F32)
    yb0, yb31 = (ypos == 0).astype(F32), (ypos == 31).astype(F32)
    half_zlo, half_zhi = 0.5 * zlo_f * z0, 0.5 * zhi_f * z7
    half_ylo, half_yhi = 0.5 * ylo_f * yb0, 0.5 * yhi_f * yb31
    own_z, own_y = 1.0 - half_zlo - half_zhi, 1.0 - half_ylo - half_yhi
    inv_m = (
        own_z
        * (own_y - 0.5 * (y_first + y_last))
        * (1.0 - 0.5 * (x_first + x_last))
    )
    invm_ref[...] = inv_m

    def fold_in(v):
        v = v + x_first * pltpu.roll(v, 1, 1) + x_last * pltpu.roll(v, 127, 1)
        return v + y_first * pltpu.roll(v, 1, 0) + y_last * pltpu.roll(v, ROWS - 1, 0)

    for i in (4, 0, 1, 5):
        loads[i].wait()
    mass = mass_ref[0:ROWS]
    level = level_ref[...]
    advect = (
        vel_ref[0:ROWS] * along_z(level, deriv)
        + vel_ref[ROWS : 2 * ROWS] * along_y(level, table, T_DY)
        + vel_ref[2 * ROWS : 3 * ROWS] * along_x(level, table, T_DXT)
    )
    lev_ref[...] = fold_in(mass * (level - (2.0 * TIME_STEP) * advect))
    diverge = (
        along_z(vel_ref[0:ROWS], deriv)
        + along_y(vel_ref[ROWS : 2 * ROWS], table, T_DY)
        + along_x(vel_ref[2 * ROWS : 3 * ROWS], table, T_DXT)
    )
    loads[2].wait()
    part_ref[...] = fold_in(mass * (source_ref[...] - (2.0 * TIME_STEP) * diverge))

    pl.semaphore_wait(barrier, n - 1)
    halo_send(0, 3, lev_ref)
    res_ref[...] = part_ref[...]
    loads[3].wait()
    solid = dot(solid_ref[0].astype(F32), mass_ref[ROWS : ROWS + EX])
    solid = jnp.concatenate(
        [jnp.broadcast_to(solid[e : e + 1], (8, 128)) for e in range(EY)], axis=0
    )
    solid = jnp.concatenate([solid] * 8, axis=0)
    halo_wait(0, 3)
    add_rim(0, res_ref, 0, 0, 0)
    add_rim(0, lev_ref, 64, 16, 4)
    outer_halo(0)
    level_new = lev_ref[...] * inv_m / mass
    level_out[...] = level_new
    coef = (GAS_RATIO - (GAS_RATIO - 1.0) * jax.nn.sigmoid(level_new / LEVEL_WIDTH)) * (
        1.0 - (1.0 - SOLID_FACTOR) * solid
    )
    flux_ref[...] = 4.0 * coef * mass
    gather_send(0, (total(coef) / (ROWS * 128.0), total(res_ref[...] * inv_m)))

    def local_solve(v):
        for z in range(8):
            ext_ref[PLANE * (z + 1) : PLANE * (z + 1) + 32] = v[32 * z : 32 * z + 32]
        planes = [ext_ref[PLANE * z : PLANE * z + PLANE] for z in range(10)]
        wide = jnp.concatenate(sine_z(planes, sine, range(10)), axis=0)
        wide = planes_y(wide, table, T_SY, 200, 208)
        wh, wl = split(wide)
        spectral = dot(jnp.concatenate([wh, wl], axis=1), table[T_SX : T_SX + 256, :])
        spectral = spectral + dot(wh, table[T_SX + 256 : T_SX + 384, :])
        sh, sl = split(spectral * den_ref[...])
        back = dot(sh, table[T_BX : T_BX + 256, :])
        back = back[:, :128] + back[:, 128:] + dot(sl, table[T_BX : T_BX + 256, :128])
        back = planes_y(back, table, T_BY, 160, 160)
        planes = [back[32 * z : 32 * z + 32] for z in range(10)]
        return jnp.concatenate(sine_z(planes, sine, range(1, 9)), axis=0)

    def helm(v):
        flux = flux_ref[...]
        out = along_z(flux * along_z(v, deriv), deriv.T)
        out = out + along_y(flux * along_y(v, table, T_DY), table, T_DYT)
        out = out + along_x(flux * along_x(v, table, T_DXT), table, T_DX)
        return out + HELM_COEF * mass_ref[0:ROWS] * v

    npad = a_ref.shape[1]
    sub_n = lax.broadcasted_iota(jnp.int32, (n, npad), 0)
    lane_n = lax.broadcasted_iota(jnp.int32, (n, npad), 1)

    def gathered(g, item):
        got = gbufs[g][:, item, :]
        return got if npad == 128 else jnp.concatenate([got] * (npad // 128), axis=1)

    def invert(k_col):
        diag = lane_n == sub_n
        k_row = jnp.sum(jnp.where(diag, k_col, 0.0), axis=0, keepdims=True)
        gap = lane_n - sub_n
        same = lane_n // ngy == sub_n // ngy
        y_link = jnp.logical_and(jnp.logical_or(gap == 1, gap == -1), same)
        z_link = jnp.logical_or(gap == ngy, gap == -ngy)
        rate = jnp.where(z_link, float(EY * EX) / EZ, 0.0) + jnp.where(
            y_link, float(EZ * EX) / EY, 0.0
        )
        rate = jnp.where(lane_n < n, rate, 0.0)
        link = 2.0 * k_col * k_row / (k_col + k_row) * rate
        diagonal = HELM_COEF * EZ * EY * EX + jnp.sum(link, axis=1, keepdims=True)
        a = jnp.where(diag, diagonal, -link)
        if ngx == 2 and n <= 64:
            left_over = list(range(ngy))
            while left_over:
                now = left_over[1::2] or left_over
                left_over = left_over[0::2] if len(left_over) > 1 else []
                cross = jnp.zeros((n, npad), jnp.bool_)
                change = None
                for j in now:
                    k, m = j, ngy + j
                    c1 = jnp.broadcast_to(a[:, k : k + 1], (n, npad))
                    c2 = jnp.broadcast_to(a[:, m : m + 1], (n, npad))
                    p11, p12, p22 = c1[k : k + 1], c2[k : k + 1], c2[m : m + 1]
                    scale = 1.0 / (p11 * p22 - p12 * p12)
                    at1, at2 = lane_n == k, lane_n == m
                    on1, on2 = sub_n == k, sub_n == m
                    r1 = jnp.where(at1[:1], -1.0, jnp.where(at2[:1], 0.0, a[k : k + 1]))
                    r2 = jnp.where(at2[:1], -1.0, jnp.where(at1[:1], 0.0, a[m : m + 1]))
                    q1 = (p22 * r1 - p12 * r2) * scale
                    q2 = (p11 * r2 - p12 * r1) * scale
                    c1 = jnp.where(on1, -1.0, jnp.where(on2, 0.0, c1))
                    c2 = jnp.where(on2, -1.0, jnp.where(on1, 0.0, c2))
                    cross = cross | at1 | at2 | on1 | on2
                    term = c1 * q1 + c2 * q2
                    change = term if change is None else change + term
                a = jnp.where(cross, 0.0, a) - change
            a_ref[...] = a
        else:
            a_ref[...] = a

            def step(k, carry):
                a = a_ref[...]
                row = a_ref[pl.ds(k, 1), :]
                col = jnp.sum(jnp.where(lane_n == k, a, 0.0), axis=1, keepdims=True)
                a_ref[...] = sweep_step(a, row, col, k, sub_n, lane_n)
                return carry

            lax.fori_loop(0, n, step, 0)

    def coarse(t_col):
        return -jnp.sum(a_ref[...] * t_col, axis=0, keepdims=True)

    def coarse_field(x):
        def value(dz, dy):
            at = me + dz * ngy + dy
            return jnp.sum(jnp.where(lane_n[:1] == at, x, 0.0), axis=1, keepdims=True)

        def along_y(dz):
            return own_y * value(dz, 0) + half_ylo * value(dz, -1) + half_yhi * value(dz, 1)

        return own_z * along_y(0) + half_zlo * along_y(-1) + half_zhi * along_y(1)

    offsets = [(dz, dy) for dz in (0, -1, 1) for dy in (0, -1, 1)]

    def shares(v):
        row = jnp.zeros((1, 128), F32)
        for d, (dz, dy) in enumerate(offsets):
            part = v * (own_z, half_zhi, half_zlo)[dz] * (own_y, half_yhi, half_ylo)[dy]
            row = row + jnp.where(lane[:1] == d, total(part), 0.0)
        return row

    def share_totals():
        got = gbufs[1][:, 0, :]
        out = jnp.zeros((n, 128), F32)
        for d, (dz, dy) in enumerate(offsets):
            value = jnp.broadcast_to(got[:, d : d + 1], (n, 128))
            shift = (dz * ngy + dy) % n
            if shift:
                value = jnp.concatenate([value[n - shift :], value[: n - shift]], axis=0)
            out = out + value
        return out if npad == 128 else jnp.concatenate([out] * (npad // 128), axis=1)

    def rows_sum(v):
        return jnp.sum(v, axis=0, keepdims=True)

    loads[6].wait()
    loads[7].wait()
    part_ref[...] = fold_in(local_solve(res_ref[...]) * inv_m)
    halo_send(1, 1)
    gather_wait(0)
    invert(gathered(0, 0))
    field = coarse_field(coarse(gathered(0, 1)))
    halo_wait(1, 1)
    search_ref[...] = part_ref[...]
    add_rim(1, search_ref, 0, 0, 0)
    z1 = search_ref[...] + field
    search_ref[...] = z1

    applied = helm(z1)
    part_ref[...] = fold_in(applied)
    halo_send(2, 2)
    gather_send(1, (shares(applied),))
    sum_rz = rows_sum(res_ref[...] * z1 * inv_m)
    sum_za = rows_sum(z1 * applied)
    app_ref[...] = part_ref[...]
    halo_wait(2, 2)
    add_rim(2, app_ref, 0, 0, 0)
    outer_halo(2)

    part_ref[...] = fold_in(local_solve(app_ref[...]) * invm_ref[...])
    halo_send(3, 1)
    gather_wait(1)
    field = coarse_field(coarse(share_totals()))
    halo_wait(3, 1)
    add_rim(3, part_ref, 0, 0, 0)
    q = part_ref[...] + field

    q_m = q * invm_ref[...]
    gz, gy, gx = along_z(q, deriv), along_y(q, table, T_DY), along_x(q, table, T_DXT)
    energy = flux_ref[...] * (gz * gz + gy * gy + gx * gx)
    energy = energy + HELM_COEF * mass_ref[0:ROWS] * (q * q)
    sum_rq = rows_sum(res_ref[...] * q_m)
    sum_aq = rows_sum(app_ref[...] * q_m)
    gather_send(2, (sum_rz, sum_za, sum_rq, sum_aq, rows_sum(energy), 0.0, 0.0, 0.0))
    for r, layers in enumerate((3, 1, 2, 1)):
        halo_drain(r, layers)
    for g in range(2):
        gather_bytes(g, gsend_sem.at[g])
    gather_wait(2)
    sums = jnp.sum(jnp.sum(gbuf2[...], axis=0), axis=1, keepdims=True)
    rz, za, rq, aq, qq = (sums[k : k + 1] for k in range(5))

    step1 = rz / za
    rz_next = step1 * (step1 * aq - rq)
    beta1 = 1.0 + rz_next / rz
    norm2 = beta1 * beta1 * za - 2.0 * beta1 * step1 * aq + step1 * step1 * qq
    step2 = rz_next / norm2
    pressure_out[...] = (step1 + step2 * beta1) * search_ref[...] - (step2 * step1) * q

    gather_bytes(2, gsend_sem.at[2])


def body(ngx, ngy, level_set, velocity, source, wick_solid):
    n = ngx * ngy
    npad = -(-n // 128) * 128
    consts = [jnp.asarray(t) for t in tables()]
    hbm = pl.BlockSpec(memory_space=pltpu.HBM)
    vmem = pl.BlockSpec(memory_space=pltpu.VMEM)
    shape = level_set.shape
    level_new, pressure = pl.pallas_call(
        functools.partial(kernel, ngx, ngy, gll_tables()[1], sine_table()),
        out_shape=[jax.ShapeDtypeStruct((ROWS, 128), F32)] * 2,
        in_specs=[hbm] * (4 + len(consts)),
        out_specs=[vmem] * 2,
        scratch_shapes=[
            pltpu.VMEM((ROWS, 128), F32),
            pltpu.VMEM((ROWS, 128), F32),
            pltpu.VMEM((ROWS, 128), F32),
            pltpu.VMEM((ROWS, 128), F32),
            pltpu.VMEM((ROWS, 128), F32),
            pltpu.VMEM((ROWS, 128), F32),
            pltpu.VMEM((ROWS, 128), F32),
            pltpu.VMEM((SPEC, 128), F32),
            pltpu.VMEM((n, npad), F32),
            pltpu.VMEM((4, 2, 96, 128), F32),
            pltpu.VMEM((4, 2, 96, 128), F32),
            pltpu.VMEM((4, 2, 24, 128), F32),
            pltpu.VMEM((4, 2, 24, 128), F32),
            pltpu.VMEM((4, 4, 8, 128), F32),
            pltpu.VMEM((4, 4, 8, 128), F32),
            pltpu.VMEM((n, 2, 128), F32),
            pltpu.VMEM((n, 1, 128), F32),
            pltpu.VMEM((n, 8, 128), F32),
            pltpu.VMEM((ROWS, 128), F32),
            pltpu.VMEM((3 * ROWS, 128), F32),
            pltpu.VMEM((ROWS, 128), F32),
            pltpu.VMEM((1, EY, EX), jnp.int32),
            *[pltpu.VMEM(t.shape, t.dtype) for t in consts],
            pltpu.SemaphoreType.DMA((4, 8)),
            pltpu.SemaphoreType.DMA((4, 8)),
            pltpu.SemaphoreType.DMA((3,)),
            pltpu.SemaphoreType.DMA((3,)),
            pltpu.SemaphoreType.DMA((8,)),
        ],
        compiler_params=pltpu.CompilerParams(
            collective_id=0, has_side_effects=True, vmem_limit_bytes=54848 * 1024
        ),
    )(
        level_set.reshape(ROWS, 128),
        velocity.reshape(3 * ROWS, 128),
        source.reshape(ROWS, 128),
        wick_solid,
        *consts,
    )
    return level_new.reshape(shape), pressure.reshape(shape)


def solution(mesh):
    placed = (
        P("gx", "gy", None),
        P(None, "gx", "gy", None),
        P("gx", "gy", None),
        P("gx", "gy", None),
    )
    return jax.shard_map(
        functools.partial(body, mesh.shape["gx"], mesh.shape["gy"]),
        mesh=mesh,
        in_specs=placed,
        out_specs=(P("gx", "gy", None), P("gx", "gy", None)),
        check_vma=False,
    )
```
